32 devices in a mesh: dp: 4 (over z), fsdp: 8 (over y, x, core).
Axes of the slice: x: 2, y: 2, z: 4, core: 2. Of those that a mesh axis runs over, the one named last changes fastest.
Arguments:
- tokens: bfloat16 [36864, 768], P(('dp', 'fsdp')), may hold values from -6 to 6
- input_weight: bfloat16 [768, 2304], P(('dp', 'fsdp')), may hold values from -0.21875 to 0.21875
- query_bias: bfloat16 [768], P(('dp', 'fsdp')), may hold values from -3 to 3
- value_bias: bfloat16 [768], P(('dp', 'fsdp')), may hold values from -2 to 2
- output_weight: bfloat16 [768, 768], P(('dp', 'fsdp')), may hold values from -0.875 to 0.875
- output_bias: bfloat16 [768], P(('dp', 'fsdp')), may hold values from -2 to 2
- first_gain: bfloat16 [768], P(('dp', 'fsdp')), may hold values from 0.5 to 1.5
- first_shift: bfloat16 [768], P(('dp', 'fsdp')), may hold values from -2 to 2
- up_weight: bfloat16 [768, 3072], P(('dp', 'fsdp')), may hold values from -0.21875 to 0.21875
- up_bias: bfloat16 [3072], P(('dp', 'fsdp')), may hold values from -2 to 2
- down_weight: bfloat16 [3072, 768], P(('dp', 'fsdp')), may hold values from -0.109375 to 0.109375
- down_bias: bfloat16 [768], P(('dp', 'fsdp')), may hold values from -2 to 2
- second_gain: bfloat16 [768], P(('dp', 'fsdp')), may hold values from 0.5 to 1.5
- second_shift: bfloat16 [768], P(('dp', 'fsdp')), may hold values from -2 to 2
- retriever_weight: bfloat16 [768, 128], P(('dp', 'fsdp')), may hold values from -0.21875 to 0.21875
- document_table: bfloat16 [8192, 128], P(('dp', 'fsdp')), may hold values from -0.5 to 0.5
- document_index: int32 [128], P(('dp', 'fsdp')), may hold values from 0 to 8191
- output_grad: bfloat16 [36864, 768], P(('dp', 'fsdp')), may hold values from -6 to 6
- score_grad: float32 [128], P(('dp', 'fsdp')), may hold values from -6 to 6
Outputs:
- output: bfloat16 [36864, 768], P(('dp', 'fsdp'))
- retrieval_scores: float32 [128], P(('dp', 'fsdp'))
- tokens_gradient: bfloat16 [36864, 768], P(('dp', 'fsdp'))
- input_weight_gradient: float32 [768, 2304], P(('dp', 'fsdp'))
- query_bias_gradient: float32 [768], P(('dp', 'fsdp'))
- value_bias_gradient: float32 [768], P(('dp', 'fsdp'))
- output_weight_gradient: float32 [768, 768], P(('dp', 'fsdp'))
- output_bias_gradient: float32 [768], P(('dp', 'fsdp'))
- first_gain_gradient: float32 [768], P(('dp', 'fsdp'))
- first_shift_gradient: float32 [768], P(('dp', 'fsdp'))
- up_weight_gradient: float32 [768, 3072], P(('dp', 'fsdp'))
- up_bias_gradient: float32 [3072], P(('dp', 'fsdp'))
- down_weight_gradient: float32 [3072, 768], P(('dp', 'fsdp'))
- down_bias_gradient: float32 [768], P(('dp', 'fsdp'))
- second_gain_gradient: float32 [768], P(('dp', 'fsdp'))
- second_shift_gradient: float32 [768], P(('dp', 'fsdp'))
- retriever_gradient: float32 [768, 128], P(('dp', 'fsdp'))
- table_gradient: float32 [8192, 128], P(('dp', 'fsdp'))
The draws below stay inside these ranges and needn't reach their ends.
All inputs are finite; a program needn't handle non-finite values.
Results may differ from the reference program's by a relative error of at most 0.014.
Values may be sent and summed in bfloat16 or wider, within the bound.
No kernel may reach another device: no remote copies, remote signals or barrier semaphores. Data moves between devices by JAX's collectives and lax.ppermute only.
A program may use at most 192 MiB of HBM per device.

```python
import math
import jax
import jax.numpy as jnp
import numpy as np
from jax import lax

D = 768
HEADS = 12
HEAD_DIM = 64
FF = 3072
R = 128
TABLE = 8192
LENGTH = 288
SEQ_DEV = 4
SEQS = 128
TOKENS = 36864


def with_ends(result, stream_key, smallest, high):
    shape = result.shape
    index_at = [jax.random.randint(jax.random.fold_in(stream_key, axis), (), 0, shape[axis]) for axis in range(len(shape))]
    result = result.at[tuple(index_at)].set(smallest)
    longest = shape.index(max(shape))
    index_at[longest] = (index_at[longest] + 1) % shape[longest]
    return result.at[tuple(index_at)].set(high)


def level_of(key, shape, split, low, top_value):
    factor_of, own = 1.0, jax.random.fold_in(key, 6)
    for axis_at, shards_of in split:
        steps = jnp.exp(jax.random.uniform(jax.random.fold_in(own, axis_at), (shards_of,), jnp.float32, low / len(split), top_value / len(split)))
        factor_of = factor_of * jnp.repeat(steps, shape[axis_at] // shards_of).reshape([-1 if axis == axis_at else 1 for axis in range(len(shape))])
    return factor_of


def cumulative_ranks(amount, skew):
    portions = [(1 << 20) // math.isqrt(grade ** skew) + 1 for grade in range(1, amount + 1)]
    width = 1 + sum(portions) // (1 << 30)
    return np.cumsum(np.array([max(1, weight // width) for weight in portions]))


def ranked_ids(own_key, dims, number_of, lean):
    table = cumulative_ranks(number_of, lean)
    lot = jax.random.randint(jax.random.fold_in(own_key, 1), dims, 0, int(table[number_of - 1]))
    rank = jnp.searchsorted(jnp.asarray(table, jnp.int32), lot, side="right")
    return jax.random.permutation(jax.random.fold_in(own_key, 2), number_of)[rank].astype(jnp.int32)


def scatter_about(key, extent, width, limit, shards=(), held_as=jnp.bfloat16):
    values = jax.random.normal(key, extent, jnp.float32) * width
    if len(shards) > 0:
        values = level_of(key, extent, shards, -0.22, 0.18) * values
    return jnp.clip(values, min=-limit, max=limit).astype(held_as)


def setup_inputs(seed: int = 0) -> dict:
    streams_of = jax.random.split(jax.random.key(seed), 20)
    return {
        "tokens": scatter_about(streams_of[0], (TOKENS, D), 1.0, 6.0, ((0, 32),)),
        "input_weight": scatter_about(streams_of[1], (D, 3 * D), D ** -0.5, 0.21875, ((0, 32),)),
        "query_bias": scatter_about(streams_of[2], (D,), 0.5, 3.0, ((0, 32),)),
        "value_bias": scatter_about(streams_of[3], (D,), 0.3, 2.0, ((0, 32),)),
        "output_weight": scatter_about(streams_of[4], (D, D), (D // 16) ** -0.5, 0.875, ((0, 32),)),
        "output_bias": scatter_about(streams_of[5], (D,), 0.3, 2.0, ((0, 32),)),
        "first_gain": jnp.clip(1.0 + 0.1 * jax.random.normal(streams_of[6], (D,), jnp.float32), 0.5, 1.5).astype(jnp.bfloat16),
        "first_shift": scatter_about(streams_of[7], (D,), 0.3, 2.0, ((0, 32),)),
        "up_weight": scatter_about(streams_of[8], (D, FF), D ** -0.5, 0.21875, ((0, 32),)),
        "up_bias": scatter_about(streams_of[9], (FF,), 0.3, 2.0, ((0, 32),)),
        "down_weight": scatter_about(streams_of[10], (FF, D), FF ** -0.5, 0.109375, ((0, 32),)),
        "down_bias": scatter_about(streams_of[11], (D,), 0.3, 2.0, ((0, 32),)),
        "second_gain": jnp.clip(1.0 + 0.1 * jax.random.normal(streams_of[12], (D,), jnp.float32), 0.5, 1.5).astype(jnp.bfloat16),
        "second_shift": scatter_about(streams_of[13], (D,), 0.3, 2.0, ((0, 32),)),
        "retriever_weight": scatter_about(streams_of[14], (D, R), D ** -0.5, 0.21875, ((0, 32),)),
        "document_table": scatter_about(streams_of[15], (TABLE, R), R ** -0.5, 0.5, ((0, 32),)),
        "document_index": with_ends(ranked_ids(streams_of[16], (SEQS,), TABLE, 2), jax.random.fold_in(streams_of[16], 3), 0, TABLE - 1).astype(jnp.int32),
        "output_grad": scatter_about(streams_of[17], (TOKENS, D), 1.0, 6.0, ((0, 32),)),
        "score_grad": scatter_about(streams_of[18], (SEQS,), 1.0, 6.0, ((0, 32),), jnp.float32),
    }


@jax.custom_vjp
def low(v):
    return lax.optimization_barrier(v.astype(jnp.bfloat16)).astype(jnp.float32)

@jax.custom_vjp
def low_back(v):
    return v

def low_keep(v):
    return (low(v), None)

def low_pass(kept, grad):
    return (grad,)

def back_keep(v):
    return (v, None)

def back_low(kept, grad):
    return (low(grad),)
low.defvjp(low_keep, low_pass)
low_back.defvjp(back_keep, back_low)

def round_both(value):
    return low_back(low(value))

def highest(left, right):
    return jnp.dot(left, right, precision=lax.Precision.HIGHEST)

def layer_norm(hidden, norm_gain, norm_shift):
    average = lax.optimization_barrier(jnp.mean(hidden, axis=-1, keepdims=True))
    centered = hidden - average
    variance = lax.optimization_barrier(jnp.mean(centered * centered, axis=-1, keepdims=True))
    return centered * lax.rsqrt(variance + 1e-12) * norm_gain + norm_shift

def forward(rows_block, params, indices):
    input_weight, query_bias, value_bias, output_weight, output_bias, first_gain, first_shift, up_weight, up_bias, down_weight, down_bias, second_gain, second_shift, retriever_weight, document_table = params
    groups = rows_block.shape[0]
    flat = rows_block.reshape(groups * LENGTH, D)
    mixed = highest(flat, input_weight)
    queries = round_both(mixed[:, :D] + query_bias).reshape(groups, LENGTH, HEADS, HEAD_DIM)
    keys_all = round_both(mixed[:, D:2 * D]).reshape(groups, LENGTH, HEADS, HEAD_DIM)
    values = round_both(mixed[:, 2 * D:] + value_bias).reshape(groups, LENGTH, HEADS, HEAD_DIM)
    scores = jnp.einsum('gqhe,gkhe->ghqk', queries, keys_all, precision=lax.Precision.HIGHEST)
    scores = low_back(scores * HEAD_DIM ** (-0.5))
    soft_low = low(jax.nn.softmax(scores, axis=-1))
    context = jnp.einsum('ghqk,gkhe->gqhe', soft_low, values, precision=lax.Precision.HIGHEST)
    context = round_both(context.reshape(groups * LENGTH, D))
    attended = low_back(highest(context, output_weight) + output_bias)
    first_out = low(layer_norm(flat + attended, first_gain, first_shift))
    inner_sum = low_back(highest(first_out, up_weight) + up_bias)
    active = low(jax.nn.gelu(inner_sum, approximate=False))
    feed_out = low_back(highest(active, down_weight) + down_bias)
    final_out = low(layer_norm(first_out + feed_out, second_gain, second_shift))
    leading = final_out.reshape(groups, LENGTH, D)[:, 0]
    projected = round_both(highest(leading, retriever_weight))
    picker = (indices[:, None] == jnp.arange(TABLE, dtype=jnp.int32)[None, :]).astype(jnp.float32)
    chosen = highest(picker, document_table)
    return (final_out.reshape(groups, LENGTH, D), lax.optimization_barrier(jnp.sum(projected * chosen, axis=-1)))

def reference(tokens, input_weight, query_bias, value_bias, output_weight, output_bias, first_gain, first_shift, up_weight, up_bias, down_weight, down_bias, second_gain, second_shift, retriever_weight, document_table, document_index, output_grad, score_grad):
    params = tuple((array_one.astype(jnp.float32) for array_one in (input_weight, query_bias, value_bias, output_weight, output_bias, first_gain, first_shift, up_weight, up_bias, down_weight, down_bias, second_gain, second_shift, retriever_weight, document_table)))
    blocks = SEQS // SEQ_DEV
    rows_all = tokens.astype(jnp.float32).reshape(blocks, SEQ_DEV, LENGTH, D)
    backs_all = output_grad.astype(jnp.float32).reshape(blocks, SEQ_DEV, LENGTH, D)
    index_all = document_index.astype(jnp.int32).reshape(blocks, SEQ_DEV)
    score_all = score_grad.astype(jnp.float32).reshape(blocks, SEQ_DEV)

    def block_step(totals, block_item):
        rows_block, back_block, indices, score_back = block_item

        def local_pass(rows_in, params_in):
            return forward(rows_in, params_in, indices)
        outputs, pullback = jax.vjp(local_pass, rows_block, params)
        back_rows, back_params = pullback((back_block, score_back))
        return (jax.tree.map(jnp.add, totals, back_params), (outputs[0], outputs[1], back_rows))
    zero_sums = jax.tree.map(jnp.zeros_like, params)
    totals, (finals, scores, back_rows) = lax.scan(block_step, zero_sums, (rows_all, backs_all, index_all, score_all))
    return (finals.reshape(TOKENS, D).astype(jnp.bfloat16), scores.reshape(SEQS), back_rows.reshape(TOKENS, D).astype(jnp.bfloat16), totals[0], totals[1], totals[2], totals[3], totals[4], totals[5], totals[6], totals[7], totals[8], totals[9], totals[10], totals[11], totals[12], totals[13], totals[14])
```

```python
import functools
import math
import jax
import jax.numpy as jnp
from jax import lax
from jax.experimental import pallas as pl
from jax.experimental.pallas import tpu as pltpu
from jax.sharding import PartitionSpec as P

HEAD_DIM = 64
EPS = 1e-12
VMEM = 56 * 2**20
bf16, f32 = jnp.bfloat16, jnp.float32
ERFC_P = 0.33
ERFC_Q = (-0.1359291, 0.46268956, -0.35544136, 0.41254396, 0.04500932, 0.20192425, 0.18283717, 0.18636611)


def dot(a, b, ca=1, cb=0):
    return lax.dot_general(a, b, (((ca,), (cb,)), ((), ())), preferred_element_type=f32)


def rows_spec(rows, cols):
    return pl.BlockSpec((rows, cols), lambda i: (i, 0))


def full_spec(shape):
    return pl.BlockSpec(shape, lambda *_: (0,) * len(shape))


def head_mask(rows, cols, h):
    lane = lax.broadcasted_iota(jnp.int32, (rows, cols), 1)
    return (lane >= h * HEAD_DIM) & (lane < (h + 1) * HEAD_DIM)


def run(body, name, grid, ins, in_specs, outs, out_specs, scratch=(), flops=0, moved=0, vmem=VMEM):
    return pl.pallas_call(
        body,
        name=name,
        grid=grid,
        in_specs=in_specs,
        out_specs=out_specs,
        out_shape=outs,
        scratch_shapes=list(scratch),
        cost_estimate=pl.CostEstimate(flops=int(flops), bytes_accessed=int(moved), transcendentals=0),
        compiler_params=pltpu.CompilerParams(vmem_limit_bytes=vmem),
    )(*ins)


def sds(shape, dtype):
    return jax.ShapeDtypeStruct(shape, dtype)


def attend_body(x_ref, w_ref, qb_ref, vb_ref, qkv_ref, soft_ref, ctx_ref):
    length = x_ref.shape[0]
    gc = ctx_ref.shape[1]
    mixed = dot(x_ref[...], w_ref[...])
    q = (mixed[:, :gc] + qb_ref[...]).astype(bf16)
    k = mixed[:, gc : 2 * gc].astype(bf16)
    v = (mixed[:, 2 * gc :] + vb_ref[...]).astype(bf16)
    qkv_ref[:, :gc] = q
    qkv_ref[:, gc : 2 * gc] = k
    qkv_ref[:, 2 * gc :] = v
    qs = q * bf16(HEAD_DIM ** -0.5)
    zero = jnp.zeros((), bf16)
    total = jnp.zeros((length, gc), f32)
    for h in range(gc // HEAD_DIM):
        mask = head_mask(length, gc, h)
        s = dot(jnp.where(mask, qs, zero), k, 1, 1)
        peak = jnp.max(s, axis=-1, keepdims=True)
        e = jnp.exp(s - peak)
        norm = 1.0 / jnp.sum(e, axis=-1, keepdims=True)
        p = (e * norm).astype(bf16)
        soft_ref[h] = p
        total += dot(p, jnp.where(mask, v, zero))
    ctx_ref[...] = total.astype(bf16)


def attend(x, w, qb, vb, seqs):
    T, D = x.shape
    gc = w.shape[1] // 3
    hg = gc // HEAD_DIM
    L = T // seqs
    return run(
        attend_body, "attend", (seqs,), (x, w, qb, vb),
        [rows_spec(L, D), full_spec(w.shape), full_spec(qb.shape), full_spec(vb.shape)],
        [sds((T, 3 * gc), bf16), sds((hg, T, L), bf16), sds((T, gc), bf16)],
        [rows_spec(L, 3 * gc), pl.BlockSpec((hg, L, L), lambda i: (0, i, 0)), rows_spec(L, gc)],
        flops=2 * T * D * 3 * gc + 16 * T * L * gc, moved=2 * (T * D + w.size + 4 * T * gc + hg * T * L),
    )


def erfc_parts(u):
    e = jnp.exp(u * u * -0.5)
    t = 1.0 / (1.0 + (ERFC_P * math.sqrt(0.5)) * jnp.abs(u))
    q = jnp.full_like(t, 0.5 * ERFC_Q[0])
    for c in ERFC_Q[1:]:
        q = q * t + 0.5 * c
    return q * t * e, e


def norm_rows(h):
    mean = jnp.mean(h, axis=-1, keepdims=True)
    c = h - mean
    var = jnp.mean(c * c, axis=-1, keepdims=True)
    inv = lax.rsqrt(var + EPS)
    return c * inv, inv


def norm_rows_back(cot, n, inv, gain):
    scaled = cot * gain
    return inv * (scaled - jnp.mean(scaled, axis=-1, keepdims=True) - n * jnp.mean(scaled * n, axis=-1, keepdims=True))


def up_body(ngroups, step, *refs):
    ctx_refs = refs[:ngroups]
    x_ref, wo_ref, ob_ref, g_ref, s_ref, wu_ref, ub_ref = refs[ngroups : ngroups + 7]
    n_ref, inv_ref, first_ref, act_ref, slope_ref = refs[ngroups + 7 :]
    gc = ctx_refs[0].shape[1]
    hidden = x_ref[...].astype(f32) + ob_ref[...]
    for g, c in enumerate(ctx_refs):
        hidden += dot(c[...], wo_ref[g * gc : (g + 1) * gc, :])
    n, inv = norm_rows(hidden)
    n_ref[...] = n
    inv_ref[...] = inv
    first = (n * g_ref[...] + s_ref[...]).astype(bf16)
    first_ref[...] = first
    ff = wu_ref.shape[1]
    for at in range(0, ff, step):
        cols = slice(at, at + step)
        u = dot(first, wu_ref[:, cols]) + ub_ref[:, cols]
        tail, e = erfc_parts(u)
        phi = jnp.where(u < 0, tail, 1.0 - tail)
        act_ref[:, cols] = (u * phi).astype(bf16)
        slope_ref[:, cols] = (phi + u * e * (1.0 / math.sqrt(2 * math.pi))).astype(bf16)


def up(ctxs, x, wo, ob, g, s, wu, ub, rows, step=512):
    T, D = x.shape
    F = wu.shape[1]
    return run(
        functools.partial(up_body, len(ctxs), step), "up", (T // rows,), (*ctxs, x, wo, ob, g, s, wu, ub),
        [rows_spec(rows, c.shape[1]) for c in ctxs] + [rows_spec(rows, D)] + [full_spec(a.shape) for a in (wo, ob, g, s, wu, ub)],
        [sds((T, D), f32), sds((T, 1), f32), sds((T, D), bf16), sds((T, F), bf16), sds((T, F), bf16)],
        [rows_spec(rows, D), rows_spec(rows, 1), rows_spec(rows, D), rows_spec(rows, F), rows_spec(rows, F)],
        flops=2 * T * D * (D + F), moved=T * D * 10 + 4 * T * F + 2 * (wo.size + wu.size),
    )


def add_rows(ref, value):
    @pl.when(pl.program_id(0) == 0)
    def _():
        ref[...] = jnp.zeros_like(ref)
    ref[...] += jnp.sum(value, axis=0, keepdims=True)


def down_body(step, first_ref, act_ref, slope_ref, w_ref, b_ref, g_ref, s_ref, og_ref, lead_ref,
              out_ref, two_ref, feed_ref, inner_ref, gg_ref, gs_ref, gb_ref, gub_ref):
    rows = first_ref.shape[0]
    hidden = first_ref[...].astype(f32) + b_ref[...] + dot(act_ref[...], w_ref[...])
    n, inv = norm_rows(hidden)
    out_ref[...] = (n * g_ref[...] + s_ref[...]).astype(bf16)
    row = lax.broadcasted_iota(jnp.int32, (rows, 1), 0)
    cot = og_ref[...].astype(f32) + jnp.where(row == 0, lead_ref[0], 0.0)
    add_rows(gg_ref, cot * n)
    add_rows(gs_ref, cot)
    two = norm_rows_back(cot, n, inv, g_ref[...])
    two_ref[...] = two
    feed = two.astype(bf16)
    feed_ref[...] = feed
    add_rows(gb_ref, feed.astype(f32))
    ff = w_ref.shape[0]
    for at in range(0, ff, step):
        cols = slice(at, at + step)
        inner = (dot(feed, w_ref[cols, :], 1, 1) * slope_ref[:, cols].astype(f32)).astype(bf16)
        inner_ref[:, cols] = inner
        @pl.when(pl.program_id(0) == 0)
        def _():
            gub_ref[:, cols] = jnp.zeros((1, step), f32)
        gub_ref[:, cols] += jnp.sum(inner.astype(f32), axis=0, keepdims=True)


def down(first, act, slope, w, b, g, s, og, lead, seqs, step=512):
    T, D = first.shape
    F = act.shape[1]
    L = T // seqs
    return run(
        functools.partial(down_body, step), "down", (seqs,), (first, act, slope, w, b, g, s, og, lead),
        [rows_spec(L, D), rows_spec(L, F), rows_spec(L, F)] + [full_spec((F, D))] + [full_spec(a.shape) for a in (b, g, s)]
        + [rows_spec(L, D), pl.BlockSpec((1, 1, D), lambda i: (i, 0, 0))],
        [sds((T, D), bf16), sds((T, D), f32), sds((T, D), bf16), sds((T, F), bf16),
         sds((1, D), f32), sds((1, D), f32), sds((1, D), f32), sds((1, F), f32)],
        [rows_spec(L, D), rows_spec(L, D), rows_spec(L, D), rows_spec(L, F)] + [full_spec((1, D))] * 3 + [full_spec((1, F))],
        flops=4 * T * D * F, moved=6 * T * F + 12 * T * D + 2 * w.size,
    )


def mid_body(two_ref, inner_ref, wu_ref, n_ref, inv_ref, g_ref, wo_ref,
             one_ref, att_ref, bctx_ref, gg_ref, gs_ref, gob_ref):
    cot = two_ref[...] + dot(inner_ref[...], wu_ref[...], 1, 1)
    n = n_ref[...]
    add_rows(gg_ref, cot * n)
    add_rows(gs_ref, cot)
    one = norm_rows_back(cot, n, inv_ref[...], g_ref[...])
    one_ref[...] = one
    att = one.astype(bf16)
    att_ref[...] = att
    add_rows(gob_ref, att.astype(f32))
    bctx_ref[...] = dot(att, wo_ref[...], 1, 1).astype(bf16)


def mid(two, inner, wu, n, inv, g, wo, rows):
    T, D = two.shape
    F = inner.shape[1]
    return run(
        mid_body, "mid", (T // rows,), (two, inner, wu, n, inv, g, wo),
        [rows_spec(rows, D), rows_spec(rows, F), full_spec(wu.shape), rows_spec(rows, D), rows_spec(rows, 1), full_spec(g.shape), full_spec(wo.shape)],
        [sds((T, D), f32), sds((T, D), bf16), sds((T, D), bf16)] + [sds((1, D), f32)] * 3,
        [rows_spec(rows, D)] * 3 + [full_spec((1, D))] * 3,
        flops=2 * T * D * (F + D), moved=2 * T * F + 16 * T * D + 2 * wu.size,
    )


def attend_back_body(qkv_ref, soft_ref, ctx_ref, bctx_ref, out_ref, gq_ref, gv_ref):
    length, gc = ctx_ref.shape
    q = qkv_ref[:, :gc]
    k = qkv_ref[:, gc : 2 * gc]
    v = qkv_ref[:, 2 * gc :]
    do = bctx_ref[...]
    prod = do.astype(f32) * ctx_ref[...].astype(f32)
    zero = jnp.zeros((), bf16)
    dq = jnp.zeros((length, gc), f32)
    dk = jnp.zeros((length, gc), f32)
    dv = jnp.zeros((length, gc), f32)
    for h in range(gc // HEAD_DIM):
        mask = head_mask(length, gc, h)
        p = soft_ref[h]
        do_h = jnp.where(mask, do, zero)
        dp = dot(do_h, v, 1, 1)
        delta = jnp.sum(jnp.where(mask, prod, 0.0), axis=-1, keepdims=True)
        ds = (p.astype(f32) * (dp - delta)).astype(bf16)
        dv += dot(p, do_h, 0, 0)
        dq += dot(ds, jnp.where(mask, k, zero))
        dk += dot(ds, jnp.where(mask, q, zero), 0, 0)
    scale = HEAD_DIM ** -0.5
    dq = (dq * scale).astype(bf16)
    dv = dv.astype(bf16)
    out_ref[:, :gc] = dq
    out_ref[:, gc : 2 * gc] = (dk * scale).astype(bf16)
    out_ref[:, 2 * gc :] = dv
    add_rows(gq_ref, dq.astype(f32))
    add_rows(gv_ref, dv.astype(f32))


def attend_back(qkv, soft, ctx, bctx, g, seqs):
    T, gc = ctx.shape
    hg = gc // HEAD_DIM
    L = T // seqs
    return run(
        attend_back_body, "attend_back", (seqs,), (qkv, soft, ctx, bctx),
        [rows_spec(L, 3 * gc), pl.BlockSpec((hg, L, L), lambda i: (0, i, 0)), rows_spec(L, gc), pl.BlockSpec((L, gc), lambda i: (i, g))],
        [sds((T, 3 * gc), bf16), sds((1, gc), f32), sds((1, gc), f32)],
        [rows_spec(L, 3 * gc), full_spec((1, gc)), full_spec((1, gc))],
        flops=32 * T * L * gc, moved=2 * (8 * T * gc + hg * T * L),
    )


def tokens_back_body(ngroups, one_ref, *refs):
    total = one_ref[...]
    for g in range(ngroups):
        total += dot(refs[g][...], refs[ngroups + g][...], 1, 1)
    refs[-1][...] = total.astype(bf16)


def tokens_back(one, mixed, ws, rows):
    T, D = one.shape
    n = len(mixed)
    return run(
        functools.partial(tokens_back_body, n), "tokens_back", (T // rows,), (one, *mixed, *ws),
        [rows_spec(rows, D)] + [rows_spec(rows, m.shape[1]) for m in mixed] + [full_spec(w.shape) for w in ws],
        sds((T, D), bf16), rows_spec(rows, D),
        flops=2 * T * D * sum(m.shape[1] for m in mixed), moved=T * D * 12,
    )


def after(x, *deps):
    return lax.optimization_barrier((x,) + deps)[0]


ANY = pl.BlockSpec(memory_space=pl.ANY)
SMEM = pl.BlockSpec(memory_space=pltpu.SMEM)
WHOLE = pl.BlockSpec(memory_space=pltpu.VMEM)
LANES = 128


def plain(body, name, ins, in_specs, outs, out_specs, scratch=(), moved=0, flops=0):
    return pl.pallas_call(
        body, name=name, in_specs=in_specs, out_specs=out_specs, out_shape=outs, scratch_shapes=list(scratch),
        cost_estimate=pl.CostEstimate(flops=int(flops), bytes_accessed=int(moved), transcendentals=0),
        compiler_params=pltpu.CompilerParams(vmem_limit_bytes=VMEM),
    )(*ins)


def cut_points(widths):
    cuts, at = [], 0
    for w in widths:
        cuts.append((at, at + w))
        at += w
    return cuts


def pack_body(D, gc, w_ref, o_ref, r_ref, v_ref, head_ref, rest_ref, held):
    G = D // gc
    rows, nvec = w_ref.shape[0], v_ref.shape[0]
    held[...] = jnp.zeros_like(held)
    held[0:nvec, 0:rows] = v_ref[...].astype(f32)
    turned = held[...].T
    for m in range(3):
        head_ref[:, m * gc : (m + 1) * gc] = w_ref[:, m * D : m * D + gc]
    head_ref[:, 3 * gc :] = turned[:rows, :].astype(bf16)
    at = 0
    for g in range(1, G):
        for m in range(3):
            rest_ref[:, at : at + gc] = w_ref[:, m * D + g * gc : m * D + (g + 1) * gc]
            at += gc
    rest_ref[:, at : at + D] = o_ref[...]
    rest_ref[:, at + D :] = r_ref[...]


def pack(w, o, r, v, gc):
    rows, D = o.shape
    head = 3 * gc + LANES
    rest = 3 * D - 3 * gc + D + r.shape[1]
    return plain(
        functools.partial(pack_body, D, gc), "pack", (w, o, r, v), [WHOLE] * 4,
        [sds((rows, head), bf16), sds((rows, rest), bf16)], [WHOLE] * 2,
        scratch=[pltpu.VMEM((LANES, LANES), f32)], moved=4 * rows * (head + rest),
    )


def stack_body(*refs):
    for k, ref in enumerate(refs[:-1]):
        refs[-1][k] = ref[...]


def stack(blocks):
    n = len(blocks)
    return plain(
        stack_body, "stack", blocks, [WHOLE] * n, sds((n,) + blocks[0].shape, bf16), WHOLE, moved=4 * n * blocks[0].size
    )


def pairs(n, flip):
    return [(i, i ^ flip) for i in range(n)]


def spread_dp(block, Z):
    return stack([block] + [lax.ppermute(block, "dp", pairs(Z, k)) for k in range(1, Z)])


def spread_fsdp(along, N):
    chips = [along] + [lax.ppermute(along, "fsdp", pairs(N, 2 * m)) for m in range(1, N // 2)]
    pieces = []
    for piece in chips:
        pieces += [piece, lax.ppermute(piece, "fsdp", pairs(N, 1))]
    return pieces


def place_body(N, cuts, turned, me_ref, *refs):
    pieces = refs[:N]
    outs = refs[N : N + len(cuts)]
    vec_ref = refs[N + len(cuts)] if turned else None
    held = refs[N + len(cuts) + turned : N + 2 * len(cuts) + turned]
    flat = refs[-3] if turned else None
    in_sem, out_sem = refs[-2:]
    Z = pieces[0].shape[0]
    copies = []
    for j in range(N):
        for k in range(Z):
            for c, (lo, hi) in enumerate(cuts):
                copies.append(
                    pltpu.make_async_copy(
                        pieces[j].at[k, :, lo:hi], held[c].at[me_ref[0] ^ k, me_ref[1] ^ j], in_sem.at[len(copies)]
                    )
                )
    for copy in copies:
        copy.start()
    for copy in copies:
        copy.wait()
    last = [pltpu.make_async_copy(held[c], outs[c], out_sem.at[c]) for c in range(len(cuts))]
    for copy in last:
        copy.start()
    if turned:
        for z in range(Z):
            for f in range(N):
                flat[z, f] = held[-1][z, f].astype(f32)
        vec_ref[...] = flat[...].reshape(vec_ref.shape[1], LANES).T[: vec_ref.shape[0]]
    for copy in last:
        copy.wait()


def place(me, pieces, widths, turned=0):
    N = len(pieces)
    Z, rows, _ = pieces[0].shape
    cuts = cut_points(widths)
    if turned and rows % 8:
        outs = place(me, pieces, widths)
        return outs + [outs[-1][:, :turned].T.astype(f32)]
    shapes = [(Z, N, rows, w) for w in widths]
    outs = plain(
        functools.partial(place_body, N, cuts, 1 if turned else 0), "place", (me, *pieces), [SMEM] + [ANY] * N,
        [sds(s, bf16) for s in shapes] + ([sds((turned, Z * N * rows), f32)] if turned else []),
        [ANY] * len(cuts) + ([WHOLE] if turned else []),
        scratch=[pltpu.VMEM(s, bf16) for s in shapes] + ([pltpu.VMEM(shapes[-1], f32)] if turned else [])
        + [pltpu.SemaphoreType.DMA((Z * N * len(cuts),)), pltpu.SemaphoreType.DMA((len(cuts),))],
        moved=4 * Z * N * rows * cuts[-1][1],
    )
    return [o.reshape(Z * N * rows, o.shape[3]) for o in outs[: len(cuts)]] + list(outs[len(cuts) :])


def grads_body(N, counts, nvec, has_retr, me_ref, *refs):
    at = 0
    outs, held = refs[-1 - N - (nvec > 0) : -1 - (nvec > 0)], refs[-1 - (nvec > 0)]
    Z, _, rows, _ = held.shape
    D = Z * N * rows
    col = 0
    for n in counts:
        y = refs[at + n][...]
        parts = [dot(r[...], y, 0, 0) for r in refs[at : at + n]]
        part = parts[0] if n == 1 else jnp.concatenate(parts, axis=0)
        w = part.shape[1]
        held[:, :, :, col : col + w] = part.reshape(Z, N, rows, w)
        at += n + 1
        col += w
    if has_retr:
        w = refs[at].shape[1]
        held[:, :, :, col : col + w] = refs[at][...].reshape(Z, N, rows, w)
        at += 1
        col += w
    if nvec:
        turn = refs[-1]
        turn[...] = jnp.zeros_like(turn)
        row = 0
        for r in refs[at : at + nvec]:
            turn[row : row + r.shape[0], :] = r[...]
            row += r.shape[0]
        held[:, :, :, col:] = turn[...].T.reshape(Z, N, rows, LANES)
    for j in range(N):
        for z in range(Z):
            outs[j][z] = held[z, me_ref[1] ^ j].astype(bf16)


def grads(me, Z, N, name, products, retr=None, vectors=(), tile=None):
    counts = [len(xs) for xs, _ in products]
    D = sum(x.shape[1] for x in products[0][0])
    rows = D // (Z * N)
    width = sum(y.shape[1] for _, y in products) + (0 if retr is None else retr.shape[1]) + (LANES if vectors else 0)
    if rows % 8:
        cols = [jnp.concatenate([dot(x, y, 0, 0) for x in xs], axis=0) for xs, y in products]
        cols += [] if retr is None else [retr]
        if vectors:
            turned = jnp.concatenate(vectors, axis=0).T
            cols += [turned, jnp.zeros((D, LANES - turned.shape[1]), f32)]
        whole = jnp.concatenate(cols, axis=1).astype(bf16).reshape(Z, N, rows, width)
        return [lax.dynamic_index_in_dim(whole, me[1] ^ j, 1, keepdims=False) for j in range(N)]
    ins = [a for xs, y in products for a in (*xs, y)] + ([] if retr is None else [retr]) + list(vectors)
    T = products[0][1].shape[0]
    if tile is None:
        tile, specs, grid = width, [full_spec(a.shape) for a in ins], (1,)
    else:
        specs, grid = [full_spec(ins[0].shape), pl.BlockSpec((T, tile), lambda i: (0, i))], (width // tile,)
    return run(
        functools.partial(grads_body, N, counts, len(vectors), retr is not None), name, grid, (me, *ins), [SMEM] + specs,
        [sds((Z, rows, width), bf16)] * N, [pl.BlockSpec((Z, rows, tile), lambda i: (0, 0, i))] * N,
        scratch=[pltpu.VMEM((Z, N, rows, tile), f32)] + ([pltpu.VMEM((LANES, D), f32)] if vectors else []),
        flops=2 * T * D * width, moved=2 * T * (D + width) + 2 * D * width,
    )


def grad_rows_body(x_ref, y_ref, o_ref):
    o_ref[...] = dot(x_ref[...], y_ref[...], 0, 0).astype(bf16)


def grad_rows(x, y, name, tile):
    T, M = x.shape
    D = y.shape[1]
    return run(
        grad_rows_body, name, (M // tile,), (x, y), [pl.BlockSpec((T, tile), lambda i: (0, i)), full_spec(y.shape)],
        sds((M, D), bf16), rows_spec(tile, D), flops=2 * T * M * D, moved=2 * (T * M + T * D + M * D),
    )


def pair_body(R, *refs):
    for m in range(R):
        refs[2 * R + m][...] = (refs[m][...].astype(f32) + refs[R + m][...].astype(f32)).astype(bf16)


def pair_sum(parts, Z, N):
    R = N // 2
    _, rows, width = parts[0].shape
    ins = [parts[2 * m] for m in range(R)]
    ins += [lax.ppermute(parts[2 * m + 1], "fsdp", pairs(N, 1)) for m in range(R)]
    block = pl.BlockSpec((1, rows, width), lambda i: (i, 0, 0))
    return run(
        functools.partial(pair_body, R), "pair_sum", (Z,), ins, [block] * (2 * R),
        [sds((Z, rows, width), bf16)] * R, [block] * R, moved=6 * R * Z * rows * width,
    )


def chips_body(n, me_ref, *refs):
    ins, outs = refs[:n], refs[n:]
    for k in range(len(outs)):
        z = me_ref[0] ^ k
        total = ins[0][z].astype(f32)
        for r in ins[1:]:
            total += r[z].astype(f32)
        outs[k][...] = total.astype(outs[k].dtype)


def chips_sum(me, sums, Z, N):
    R = N // 2
    _, rows, width = sums[0].shape
    got = [lax.ppermute(sums[m], "fsdp", pairs(N, 2 * m)) for m in range(1, R)]
    return plain(
        functools.partial(chips_body, R), "chips_sum", (me, sums[0], *got), [SMEM] + [WHOLE] * R,
        [sds((rows, width), f32)] + [sds((rows, width), bf16)] * (Z - 1), [WHOLE] * Z,
        moved=2 * (R + 1) * Z * rows * width,
    )


def last_body(n, cuts, turned, *refs):
    ins, outs = refs[:n], refs[n : n + len(cuts)]
    for c, (out, (lo, hi)) in enumerate(zip(outs, cuts)):
        total = ins[0][:, lo:hi].astype(f32)
        for r in ins[1:]:
            total += r[:, lo:hi].astype(f32)
        if turned and c == len(cuts) - 1:
            turn = refs[-1]
            rows = total.shape[0]
            turn[...] = jnp.zeros_like(turn)
            turn[0:rows, :] = total
            out[...] = turn[...].T[: out.shape[0], : out.shape[1]]
        else:
            out[...] = total


def last_sum(outs, Z, widths, turned=0):
    rows = outs[0].shape[0]
    got = [lax.ppermute(outs[k], "dp", pairs(Z, k)) for k in range(1, Z)]
    cuts = cut_points(widths)
    shapes = [(rows, w) for w in widths]
    if turned:
        shapes[-1] = (turned, rows)
    return plain(
        functools.partial(last_body, Z, cuts, turned), "last_sum", (outs[0], *got), [WHOLE] * Z,
        [sds(s, f32) for s in shapes], [WHOLE] * len(cuts), moved=2 * (Z + 2) * rows * cuts[-1][1],
        scratch=[pltpu.VMEM((LANES, LANES), f32)] if turned else [],
    )


def local(
    Z, N, tokens, input_weight, query_bias, value_bias, output_weight, output_bias, first_gain, first_shift,
    up_weight, up_bias, down_weight, down_bias, second_gain, second_shift, retriever_weight, document_table,
    document_index, output_grad, score_grad,
):
    both = ("dp", "fsdp")
    T, D = tokens.shape
    rows = input_weight.shape[0]
    F = up_weight.shape[1]
    Rw = retriever_weight.shape[1]
    seqs = document_index.shape[0]
    L = T // seqs
    gc = 4 * HEAD_DIM
    G = D // gc
    Q = F // D
    me = jnp.stack([lax.axis_index("dp"), lax.axis_index("fsdp")]).astype(jnp.int32)

    trows, drows = document_table.shape[0], down_weight.shape[0]
    folds = -(-trows // drows)
    folded = jnp.pad(document_table, ((0, folds * drows - trows), (0, 0)))
    wd = lax.all_gather(
        jnp.concatenate([down_weight] + [folded[i * drows : (i + 1) * drows] for i in range(folds)], axis=1),
        both, axis=0, tiled=True,
    )

    vectors = jnp.concatenate(
        [query_bias, value_bias, output_bias, first_gain, first_shift, down_bias, second_gain, second_shift, up_bias]
    ).reshape(8 + Q, rows)
    head, rest = pack(input_weight, output_weight, retriever_weight, vectors, gc)
    head = spread_dp(head, Z)
    rest = spread_dp(after(rest, head), Z)
    wu = spread_dp(after(up_weight, rest), Z)
    head = spread_fsdp(head, N)
    rest = spread_fsdp(after(rest, *head), N)
    wu = spread_fsdp(after(wu, *rest), N)
    win = [None] * G
    win[0], _, vec = place(me, head, [3 * gc, LANES], turned=16)
    vec, tok = lax.optimization_barrier((vec, tokens))
    qb, vb, ob, fg, fs, db, sg, ss = (vec[i : i + 1] for i in range(8))
    ub = vec[8 : 8 + Q].reshape(Q, Z * N, rows).transpose(1, 0, 2).reshape(1, F)

    qkv, soft, ctx = [None] * G, [None] * G, [None] * G

    def attend_group(g):
        cols = slice(g * gc, (g + 1) * gc)
        qkv[g], soft[g], ctx[g] = attend(tokens, win[g], qb[:, cols], vb[:, cols], seqs)

    attend_group(0)
    rest = [after(p, ctx[0]) for p in rest]
    *win[1:], wo, wr = place(me, rest, [3 * gc] * (G - 1) + [D, Rw])
    for g in range(1, G):
        attend_group(g)
    (wu,) = place(me, [after(p, ctx[G - 1]) for p in wu], [F])
    n, inv, first, act, slope = up(ctx, tokens, wo, ob, fg, fs, wu, ub, L)

    owner, within = document_index // trows, document_index % trows
    at_row, at_col = owner * drows + within % drows, D + Rw * (within // drows)
    chosen = jnp.concatenate([lax.dynamic_slice(wd, (at_row[s], at_col[s]), (1, Rw)) for s in range(seqs)], axis=0)
    back_projected = (score_grad[:, None] * chosen.astype(f32)).astype(bf16)
    lead = dot(back_projected, wr, 1, 1)
    final, two, feed, inner, gsg, gss, gdb, gub = down(
        first, act, slope, wd, db, sg, ss, output_grad, lead.reshape(seqs, 1, D), seqs
    )
    leading = final.reshape(seqs, L, D)[:, 0]
    projected = dot(leading, wr).astype(bf16).astype(f32)
    scores = jnp.sum(projected * chosen.astype(f32), axis=-1)
    retriever_back = dot(leading, back_projected, 0, 0)

    term = jnp.concatenate(
        [score_grad[:, None] * projected, jnp.broadcast_to(document_index[:, None].astype(f32), (seqs, LANES))], axis=1
    )
    term = jnp.pad(term, ((0, 32 - seqs), (0, 0)))
    term = lax.all_gather(term, both, axis=0, tiled=True).reshape(Z * N, 32, -1)[:, :seqs].reshape(Z * N * seqs, -1)
    ids = term[:, Rw].astype(jnp.int32) - (me[0] * N + me[1]) * trows
    picker = (jnp.arange(trows, dtype=jnp.int32)[:, None] == ids[None, :]).astype(f32)
    table_back = jnp.dot(picker, term[:, :Rw], precision=lax.Precision.HIGHEST)

    down_back = grad_rows(act, feed, "down_grad", D)
    inner, down_back = lax.optimization_barrier((inner, down_back))
    down_back = lax.psum_scatter(down_back, both, scatter_dimension=0, tiled=True).astype(f32)
    up_parts = grads(me, Z, N, "up_grad", [([first], inner)], tile=D)
    two, *up_parts = lax.optimization_barrier((two, *up_parts))
    one, att, bctx, gfg, gfs, gob = mid(two, inner, wu, n, inv, fg, wo, L)
    up_sums = pair_sum(up_parts, Z, N)
    mixed, gq, gv = [None] * G, [None] * G, [None] * G
    for g in range(G - 1):
        mixed[g], gq[g], gv[g] = attend_back(qkv[g], soft[g], ctx[g], bctx, g, seqs)
    gub = gub.reshape(Z * N, Q, rows).transpose(1, 0, 2).reshape(Q, D)
    parts = grads(
        me, Z, N, "mix_grad", [(ctx, att)] + [([tokens], mixed[g]) for g in range(G - 1)],
        retr=retriever_back, vectors=[gob, gfg, gfs, gdb, gsg, gss, gub],
    )
    bctx, *parts = lax.optimization_barrier((bctx, *parts))
    up_sums = chips_sum(me, up_sums, Z, N)
    mix_sums = pair_sum(parts, Z, N)
    g = G - 1
    mixed[g], gq[g], gv[g] = attend_back(qkv[g], soft[g], ctx[g], bctx, g, seqs)
    parts = grads(
        me, Z, N, "in_grad", [([tokens], mixed[g])],
        vectors=[jnp.concatenate(gq, axis=1), jnp.concatenate(gv, axis=1)],
    )
    one, *parts = lax.optimization_barrier((one, *parts))
    in_sums = pair_sum(parts, Z, N)
    back_tokens = tokens_back(one, mixed, win, L)
    (up_back,) = last_sum(up_sums, Z, [F])
    mix_sums = chips_sum(me, mix_sums, Z, N)
    in_sums = chips_sum(me, in_sums, Z, N)
    output_back, *pieces, retriever_back, small_one = last_sum(mix_sums, Z, [D] + [3 * gc] * (G - 1) + [Rw, LANES], turned=16)
    last, small_two = last_sum(in_sums, Z, [3 * gc, LANES], turned=8)
    pieces += [last]
    input_back = jnp.concatenate([p[:, m * gc : (m + 1) * gc] for m in range(3) for p in pieces], axis=1)
    ob_back, fg_back, fs_back, db_back, sg_back, ss_back = (small_one[i] for i in range(6))
    ub_back = small_one[6 : 6 + Q].reshape(-1)
    return (
        final, scores, back_tokens, input_back, small_two[0], small_two[1], output_back, ob_back, fg_back, fs_back,
        up_back, ub_back, down_back, db_back, sg_back, ss_back, retriever_back, table_back,
    )


def solution(mesh):
    both = ("dp", "fsdp")
    mat, vec = P(both, None), P(both)
    in_specs = (mat, mat, vec, vec, mat, vec, vec, vec, mat, vec, mat, vec, vec, vec, mat, mat, vec, mat, vec)
    out_specs = (mat, vec, mat, mat, vec, vec, mat, vec, vec, vec, mat, vec, mat, vec, vec, vec, mat, mat)
    body = functools.partial(local, mesh.shape["dp"], mesh.shape["fsdp"])
    return jax.shard_map(body, mesh=mesh, in_specs=in_specs, out_specs=out_specs, check_vma=False)
```

```python
import functools
import math
import jax
import jax.numpy as jnp
from jax import lax
from jax.experimental import pallas as pl
from jax.experimental.pallas import tpu as pltpu
from jax.sharding import PartitionSpec as P

HEAD_DIM = 64
EPS = 1e-12
QB, VB, OB, FG, FS, DB, SG, SS, UB = range(9)
bf16, f32 = jnp.bfloat16, jnp.float32
ERFC_P = 0.33
ERFC_Q = (-0.1359291, 0.46268956, -0.35544136, 0.41254396, 0.04500932, 0.20192425, 0.18283717, 0.18636611)


def dot(a, b, ca=1, cb=0):
    return lax.dot_general(a, b, (((ca,), (cb,)), ((), ())), preferred_element_type=f32)


def rows_spec(rows, cols):
    return pl.BlockSpec((rows, cols), lambda i: (i, 0))


def full_spec(shape):
    return pl.BlockSpec(shape, lambda *_: (0,) * len(shape))


def head_mask(rows, cols, h):
    lane = lax.broadcasted_iota(jnp.int32, (rows, cols), 1)
    return (lane >= h * HEAD_DIM) & (lane < (h + 1) * HEAD_DIM)


def run(body, name, grid, ins, in_specs, outs, out_specs, scratch=(), flops=0, moved=0, vmem=60, alias=None):
    return pl.pallas_call(
        body,
        name=name,
        grid=grid,
        in_specs=in_specs,
        out_specs=out_specs,
        out_shape=outs,
        scratch_shapes=list(scratch),
        cost_estimate=estimate(flops, moved),
        input_output_aliases=alias or {},
        compiler_params=pltpu.CompilerParams(vmem_limit_bytes=vmem * 2**20),
    )(*ins)


def estimate(flops, moved):
    return pl.CostEstimate(flops=int(flops), bytes_accessed=int(moved), transcendentals=0)


def sds(shape, dtype):
    return jax.ShapeDtypeStruct(shape, dtype)


def attend_body(x_ref, w_ref, v_ref, qkv_ref, soft_ref, ctx_ref):
    length = x_ref.shape[0]
    gc = ctx_ref.shape[1]
    mixed = dot(x_ref[...], w_ref[...])
    q = (mixed[:, :gc] + v_ref[QB : QB + 1, :]).astype(bf16)
    k = mixed[:, gc : 2 * gc].astype(bf16)
    v = (mixed[:, 2 * gc :] + v_ref[VB : VB + 1, :]).astype(bf16)
    qkv_ref[:, :gc] = q
    qkv_ref[:, gc : 2 * gc] = k
    qkv_ref[:, 2 * gc :] = v
    qs = q * bf16(HEAD_DIM ** -0.5)
    zero = jnp.zeros((), bf16)
    total = jnp.zeros((length, gc), f32)
    for h in range(gc // HEAD_DIM):
        mask = head_mask(length, gc, h)
        s = dot(jnp.where(mask, qs, zero), k, 1, 1)
        peak = jnp.max(s, axis=-1, keepdims=True)
        e = jnp.exp(s - peak)
        norm = 1.0 / jnp.sum(e, axis=-1, keepdims=True)
        p = (e * norm).astype(bf16)
        soft_ref[h] = p
        total += dot(p, jnp.where(mask, v, zero))
    ctx_ref[...] = total.astype(bf16)


def attend(x, w, vec, g, seqs):
    T, D = x.shape
    gc = w.shape[1] // 3
    hg = gc // HEAD_DIM
    L = T // seqs
    return run(
        attend_body, "attend", (seqs,), (x, w, vec),
        [rows_spec(L, D), full_spec(w.shape), pl.BlockSpec((vec.shape[0], gc), lambda i: (0, g))],
        [sds((T, 3 * gc), bf16), sds((hg, T, L), bf16), sds((T, gc), bf16)],
        [rows_spec(L, 3 * gc), pl.BlockSpec((hg, L, L), lambda i: (0, i, 0)), rows_spec(L, gc)],
        flops=2 * T * D * 3 * gc + 16 * T * L * gc, moved=2 * (T * D + w.size + 4 * T * gc + hg * T * L),
    )


def erfc_parts(u):
    e = jnp.exp(u * u * -0.5)
    t = 1.0 / (1.0 + (ERFC_P * math.sqrt(0.5)) * jnp.abs(u))
    q = jnp.full_like(t, 0.5 * ERFC_Q[0])
    for c in ERFC_Q[1:]:
        q = q * t + 0.5 * c
    return q * t * e, e


def norm_rows(h):
    mean = jnp.mean(h, axis=-1, keepdims=True)
    c = h - mean
    var = jnp.mean(c * c, axis=-1, keepdims=True)
    inv = lax.rsqrt(var + EPS)
    return c * inv, inv


def norm_rows_back(cot, n, inv, gain):
    scaled = cot * gain
    return inv * (scaled - jnp.mean(scaled, axis=-1, keepdims=True) - n * jnp.mean(scaled * n, axis=-1, keepdims=True))


def up_body(ngroups, step, *refs):
    ctx_refs = refs[:ngroups]
    x_ref, wo_ref, v_ref, wu_ref, ub_ref = refs[ngroups : ngroups + 5]
    n_ref, inv_ref, first_ref, act_ref, slope_ref = refs[ngroups + 5 :]
    gc = ctx_refs[0].shape[1]
    hidden = x_ref[...].astype(f32) + v_ref[OB : OB + 1, :]
    for g, c in enumerate(ctx_refs):
        hidden += dot(c[...], wo_ref[g * gc : (g + 1) * gc, :])
    n, inv = norm_rows(hidden)
    n_ref[...] = n
    inv_ref[...] = inv
    first = (n * v_ref[FG : FG + 1, :] + v_ref[FS : FS + 1, :]).astype(bf16)
    first_ref[...] = first
    ff = wu_ref.shape[1]
    for at in range(0, ff, step):
        cols = slice(at, at + step)
        u = dot(first, wu_ref[:, cols]) + ub_ref[:, cols]
        tail, e = erfc_parts(u)
        phi = jnp.where(u < 0, tail, 1.0 - tail)
        act_ref[:, cols] = (u * phi).astype(bf16)
        slope_ref[:, cols] = (phi + u * e * (1.0 / math.sqrt(2 * math.pi))).astype(bf16)


def up(ctxs, x, wo, vec, wu, ub, rows, step=512):
    T, D = x.shape
    F = ub.shape[1]
    return run(
        functools.partial(up_body, len(ctxs), step), "up", (T // rows,), (*ctxs, x, wo, vec, wu, ub),
        [rows_spec(rows, c.shape[1]) for c in ctxs] + [rows_spec(rows, D)] + [full_spec(wo.shape), full_spec(vec.shape), full_spec((D, F)), full_spec(ub.shape)],
        [sds((T, D), f32), sds((T, 1), f32), sds((T, D), bf16), sds((T, F), bf16), sds((T, F), bf16)],
        [rows_spec(rows, D), rows_spec(rows, 1), rows_spec(rows, D), rows_spec(rows, F), rows_spec(rows, F)],
        flops=2 * T * D * (D + F), moved=T * D * 10 + 4 * T * F + 2 * (wo.size + wu.size),
    )


def add_rows(ref, value):
    @pl.when(pl.program_id(0) == 0)
    def _():
        ref[...] = jnp.zeros_like(ref)
    ref[...] += jnp.sum(value, axis=0, keepdims=True)


def down_body(step, first_ref, act_ref, slope_ref, w_ref, v_ref, og_ref, lead_ref,
              out_ref, top_ref, two_ref, feed_ref, inner_ref, gg_ref, gs_ref, gb_ref, gub_ref):
    rows = first_ref.shape[0]
    gain = v_ref[SG : SG + 1, :]
    hidden = first_ref[...].astype(f32) + v_ref[DB : DB + 1, :] + dot(act_ref[...], w_ref[...])
    n, inv = norm_rows(hidden)
    out = (n * gain + v_ref[SS : SS + 1, :]).astype(bf16)
    out_ref[...] = out
    top_ref[0] = out[0:16, :].astype(f32)[0:1, :]
    row = lax.broadcasted_iota(jnp.int32, (rows, 1), 0)
    cot = og_ref[...].astype(f32) + jnp.where(row == 0, lead_ref[0], 0.0)
    add_rows(gg_ref, cot * n)
    add_rows(gs_ref, cot)
    two = norm_rows_back(cot, n, inv, gain)
    two_ref[...] = two
    feed = two.astype(bf16)
    feed_ref[...] = feed
    add_rows(gb_ref, feed.astype(f32))
    ff = w_ref.shape[0]
    for at in range(0, ff, step):
        cols = slice(at, at + step)
        inner = (dot(feed, w_ref[cols, :], 1, 1) * slope_ref[:, cols].astype(f32)).astype(bf16)
        inner_ref[:, cols] = inner
        @pl.when(pl.program_id(0) == 0)
        def _():
            gub_ref[:, cols] = jnp.zeros((1, step), f32)
        gub_ref[:, cols] += jnp.sum(inner.astype(f32), axis=0, keepdims=True)


def down(first, act, slope, w, vec, og, lead, seqs, step=512):
    T, D = first.shape
    F = act.shape[1]
    L = T // seqs
    return run(
        functools.partial(down_body, step), "down", (seqs,), (first, act, slope, w, vec, og, lead),
        [rows_spec(L, D), rows_spec(L, F), rows_spec(L, F)] + [full_spec((F, D)), full_spec(vec.shape)]
        + [rows_spec(L, D), pl.BlockSpec((1, 1, D), lambda i: (i, 0, 0))],
        [sds((T, D), bf16), sds((seqs, 1, D), f32), sds((T, D), f32), sds((T, D), bf16), sds((T, F), bf16),
         sds((1, D), f32), sds((1, D), f32), sds((1, D), f32), sds((1, F), f32)],
        [rows_spec(L, D), pl.BlockSpec((1, 1, D), lambda i: (i, 0, 0)), rows_spec(L, D), rows_spec(L, D), rows_spec(L, F)] + [full_spec((1, D))] * 3 + [full_spec((1, F))],
        flops=4 * T * D * F, moved=6 * T * F + 12 * T * D + 2 * w.size,
    )


def mid_body(two_ref, inner_ref, wu_ref, n_ref, inv_ref, v_ref, wo_ref,
             one_ref, att_ref, bctx_ref, gg_ref, gs_ref, gob_ref):
    cot = two_ref[...] + dot(inner_ref[...], wu_ref[...], 1, 1)
    n = n_ref[...]
    add_rows(gg_ref, cot * n)
    add_rows(gs_ref, cot)
    one = norm_rows_back(cot, n, inv_ref[...], v_ref[FG : FG + 1, :])
    one_ref[...] = one
    att = one.astype(bf16)
    att_ref[...] = att
    add_rows(gob_ref, att.astype(f32))
    bctx_ref[...] = dot(att, wo_ref[...], 1, 1).astype(bf16)


def mid(two, inner, wu, n, inv, vec, wo, rows):
    T, D = two.shape
    F = inner.shape[1]
    return run(
        mid_body, "mid", (T // rows,), (two, inner, wu, n, inv, vec, wo),
        [rows_spec(rows, D), rows_spec(rows, F), full_spec((D, F)), rows_spec(rows, D), rows_spec(rows, 1), full_spec(vec.shape), full_spec(wo.shape)],
        [sds((T, D), f32), sds((T, D), bf16), sds((T, D), bf16)] + [sds((1, D), f32)] * 3,
        [rows_spec(rows, D)] * 3 + [full_spec((1, D))] * 3,
        flops=2 * T * D * (F + D), moved=2 * T * F + 16 * T * D + 2 * wu.size,
    )


def attend_back_body(qkv_ref, soft_ref, ctx_ref, bctx_ref, out_ref, gq_ref, gv_ref):
    length, gc = ctx_ref.shape
    q = qkv_ref[:, :gc]
    k = qkv_ref[:, gc : 2 * gc]
    v = qkv_ref[:, 2 * gc :]
    do = bctx_ref[...]
    prod = do.astype(f32) * ctx_ref[...].astype(f32)
    zero = jnp.zeros((), bf16)
    dq = jnp.zeros((length, gc), f32)
    dk = jnp.zeros((length, gc), f32)
    dv = jnp.zeros((length, gc), f32)
    for h in range(gc // HEAD_DIM):
        mask = head_mask(length, gc, h)
        p = soft_ref[h]
        do_h = jnp.where(mask, do, zero)
        dp = dot(do_h, v, 1, 1)
        delta = jnp.sum(jnp.where(mask, prod, 0.0), axis=-1, keepdims=True)
        ds = (p.astype(f32) * (dp - delta)).astype(bf16)
        dv += dot(p, do_h, 0, 0)
        dq += dot(ds, jnp.where(mask, k, zero))
        dk += dot(ds, jnp.where(mask, q, zero), 0, 0)
    scale = HEAD_DIM ** -0.5
    dq = (dq * scale).astype(bf16)
    dv = dv.astype(bf16)
    out_ref[:, :gc] = dq
    out_ref[:, gc : 2 * gc] = (dk * scale).astype(bf16)
    out_ref[:, 2 * gc :] = dv
    add_rows(gq_ref, dq.astype(f32))
    add_rows(gv_ref, dv.astype(f32))


def attend_back(qkv, soft, ctx, bctx, g, seqs):
    T, gc = ctx.shape
    hg = gc // HEAD_DIM
    L = T // seqs
    return run(
        attend_back_body, "attend_back", (seqs,), (qkv, soft, ctx, bctx),
        [rows_spec(L, 3 * gc), pl.BlockSpec((hg, L, L), lambda i: (0, i, 0)), rows_spec(L, gc), pl.BlockSpec((L, gc), lambda i: (i, g))],
        [sds((T, 3 * gc), bf16), sds((1, gc), f32), sds((1, gc), f32)],
        [rows_spec(L, 3 * gc), full_spec((1, gc)), full_spec((1, gc))],
        flops=32 * T * L * gc, moved=2 * (8 * T * gc + hg * T * L),
    )


def tokens_back_body(ngroups, one_ref, *refs):
    total = one_ref[...]
    for g in range(ngroups):
        total += dot(refs[g][...], refs[ngroups + g][...], 1, 1)
    refs[-1][...] = total.astype(bf16)


def tokens_back(one, mixed, ws, rows):
    T, D = one.shape
    n = len(mixed)
    return run(
        functools.partial(tokens_back_body, n), "tokens_back", (T // rows,), (one, *mixed, *ws),
        [rows_spec(rows, D)] + [rows_spec(rows, m.shape[1]) for m in mixed] + [full_spec(w.shape) for w in ws],
        sds((T, D), bf16), rows_spec(rows, D),
        flops=2 * T * D * sum(m.shape[1] for m in mixed), moved=T * D * 12,
    )


def after(x, *deps):
    return lax.optimization_barrier((x,) + deps)[0]


ANY = pl.BlockSpec(memory_space=pl.ANY)
SMEM = pl.BlockSpec(memory_space=pltpu.SMEM)
LANES = 128


def once(body, name, ins, in_specs, outs, scratch=(), moved=0, flops=0, vmem=60):
    specs = [full_spec(a.shape) if spec is None else spec for a, spec in zip(ins, in_specs)]
    return run(body, name, (1,), ins, specs, outs, [full_spec(o.shape) for o in outs], scratch, flops, moved, vmem)


def cut_points(widths):
    cuts, at = [], 0
    for w in widths:
        cuts.append((at, at + w))
        at += w
    return cuts


def pack_body(D, gc, nvec, *refs):
    w_ref, o_ref, r_ref, u_ref, t_ref = refs[:5]
    head_ref, rest_ref, up_ref, held = refs[5 + nvec :]
    G = D // gc
    rows = w_ref.shape[0]
    held[...] = jnp.zeros_like(held)
    row = 0
    for v_ref in refs[5 : 5 + nvec]:
        v = v_ref[...].astype(f32)
        for at in range(0, v.shape[1], rows):
            held[row : row + 1, 0:rows] = v[:, at : at + rows]
            row += 1
    turned = held[...].T
    for m in range(3):
        head_ref[:, m * gc : (m + 1) * gc] = w_ref[:, m * D : m * D + gc]
    head_ref[:, 3 * gc :] = turned[:rows, :].astype(bf16)
    at = 0
    for g in range(1, G):
        for m in range(3):
            rest_ref[:, at : at + gc] = w_ref[:, m * D + g * gc : m * D + (g + 1) * gc]
            at += gc
    rest_ref[:, at : at + D] = o_ref[...]
    rest_ref[:, at + D :] = r_ref[...]
    trows, width = t_ref.shape
    at = u_ref.shape[1]
    up_ref[:, :at] = u_ref[...]
    for lo in range(0, trows, rows):
        n = min(rows, trows - lo)
        up_ref[:n, at : at + width] = t_ref[lo : lo + n, :]
        if n < rows:
            up_ref[n:, at : at + width] = jnp.zeros((rows - n, width), bf16)
        at += width


def pack(w, o, r, u, t, vectors, gc):
    rows, D = o.shape
    head = 3 * gc + LANES
    rest = 3 * D - 3 * gc + D + r.shape[1]
    ups = u.shape[1] + -(-t.shape[0] // rows) * t.shape[1]
    return once(
        functools.partial(pack_body, D, gc, len(vectors)), "pack", (w, o, r, u, t, *vectors), [None] * (5 + len(vectors)),
        [sds((rows, head), bf16), sds((rows, rest), bf16), sds((rows, ups), bf16)],
        scratch=[pltpu.VMEM((LANES, LANES), f32)], moved=4 * rows * (head + rest + ups),
    )


def pairs(n, flip):
    return [(i, i ^ flip) for i in range(n)]


def along_dp(block, Z):
    return [block] + [lax.ppermute(block, "dp", pairs(Z, k)) for k in range(1, Z)]


def between_chips(blocks, N):
    return lax.all_to_all(blocks, "fsdp", 0, 0, axis_index_groups=[list(range(c, N, 2)) for c in range(2)], tiled=True)


def other_core(blocks, N):
    return lax.ppermute(blocks, "fsdp", pairs(N, 1))


def repeat_body(*refs):
    out = refs[-1]
    for r in range(out.shape[0]):
        for k, ref in enumerate(refs[:-1]):
            out[r, k] = ref[...]


def repeat(blocks, R):
    n = len(blocks)
    return once(
        repeat_body, "repeat", blocks, [None] * n, [sds((R, n) + blocks[0].shape, bf16)], moved=2 * (R + 1) * n * blocks[0].size
    )[0]


def place_body(n, cuts, turned, me_ref, *refs):
    pieces = refs[:n]
    outs = refs[n : n + len(cuts)]
    vec_ref = refs[n + len(cuts)] if turned else None
    held = refs[n + len(cuts) + turned : n + 2 * len(cuts) + turned]
    flat = refs[-3] if turned else None
    in_sem, out_sem = refs[-2:]
    Z = held[0].shape[0]
    copies = []
    for k in range(Z):
        for other in range(2):
            piece = pieces[other].at[:, k] if n == 2 else pieces[other * Z + k]
            for c, (lo, hi) in enumerate(cuts):
                copy = pltpu.make_async_copy(
                    piece.at[:, :, lo:hi], held[c].at[me_ref[0] ^ k, :, me_ref[2] ^ other], in_sem.at[len(copies)]
                )
                copies.append((copy, k))
    for copy, _ in copies:
        copy.start()
    last = []
    for k in range(Z):
        for copy, slot in copies:
            if slot == k:
                copy.wait()
        for c in range(len(cuts)):
            z = me_ref[0] ^ k
            last.append(pltpu.make_async_copy(held[c].at[z], outs[c].at[z], out_sem.at[k * len(cuts) + c]))
            last[-1].start()
    if turned:
        for z in range(Z):
            for r in range(held[-1].shape[1]):
                for c in range(2):
                    flat[z, r, c] = held[-1][z, r, c].astype(f32)
        vec_ref[...] = flat[...].reshape(vec_ref.shape[1], LANES).T[: vec_ref.shape[0]]
    for copy in last:
        copy.wait()


def place(me, pieces, Z, widths, turned=0):
    n = len(pieces)
    R, rows = pieces[0].shape[0], pieces[0].shape[-2]
    cuts = cut_points(widths)
    if turned and rows % 8:
        outs = place(me, pieces, Z, widths)
        return outs + [outs[-1][:, :turned].T.astype(f32)]
    shapes = [(Z, R, 2, rows, w) for w in widths]
    total = 2 * Z * R * rows
    outs = run(
        functools.partial(place_body, n, cuts, 1 if turned else 0), "place", (1,), (me, *pieces), [SMEM] + [ANY] * n,
        [sds(s, bf16) for s in shapes] + ([sds((turned, total), f32)] if turned else []),
        [ANY] * len(cuts) + ([full_spec((turned, total))] if turned else []),
        scratch=[pltpu.VMEM(s, bf16) for s in shapes] + ([pltpu.VMEM(shapes[-1], f32)] if turned else [])
        + [pltpu.SemaphoreType.DMA((2 * Z * len(cuts),)), pltpu.SemaphoreType.DMA((Z * len(cuts),))],
        moved=4 * total * cuts[-1][1], vmem=60,
    )
    return [o.reshape(total, o.shape[-1]) for o in outs[: len(cuts)]] + list(outs[len(cuts) :])


def hand_out(me_ref, held, keep_ref, send_ref):
    Z, R = held.shape[:2]
    for r in range(R):
        for z in range(Z):
            keep_ref[r, z] = held[z, r, me_ref[2]].astype(bf16)
            send_ref[r, z] = held[z, r, 1 - me_ref[2]].astype(bf16)


def grads_body(counts, nvec, has_retr, me_ref, *refs):
    at_held = len(refs) - 1 - (2 if nvec else 0)
    held = refs[at_held]
    Z, R, _, rows, _ = held.shape
    D = Z * R * 2 * rows
    at, col = 0, 0
    for n in counts:
        y = refs[at + n][...]
        parts = [dot(r[...], y, 0, 0) for r in refs[at : at + n]]
        part = parts[0] if n == 1 else jnp.concatenate(parts, axis=0)
        w = part.shape[1]
        held[:, :, :, :, col : col + w] = part.reshape(Z, R, 2, rows, w)
        at += n + 1
        col += w
    if has_retr:
        w = refs[at].shape[1]
        held[:, :, :, :, col : col + w] = refs[at][...].reshape(Z, R, 2, rows, w)
        at += 1
        col += w
    if nvec:
        turn = refs[-1]
        turn[...] = jnp.zeros_like(turn)
        row, lane = 0, 0
        for r in refs[at : at + nvec]:
            w = r.shape[1]
            if w <= D:
                turn[row : row + 1, lane : lane + w] = r[...]
                lane += w
                if lane == D:
                    row, lane = row + 1, 0
        total = turn[...].T.reshape(Z, R, 2, rows, LANES)
        r = refs[at + nvec - 1]
        if r.shape[1] > D:
            Q = r.shape[1] // D
            wide = refs[-2]
            wide[...] = jnp.zeros_like(wide)
            place_of = lax.broadcasted_iota(jnp.int32, r.shape, 1) % (Q * rows) // rows
            for q in range(Q):
                wide[row + q : row + q + 1, :] = jnp.where(place_of == q, r[...], 0.0)
            spread = wide[...].T.reshape(Z * R * 2, Q, rows, LANES)
            for q in range(Q):
                total += spread[:, q].reshape(total.shape)
        held[:, :, :, :, col:] = total
    hand_out(me_ref, held, refs[at_held - 2], refs[at_held - 1])


def hand_out_plain(me, whole, Z, N, rows):
    whole = whole.astype(bf16).reshape(Z, N // 2, 2, rows, -1).swapaxes(0, 1)
    return [lax.dynamic_index_in_dim(whole, c, 2, keepdims=False) for c in (me[2], 1 - me[2])]


def grads(me, Z, N, name, products, retr=None, vectors=(), tile=None):
    counts = [len(xs) for xs, _ in products]
    D = sum(x.shape[1] for x in products[0][0])
    rows, R = D // (Z * N), N // 2
    width = sum(y.shape[1] for _, y in products) + (0 if retr is None else retr.shape[1]) + (LANES if vectors else 0)
    if rows % 8:
        cols = [jnp.concatenate([dot(x, y, 0, 0) for x in xs], axis=0) for xs, y in products]
        cols += [] if retr is None else [retr]
        if vectors:
            narrow = jnp.concatenate([v for v in vectors if v.shape[1] <= D], axis=1).reshape(-1, D)
            wide = [v.reshape(Z * N, -1, rows).swapaxes(0, 1).reshape(-1, D) for v in vectors if v.shape[1] > D]
            turned = jnp.concatenate([narrow] + wide, axis=0).T
            cols += [turned, jnp.zeros((D, LANES - turned.shape[1]), f32)]
        return hand_out_plain(me, jnp.concatenate(cols, axis=1), Z, N, rows)
    ins = [a for xs, y in products for a in (*xs, y)] + ([] if retr is None else [retr]) + list(vectors)
    T = products[0][1].shape[0]
    if tile is None:
        tile, specs, grid = width, [full_spec(a.shape) for a in ins], (1,)
    else:
        specs, grid = [full_spec(ins[0].shape), pl.BlockSpec((T, tile), lambda i: (0, i))], (width // tile,)
    return run(
        functools.partial(grads_body, counts, len(vectors), retr is not None), name, grid, (me, *ins), [SMEM] + specs,
        [sds((R, Z, rows, width), bf16)] * 2, [pl.BlockSpec((R, Z, rows, tile), lambda i: (0, 0, 0, i))] * 2,
        scratch=[pltpu.VMEM((Z, R, 2, rows, tile), f32)]
        + ([pltpu.VMEM((LANES, max(D, vectors[-1].shape[1])), f32), pltpu.VMEM((LANES, D), f32)] if vectors else []),
        flops=2 * T * D * width, moved=2 * T * (D + width) + 2 * D * width,
    )


def down_grad_body(me_ref, x_ref, y_ref, keep_ref, send_ref, held):
    held[...] = dot(x_ref[...], y_ref[...], 0, 0).reshape(held.shape)
    hand_out(me_ref, held, keep_ref, send_ref)


def down_grad(me, Z, N, act, feed):
    T, D = feed.shape
    F = act.shape[1]
    R, rows = N // 2, F // (Z * N)
    if rows % 8:
        return hand_out_plain(me, dot(act, feed, 0, 0), Z, N, rows)
    return run(
        down_grad_body, "down_grad", (Z,), (me, act, feed),
        [SMEM, pl.BlockSpec((T, N * rows), lambda i: (0, i)), full_spec(feed.shape)],
        [sds((R, Z, rows, D), bf16)] * 2, [pl.BlockSpec((R, 1, rows, D), lambda i: (0, i, 0, 0))] * 2,
        scratch=[pltpu.VMEM((1, R, 2, rows, D), f32)], flops=2 * T * F * D, moved=2 * (T * F + T * D + F * D),
    )


def pair_body(n, me_ref, *refs):
    out_ref = refs[-1]
    width = out_ref.shape[3]
    at = 0
    for keep_ref, got_ref in zip(refs[:n], refs[n : 2 * n]):
        rows = keep_ref.shape[2]
        for lo in range(0, keep_ref.shape[3], width):
            cols = slice(lo, lo + width)
            out_ref[:, :, at : at + rows, :] = (
                keep_ref[:, :, :, cols].astype(f32) + got_ref[:, :, :, cols].astype(f32)
            ).astype(bf16)
            at += rows
    if len(refs) > 2 * n + 1:
        mine, other = refs[2 * n][...].astype(f32), refs[2 * n + 1][...].astype(f32)
        first = me_ref[2] == 0
        both = [jnp.where(first, mine, other), jnp.where(first, other, mine)]
        n_rows, w = mine.shape
        line = jnp.concatenate(both + [jnp.zeros((n_rows, width - 2 * w), f32)], axis=1).astype(bf16)
        for z in range(out_ref.shape[1]):
            out_ref[0, z, at : at + n_rows, :] = line


def pair_sum(parts, N, tok, me=None, term=None):
    n = len(parts)
    keeps = [keep for keep, _ in parts]
    got = [other_core(send, N) for _, send in parts]
    R, Z, _, width = keeps[0].shape
    rows = sum(k.size for k in keeps) // (R * Z * width)
    keeps[0] = after(keeps[0], tok)
    ins = keeps + got
    specs = [pl.BlockSpec((1,) + a.shape[1:], lambda i: (i, 0, 0, 0)) for a in ins]
    if term is not None:
        ins += [term, other_core(term, N)]
        specs += [full_spec(term.shape)] * 2
        rows += term.shape[0]
    return run(
        functools.partial(pair_body, n), "pair_sum", (R,), [jnp.zeros((3,), jnp.int32) if me is None else me] + ins, [SMEM] + specs,
        sds((R, Z, rows, width), bf16), pl.BlockSpec((1, Z, rows, width), lambda i: (i, 0, 0, 0)), moved=6 * R * Z * rows * width, vmem=60,
    )


def spots(n, width, shape):
    each = width // shape[1]
    return [(t // each * shape[0], t % each * shape[1]) for t in range(n)], -(-n // each) * shape[0]


def chips_body(term, me_ref, in_ref, *outs):
    R, _, rows, width = in_ref.shape
    rows -= term[0]
    where, _ = spots(2 * R, width, term)
    for k, out in enumerate(outs):
        z = me_ref[0] ^ k
        total = in_ref[0, z, :rows].astype(f32)
        for r in range(1, R):
            total += in_ref[r, z, :rows].astype(f32)
        out[:rows, :] = total.astype(out.dtype)
        if term[0]:
            out[rows:, :] = jnp.zeros((out.shape[0] - rows, width), out.dtype)
            for t, (row, col) in enumerate(where):
                tile = in_ref[t // 2, z, rows : rows + term[0], t % 2 * term[1] : (t % 2 + 1) * term[1]]
                out[rows + row : rows + row + term[0], col : col + term[1]] = tile.astype(out.dtype)


def chips_sum(me, got, tok, term=(0, LANES)):
    R, Z, rows, width = got.shape
    rows += spots(2 * R, width, term)[1] - term[0]
    return once(
        functools.partial(chips_body, term), "chips_sum", (me, after(got, tok)), [SMEM, None],
        [sds((rows, width), f32)] + [sds((rows, width), bf16)] * (Z - 1), moved=2 * got.size + 2 * Z * rows * width,
    )


def total_of(parts, lo, hi, rows=None):
    total = parts[0][:rows, lo:hi].astype(f32)
    for p in parts[1:]:
        total += p[:rows, lo:hi].astype(f32)
    return total


def last_body(n, cuts, G, gc, *refs):
    parts, (in_ref, out_ref, retr_ref, small_ref, turn) = refs[:n], refs[n:]
    rows = parts[0].shape[0]
    out_ref[...] = total_of(parts, *cuts[0])
    for g in range(G):
        group = total_of(parts, *cuts[1 + g])
        for m in range(3):
            in_ref[:, (m * G + g) * gc : (m * G + g + 1) * gc] = group[:, m * gc : (m + 1) * gc]
    retr_ref[...] = total_of(parts, *cuts[1 + G])
    turn[...] = jnp.zeros_like(turn)
    turn[0:rows, :] = total_of(parts, *cuts[2 + G])
    small_ref[...] = turn[...].T[: small_ref.shape[0], :rows]


def last_sum(ins, widths, turned, G, gc):
    rows = ins[0].shape[0]
    cuts = cut_points(widths)
    shapes = [(rows, 3 * G * gc), (rows, widths[0]), (rows, widths[-2]), (turned, rows)]
    return once(
        functools.partial(last_body, len(ins), cuts, G, gc), "last_sum", ins, [None] * len(ins), [sds(s, f32) for s in shapes],
        scratch=[pltpu.VMEM((LANES, LANES), f32)], moved=12 * rows * cuts[-1][1],
    )


def last_feed_body(n, term, N, me_ref, *refs):
    parts, (down_ref, up_ref, table_ref, held) = refs[:n], refs[n:]
    drows, D = down_ref.shape
    rows = up_ref.shape[0]
    total = total_of(parts, 0, D, 2 * drows)
    down_ref[...] = total[:drows]
    for q in range(drows // rows):
        up_ref[:, q * D : (q + 1) * D] = total[drows + q * rows : drows + (q + 1) * rows]
    where, _ = spots(N, D, term)
    trows = table_ref.shape[0]
    count, half = N * n * term[0], term[0] // 2
    for i, p in enumerate(parts):
        for t, (row, col) in enumerate(where):
            at = (i * N + t) * term[0]
            tile = p[2 * drows + row : 2 * drows + row + term[0], col : col + term[1]]
            held[at : at + term[0], :] = tile.astype(f32)
    held[count:, :] = jnp.zeros((term[0], term[1]), f32)
    below = held[half : half + count, :]
    ids = (below[:, 0:1] * 256.0 + below[:, 1:2]).astype(jnp.int32) - (me_ref[0] * N + 2 * me_ref[1] + me_ref[2]) * trows
    line = lax.broadcasted_iota(jnp.int32, (count, trows), 0) % term[0]
    picker = (lax.broadcasted_iota(jnp.int32, (count, trows), 1) == ids) & (line < half)
    table_ref[...] = dot(picker.astype(bf16), held[0:count, :].astype(bf16), 0, 0)


def last_feed(me, ins, F, tok, trows, term, N):
    D = ins[0].shape[1]
    both = ins[0].shape[0] - spots(N, D, term)[1]
    return once(
        functools.partial(last_feed_body, len(ins), term, N), "last_feed", (me, after(ins[0], tok), *ins[1:]), [SMEM] + [None] * len(ins),
        [sds((both // 2, D), f32), sds((both // 2 * D // F, F), f32), sds((trows, term[1]), f32)], moved=12 * both * D,
        scratch=[pltpu.VMEM(((N * len(ins) + 1) * term[0], term[1]), f32)],
    )


def along_dp_sums(sums):
    return [sums[0]] + [lax.ppermute(sums[k], "dp", pairs(len(sums), k)) for k in range(1, len(sums))]


def lookup_body(F, trows, rows, index_ref, sg_ref, w_ref, r_ref, chosen_ref, back_ref, lead_ref, held, sem):
    seqs, _, width = held.shape
    copies = []
    for s in range(seqs):
        owner, within = index_ref[s] // trows, index_ref[s] % trows
        at = owner * rows + within % rows
        row = pl.multiple_of((at // 16) * 16, 16)
        col = pl.multiple_of(F + width * (within // rows), LANES)
        copies.append(
            (pltpu.make_async_copy(w_ref.at[pl.ds(row, 16), pl.ds(col, width)], held.at[s], sem.at[s]), at % 16)
        )
        copies[s][0].start()
    chosen_ref[...] = jnp.zeros_like(chosen_ref)
    line = lax.broadcasted_iota(jnp.int32, (16, width), 0)
    for s in range(seqs):
        copies[s][0].wait()
        block = jnp.where(line == copies[s][1], held[s].astype(f32), 0.0)
        chosen_ref[s : s + 1, :] = jnp.sum(block, axis=0, keepdims=True)
    back_ref[...] = jnp.zeros_like(back_ref)
    back_ref[0:seqs, :] = sg_ref[...] * chosen_ref[0:seqs, :]
    lead = dot(back_ref[...].astype(bf16), r_ref[...], 1, 1)
    for s in range(seqs):
        lead_ref[s] = lead[s : s + 1, :]


def lookup(index, sg, table, wr, F, trows, rows):
    seqs, width = sg.shape[0], wr.shape[1]
    return once(
        functools.partial(lookup_body, F, trows, rows), "lookup", (index, sg, table, wr), [SMEM, None, ANY, None],
        [sds((16, width), f32), sds((16, width), f32), sds((seqs, 1, wr.shape[0]), f32)],
        scratch=[pltpu.VMEM((seqs, 16, width), bf16), pltpu.SemaphoreType.DMA((seqs,))], moved=4 * wr.size,
    )


def score_body(top_ref, r_ref, chosen_ref, back_ref, sg_ref, id_ref, score_ref, retr_ref, term_ref, held):
    seqs = top_ref.shape[0]
    width = r_ref.shape[1]
    held[...] = jnp.zeros_like(held)
    for s in range(seqs):
        held[s : s + 1, :] = top_ref[s]
    leading = held[...].astype(bf16)
    projected = dot(leading, r_ref[...]).astype(bf16).astype(f32)[:seqs]
    score_ref[...] = jnp.sum(projected * chosen_ref[0:seqs, :], axis=-1, keepdims=True)
    retr_ref[...] = dot(leading, back_ref[...].astype(bf16), 0, 0)
    lane = lax.broadcasted_iota(jnp.int32, (seqs, width), 1)
    high, low = id_ref[...] // 256, id_ref[...] % 256
    ids = jnp.where(lane == 0, high, jnp.where(lane == 1, low, 0)).astype(f32)
    term_ref[...] = jnp.concatenate([sg_ref[...] * projected, ids], axis=0).astype(bf16)


def score(top, wr, chosen, back, sg, index):
    seqs, _, D = top.shape
    width = wr.shape[1]
    return once(
        score_body, "score", (top, wr, chosen, back, sg, index), [None] * 6,
        [sds((seqs, 1), f32), sds((D, width), f32), sds((2 * seqs, width), bf16)],
        scratch=[pltpu.VMEM((16, D), f32)], moved=8 * wr.size,
    )


def bias_row_body(Z, N, Q, s_ref, v_ref, out_ref):
    D = s_ref.shape[0]
    rows = D // (Z * N)
    lane = lax.broadcasted_iota(jnp.int32, (Z * N, rows, LANES), 2)
    whole = s_ref[...].astype(f32).reshape(Z * N, rows, LANES)
    parts = [jnp.where(lane == UB + q, whole, 0.0).reshape(Z * N, 1, rows, LANES) for q in range(Q)]
    turned = jnp.concatenate(parts, axis=1).reshape(Q * D, LANES).T
    out_ref[...] = jnp.sum(turned, axis=0, keepdims=True)


def bias_row(small, vec, Z, N, Q):
    D = small.shape[0]
    rows = D // (Z * N)
    if rows % 8:
        return vec[UB : UB + Q].reshape(Q, Z * N, rows).transpose(1, 0, 2).reshape(1, Q * D)
    return once(
        functools.partial(bias_row_body, Z, N, Q), "bias_row", (small, vec), [None] * 2, [sds((1, Q * D), f32)],
        moved=8 * Q * D * LANES,
    )[0]


def local(
    Z, N, tokens, input_weight, query_bias, value_bias, output_weight, output_bias, first_gain, first_shift,
    up_weight, up_bias, down_weight, down_bias, second_gain, second_shift, retriever_weight, document_table,
    document_index, output_grad, score_grad,
):
    both = ("dp", "fsdp")
    T, D = tokens.shape
    R = N // 2
    F = up_weight.shape[1]
    Rw = retriever_weight.shape[1]
    seqs = document_index.shape[0]
    L = T // seqs
    gc = 4 * HEAD_DIM
    G = D // gc
    Q = F // D
    trows, rows = document_table.shape[0], input_weight.shape[0]
    f = lax.axis_index("fsdp")
    me = jnp.stack([lax.axis_index("dp"), f // 2, f % 2]).astype(jnp.int32)

    vectors = [
        v.reshape(1, -1)
        for v in (query_bias, value_bias, output_bias, first_gain, first_shift, down_bias, second_gain, second_shift, up_bias)
    ]
    head, rest, wu = pack(input_weight, output_weight, retriever_weight, up_weight, document_table, vectors, gc)
    wu = lax.all_gather(wu, both, axis=0, tiled=True)
    head = repeat(along_dp(head, Z), R)
    rest = along_dp(after(rest, head), Z)
    head = between_chips(head, N)
    win = [None] * G
    win[0], small, vec = place(me, [head, other_core(head, N)], Z, [3 * gc, LANES], turned=16)
    rest = repeat([after(p, vec) for p in rest], R)
    wd = along_dp(after(down_weight, rest), Z)
    rest = between_chips(rest, N)

    qkv, soft, ctx = [None] * G, [None] * G, [None] * G

    def attend_group(g, tok):
        qkv[g], soft[g], ctx[g] = attend(after(tokens, tok), win[g], vec, g, seqs)

    ub = bias_row(small, vec, Z, N, Q)
    attend_group(0, ub)
    wd = repeat([after(w, ctx[0]) for w in wd], R)
    rest = after(rest, wd)
    *win[1:], wo, wr = place(me, [rest, other_core(rest, N)], Z, [3 * gc] * (G - 1) + [D, Rw])
    wd = between_chips(wd, N)
    for g in range(1, G):
        attend_group(g, ctx[g - 1])
    wd = after(wd, ctx[G - 1])
    n, inv, first, act, slope = up(ctx, tokens, wo, vec, wu, ub, L)
    (wd,) = place(me, [after(wd, first), other_core(wd, N)], Z, [D])
    chosen, back_projected, lead = lookup(document_index, score_grad.reshape(seqs, 1), after(wu, first), wr, F, trows, rows)
    final, top, two, feed, inner, gsg, gss, gdb, gub = down(first, act, slope, wd, vec, output_grad, lead, seqs)
    scores, retriever_back, term = score(top, wr, chosen, back_projected, score_grad.reshape(seqs, 1), document_index.reshape(seqs, 1))
    down_parts = down_grad(me, Z, N, act, feed)
    up_parts = grads(me, Z, N, "up_grad", [([after(first, *down_parts)], inner)], tile=D)
    feed_sums = pair_sum([down_parts, up_parts], N, up_parts[0], me, term)
    one, att, bctx, gfg, gfs, gob = mid(after(two, feed_sums), inner, wu, n, inv, vec, wo, L)
    mixed, gq, gv = [None] * G, [None] * G, [None] * G
    for g in range(G):
        mixed[g], gq[g], gv[g] = attend_back(
            qkv[g], soft[g], ctx[g], after(bctx, mixed[g - 1]) if g else bctx, g, seqs
        )
    parts = grads(
        me, Z, N, "mix_grad", [(ctx, att)] + [([tokens], m) for m in mixed],
        retr=retriever_back, vectors=gq + gv + [gob, gfg, gfs, gdb, gsg, gss, gub],
    )
    feed_sums = chips_sum(me, between_chips(feed_sums, N), parts[0], term.shape)
    mix_sums = pair_sum([parts], N, feed_sums[0])
    back_tokens = tokens_back(after(one, mix_sums), mixed, win, L)
    down_back, up_back, table_back = last_feed(me, along_dp_sums(feed_sums), F, back_tokens, trows, term.shape, N)
    mix_sums = chips_sum(me, between_chips(mix_sums, N), down_back)
    input_back, output_back, retriever_back, small = last_sum(
        along_dp_sums(mix_sums), [D] + [3 * gc] * G + [Rw, LANES], 16, G, gc
    )
    ub_back = small[8 : 8 + Q].reshape(-1)
    return (
        final, scores.reshape(seqs), back_tokens, input_back, small[0], small[1], output_back, small[2], small[3], small[4],
        up_back, ub_back, down_back, small[5], small[6], small[7], retriever_back, table_back,
    )


def solution(mesh):
    both = ("dp", "fsdp")
    mat, vec = P(both, None), P(both)
    in_specs = (mat, mat, vec, vec, mat, vec, vec, vec, mat, vec, mat, vec, vec, vec, mat, mat, vec, mat, vec)
    out_specs = (mat, vec, mat, mat, vec, vec, mat, vec, vec, vec, mat, vec, mat, vec, vec, vec, mat, mat)
    body = functools.partial(local, mesh.shape["dp"], mesh.shape["fsdp"])
    return jax.shard_map(body, mesh=mesh, in_specs=in_specs, out_specs=out_specs, check_vma=False)
```

```python
import functools
import math
import jax
import jax.numpy as jnp
from jax import lax
from jax.experimental import pallas as pl
from jax.experimental.pallas import tpu as pltpu
from jax.sharding import PartitionSpec as P

HEAD_DIM = 64
EPS = 1e-12
QB, VB, OB, FG, FS, DB, SG, SS, UB = range(9)
bf16, f32 = jnp.bfloat16, jnp.float32


def dot(a, b, ca=1, cb=0):
    return lax.dot_general(a, b, (((ca,), (cb,)), ((), ())), preferred_element_type=f32)


def rows_spec(rows, cols):
    return pl.BlockSpec((rows, cols), lambda i: (i, 0))


def full_spec(shape):
    return pl.BlockSpec(shape, lambda *_: (0,) * len(shape))


def head_mask(rows, cols, h):
    lane = lax.broadcasted_iota(jnp.int32, (rows, cols), 1)
    return (lane >= h * HEAD_DIM) & (lane < (h + 1) * HEAD_DIM)


def run(body, name, grid, ins, in_specs, outs, out_specs, scratch=(), flops=0, moved=0, vmem=60, alias=None):
    return pl.pallas_call(
        body,
        name=name,
        grid=grid,
        in_specs=in_specs,
        out_specs=out_specs,
        out_shape=outs,
        scratch_shapes=list(scratch),
        cost_estimate=estimate(flops, moved),
        input_output_aliases=alias or {},
        compiler_params=pltpu.CompilerParams(vmem_limit_bytes=vmem * 2**20),
    )(*ins)


def estimate(flops, moved):
    return pl.CostEstimate(flops=int(flops), bytes_accessed=int(moved), transcendentals=0)


def sds(shape, dtype):
    return jax.ShapeDtypeStruct(shape, dtype)


def attend_body(x_ref, w_ref, v_ref, *refs):
    qkv_ref, soft_ref, ctx_ref = refs[-3:]
    length = x_ref.shape[0]
    gc = ctx_ref.shape[1]
    mixed = dot(x_ref[...], w_ref[...])
    q = (mixed[:, :gc] + v_ref[QB : QB + 1, :]).astype(bf16)
    k = mixed[:, gc : 2 * gc].astype(bf16)
    v = (mixed[:, 2 * gc :] + v_ref[VB : VB + 1, :]).astype(bf16)
    qkv_ref[:, :gc] = q
    qkv_ref[:, gc : 2 * gc] = k
    qkv_ref[:, 2 * gc :] = v
    qs = q * bf16(HEAD_DIM ** -0.5)
    zero = jnp.zeros((), bf16)
    total = jnp.zeros((length, gc), f32)
    for h in range(gc // HEAD_DIM):
        mask = head_mask(length, gc, h)
        s = dot(jnp.where(mask, qs, zero), k, 1, 1)
        peak = jnp.max(s, axis=-1, keepdims=True)
        e = jnp.exp(s - peak)
        norm = 1.0 / jnp.sum(e, axis=-1, keepdims=True)
        p = (e * norm).astype(bf16)
        soft_ref[h] = p
        total += dot(p, jnp.where(mask, v, zero))
    ctx_ref[...] = total.astype(bf16)


def attend(x, w, vec, seqs, groups, at, into=()):
    T, D = x.shape
    gc = D // groups
    hg = gc // HEAD_DIM
    L = T // seqs
    count = w.shape[1] // (3 * gc)
    ins = (x, w, vec, *into)
    return run(
        attend_body, "attend", (count, seqs), ins,
        [
            pl.BlockSpec((L, D), lambda g, s: (s, 0)), pl.BlockSpec((D, 3 * gc), lambda g, s: (0, g)),
            pl.BlockSpec((vec.shape[0], gc), lambda g, s: (0, at + g)),
        ] + [pl.BlockSpec(memory_space=pl.ANY)] * len(into),
        [sds((groups, T, 3 * gc), bf16), sds((groups, hg, T, L), bf16), sds((groups, T, gc), bf16)],
        [
            pl.BlockSpec((None, L, 3 * gc), lambda g, s: (at + g, s, 0)),
            pl.BlockSpec((None, hg, L, L), lambda g, s: (at + g, 0, s, 0)),
            pl.BlockSpec((None, L, gc), lambda g, s: (at + g, s, 0)),
        ],
        flops=count * (2 * T * D * 3 * gc + 16 * T * L * gc), moved=2 * (T * D + w.size + count * (4 * T * gc + hg * T * L)),
        alias={3 + i: i for i in range(len(into))},
    )


def norm_rows(h):
    mean = jnp.mean(h, axis=-1, keepdims=True)
    c = h - mean
    var = jnp.mean(c * c, axis=-1, keepdims=True)
    inv = lax.rsqrt(var + EPS)
    return c * inv, inv


def norm_rows_back(cot, n, inv, gain):
    scaled = cot * gain
    return inv * (scaled - jnp.mean(scaled, axis=-1, keepdims=True) - n * jnp.mean(scaled * n, axis=-1, keepdims=True))


def up_body(step, ctx_ref, x_ref, wo_ref, v_ref, wu_ref, ub_ref, n_ref, inv_ref, first_ref, act_ref, slope_ref):
    G, _, gc = ctx_ref.shape
    hidden = x_ref[...].astype(f32) + v_ref[OB : OB + 1, :]
    for g in range(G):
        hidden += dot(ctx_ref[g], wo_ref[g * gc : (g + 1) * gc, :])
    n, inv = norm_rows(hidden)
    n_ref[...] = n
    inv_ref[...] = inv
    first = (n * v_ref[FG : FG + 1, :] + v_ref[FS : FS + 1, :]).astype(bf16)
    first_ref[...] = first
    ff = wu_ref.shape[1]
    for at in range(0, ff, step):
        cols = slice(at, at + step)
        u = dot(first, wu_ref[:, cols]) + ub_ref[:, cols]
        phi = 0.5 + 0.5 * lax.erf(u * math.sqrt(0.5))
        act_ref[:, cols] = (u * phi).astype(bf16)
        slope_ref[:, cols] = (phi + u * jnp.exp(u * u * -0.5) * (1.0 / math.sqrt(2 * math.pi))).astype(bf16)


def out_spec(D, F):
    return pl.BlockSpec((D, D), lambda i: (0, F // D))


def up(ctx, x, vec, wide, ub, rows, step=512):
    T, D = x.shape
    F = ub.shape[1]
    return run(
        functools.partial(up_body, step), "up", (T // rows,), (ctx, x, wide, vec, wide, ub),
        [pl.BlockSpec((ctx.shape[0], rows, ctx.shape[2]), lambda i: (0, i, 0)), rows_spec(rows, D)] + [out_spec(D, F), full_spec(vec.shape), full_spec((D, F)), full_spec(ub.shape)],
        [sds((T, D), f32), sds((T, 1), f32), sds((T, D), bf16), sds((T, F), bf16), sds((T, F), bf16)],
        [rows_spec(rows, D), rows_spec(rows, 1), rows_spec(rows, D), rows_spec(rows, F), rows_spec(rows, F)],
        flops=2 * T * D * (D + F), moved=T * D * 10 + 4 * T * F + 2 * D * (D + F),
    )


def add_rows(ref, value, cols=slice(None), axis=0):
    held = jnp.where(pl.program_id(axis) == 0, 0.0, ref[:, cols])
    ref[:, cols] = held + jnp.sum(value, axis=0, keepdims=True)


def down_body(step, first_ref, act_ref, slope_ref, w_ref, v_ref, og_ref, lead_ref,
              out_ref, top_ref, two_ref, feed_ref, inner_ref, gg_ref, gs_ref, gb_ref, gub_ref):
    rows = first_ref.shape[0]
    gain = v_ref[SG : SG + 1, :]
    hidden = first_ref[...].astype(f32) + v_ref[DB : DB + 1, :] + dot(act_ref[...], w_ref[...])
    n, inv = norm_rows(hidden)
    out = (n * gain + v_ref[SS : SS + 1, :]).astype(bf16)
    out_ref[...] = out
    top_ref[0] = out[0:16, :].astype(f32)[0:1, :]
    row = lax.broadcasted_iota(jnp.int32, (rows, 1), 0)
    cot = og_ref[...].astype(f32) + jnp.where(row == 0, lead_ref[0], 0.0)
    add_rows(gg_ref, cot * n)
    add_rows(gs_ref, cot)
    two = norm_rows_back(cot, n, inv, gain)
    two_ref[...] = two
    feed = two.astype(bf16)
    feed_ref[...] = feed
    add_rows(gb_ref, feed.astype(f32))
    ff = w_ref.shape[0]
    for at in range(0, ff, step):
        cols = slice(at, at + step)
        inner = (dot(feed, w_ref[cols, :], 1, 1) * slope_ref[:, cols].astype(f32)).astype(bf16)
        inner_ref[:, cols] = inner
        add_rows(gub_ref, inner.astype(f32), cols)


def down(first, act, slope, w, vec, og, lead, seqs, step=512):
    T, D = first.shape
    F = act.shape[1]
    L = T // seqs
    return run(
        functools.partial(down_body, step), "down", (seqs,), (first, act, slope, w, vec, og, lead),
        [rows_spec(L, D), rows_spec(L, F), rows_spec(L, F)] + [full_spec((F, D)), full_spec(vec.shape)]
        + [rows_spec(L, D), pl.BlockSpec((1, 1, D), lambda i: (i, 0, 0))],
        [sds((T, D), bf16), sds((seqs, 1, D), f32), sds((T, D), f32), sds((T, D), bf16), sds((T, F), bf16),
         sds((1, D), f32), sds((1, D), f32), sds((1, D), f32), sds((1, F), f32)],
        [rows_spec(L, D), pl.BlockSpec((1, 1, D), lambda i: (i, 0, 0)), rows_spec(L, D), rows_spec(L, D), rows_spec(L, F)] + [full_spec((1, D))] * 3 + [full_spec((1, F))],
        flops=4 * T * D * F, moved=6 * T * F + 12 * T * D + 2 * w.size,
    )


def mid_body(two_ref, inner_ref, wu_ref, n_ref, inv_ref, v_ref, wo_ref,
             one_ref, att_ref, bctx_ref, gg_ref, gs_ref, gob_ref):
    cot = two_ref[...] + dot(inner_ref[...], wu_ref[...], 1, 1)
    n = n_ref[...]
    add_rows(gg_ref, cot * n)
    add_rows(gs_ref, cot)
    one = norm_rows_back(cot, n, inv_ref[...], v_ref[FG : FG + 1, :])
    one_ref[...] = one
    att = one.astype(bf16)
    att_ref[...] = att
    add_rows(gob_ref, att.astype(f32))
    bctx_ref[...] = dot(att, wo_ref[...], 1, 1).astype(bf16)


def mid(two, inner, wide, n, inv, vec, rows):
    T, D = two.shape
    F = inner.shape[1]
    return run(
        mid_body, "mid", (T // rows,), (two, inner, wide, n, inv, vec, wide),
        [rows_spec(rows, D), rows_spec(rows, F), full_spec((D, F)), rows_spec(rows, D), rows_spec(rows, 1), full_spec(vec.shape), out_spec(D, F)],
        [sds((T, D), f32), sds((T, D), bf16), sds((T, D), bf16)] + [sds((1, D), f32)] * 3,
        [rows_spec(rows, D)] * 3 + [full_spec((1, D))] * 3,
        flops=2 * T * D * (F + D), moved=2 * T * F + 16 * T * D + 2 * D * (D + F),
    )


def attend_back_body(qkv_ref, soft_ref, ctx_ref, bctx_ref, out_ref, gq_ref, gv_ref):
    length, gc = ctx_ref.shape
    q = qkv_ref[:, :gc]
    k = qkv_ref[:, gc : 2 * gc]
    v = qkv_ref[:, 2 * gc :]
    do = bctx_ref[...]
    prod = do.astype(f32) * ctx_ref[...].astype(f32)
    zero = jnp.zeros((), bf16)
    dq = jnp.zeros((length, gc), f32)
    dk = jnp.zeros((length, gc), f32)
    dv = jnp.zeros((length, gc), f32)
    for h in range(gc // HEAD_DIM):
        mask = head_mask(length, gc, h)
        p = soft_ref[h]
        do_h = jnp.where(mask, do, zero)
        dp = dot(do_h, v, 1, 1)
        delta = jnp.sum(jnp.where(mask, prod, 0.0), axis=-1, keepdims=True)
        ds = (p.astype(f32) * (dp - delta)).astype(bf16)
        dv += dot(p, do_h, 0, 0)
        dq += dot(ds, jnp.where(mask, k, zero))
        dk += dot(ds, jnp.where(mask, q, zero), 0, 0)
    scale = HEAD_DIM ** -0.5
    dq = (dq * scale).astype(bf16)
    dv = dv.astype(bf16)
    out_ref[:, :gc] = dq
    out_ref[:, gc : 2 * gc] = (dk * scale).astype(bf16)
    out_ref[:, 2 * gc :] = dv
    add_rows(gq_ref, dq.astype(f32), axis=1)
    add_rows(gv_ref, dv.astype(f32), axis=1)


def attend_back(qkv, soft, ctx, bctx, seqs):
    G, T, gc = ctx.shape
    hg = gc // HEAD_DIM
    L = T // seqs
    line = lambda w: pl.BlockSpec((None, L, w), lambda g, s: (g, s, 0))
    row = pl.BlockSpec((1, gc), lambda g, s: (0, g))
    return run(
        attend_back_body, "attend_back", (G, seqs), (qkv, soft, ctx, bctx),
        [
            line(3 * gc), pl.BlockSpec((None, hg, L, L), lambda g, s: (g, 0, s, 0)), line(gc),
            pl.BlockSpec((L, gc), lambda g, s: (s, g)),
        ],
        [sds((G, T, 3 * gc), bf16), sds((1, G * gc), f32), sds((1, G * gc), f32)], [line(3 * gc), row, row],
        flops=G * 32 * T * L * gc, moved=2 * G * (8 * T * gc + hg * T * L),
    )


def tokens_back_body(one_ref, mixed_ref, *refs):
    total = one_ref[...]
    width = mixed_ref.shape[2]
    g = 0
    for w_ref in refs[:-1]:
        for at in range(0, w_ref.shape[1], width):
            total += dot(mixed_ref[g], w_ref[:, at : at + width], 1, 1)
            g += 1
    refs[-1][...] = total.astype(bf16)


def tokens_back(one, mixed, ws, rows):
    T, D = one.shape
    G, _, width = mixed.shape
    return run(
        tokens_back_body, "tokens_back", (T // rows,), (one, mixed, *ws),
        [rows_spec(rows, D), pl.BlockSpec((G, rows, width), lambda i: (0, i, 0))] + [full_spec(w.shape) for w in ws],
        sds((T, D), bf16), rows_spec(rows, D), flops=2 * T * D * G * width, moved=T * D * 12,
    )


def after(x, *deps):
    return lax.optimization_barrier((x,) + deps)[0]


ANY = pl.BlockSpec(memory_space=pl.ANY)
SMEM = pl.BlockSpec(memory_space=pltpu.SMEM)
LANES = 128


def once(body, name, ins, in_specs, outs, scratch=(), moved=0, flops=0, vmem=60):
    specs = [full_spec(a.shape) if spec is None else spec for a, spec in zip(ins, in_specs)]
    return run(body, name, (1,), ins, specs, outs, [full_spec(o.shape) for o in outs], scratch, flops, moved, vmem)


def cut_points(widths):
    cuts, at = [], 0
    for w in widths:
        cuts.append((at, at + w))
        at += w
    return cuts


def pack_body(D, gc, nvec, *refs):
    w_ref, o_ref, r_ref, u_ref, t_ref = refs[:5]
    head_ref, rest_ref, up_ref, held = refs[5 + nvec :]
    G = D // gc
    rows = w_ref.shape[0]
    held[...] = jnp.zeros_like(held)
    row = 0
    for v_ref in refs[5 : 5 + nvec]:
        v = v_ref[...].astype(f32)
        for at in range(0, v.shape[1], rows):
            held[row : row + 1, 0:rows] = v[:, at : at + rows]
            row += 1
    turned = held[...].T
    for m in range(3):
        head_ref[:, m * gc : (m + 1) * gc] = w_ref[:, m * D : m * D + gc]
    head_ref[:, 3 * gc :] = turned[:rows, :].astype(bf16)
    at = 0
    for g in range(1, G):
        for m in range(3):
            rest_ref[:, at : at + gc] = w_ref[:, m * D + g * gc : m * D + (g + 1) * gc]
            at += gc
    trows, width = t_ref.shape
    F = u_ref.shape[1]
    at = F + D + r_ref.shape[1]
    up_ref[:, :F] = u_ref[...]
    up_ref[:, F : F + D] = o_ref[...]
    up_ref[:, F + D : at] = r_ref[...]
    for lo in range(0, trows, rows):
        n = min(rows, trows - lo)
        up_ref[:n, at : at + width] = t_ref[lo : lo + n, :]
        if n < rows:
            up_ref[n:, at : at + width] = jnp.zeros((rows - n, width), bf16)
        at += width


def pack(w, o, r, u, t, vectors, gc):
    rows, D = o.shape
    head = 3 * gc + LANES
    rest = 3 * D - 3 * gc
    ups = u.shape[1] + D + r.shape[1] + -(-t.shape[0] // rows) * t.shape[1]
    return once(
        functools.partial(pack_body, D, gc, len(vectors)), "pack", (w, o, r, u, t, *vectors), [None] * (5 + len(vectors)),
        [sds((rows, head), bf16), sds((rows, rest), bf16), sds((rows, ups), bf16)],
        scratch=[pltpu.VMEM((LANES, LANES), f32)], moved=4 * rows * (head + rest + ups),
    )


def pairs(n, flip):
    return [(i, i ^ flip) for i in range(n)]


def along_dp(block, Z):
    return [block] + [lax.ppermute(block, "dp", pairs(Z, k)) for k in range(1, Z)]


def between_chips(blocks, N):
    return lax.all_to_all(blocks, "fsdp", 0, 0, axis_index_groups=[list(range(c, N, 2)) for c in range(2)], tiled=True)


def other_core(blocks, N):
    return lax.ppermute(blocks, "fsdp", pairs(N, 1))


def repeat_body(*refs):
    out = refs[-1]
    for r in range(out.shape[0]):
        for k, ref in enumerate(refs[:-1]):
            out[r, k] = ref[...]


def repeat(blocks, R):
    n = len(blocks)
    return once(
        repeat_body, "repeat", blocks, [None] * n, [sds((R, n) + blocks[0].shape, bf16)], moved=2 * (R + 1) * n * blocks[0].size
    )[0]


def place_body(n, cuts, turned, me_ref, *refs):
    pieces = refs[:n]
    outs = refs[n : n + len(cuts)]
    vec_ref = refs[n + len(cuts)] if turned else None
    held = refs[n + len(cuts) + turned : n + 2 * len(cuts) + turned]
    flat = refs[-3] if turned else None
    in_sem, out_sem = refs[-2:]
    Z = held[0].shape[0]
    copies = []
    for k in range(Z):
        for other in range(2):
            piece = pieces[other].at[:, k] if n == 2 else pieces[other * Z + k]
            for c, (lo, hi) in enumerate(cuts):
                copy = pltpu.make_async_copy(
                    piece.at[:, :, lo:hi], held[c].at[me_ref[0] ^ k, :, me_ref[2] ^ other], in_sem.at[len(copies)]
                )
                copies.append((copy, k))
    for copy, _ in copies:
        copy.start()
    last = []
    for k in range(Z):
        for copy, slot in copies:
            if slot == k:
                copy.wait()
        for c in range(len(cuts)):
            z = me_ref[0] ^ k
            last.append(pltpu.make_async_copy(held[c].at[z], outs[c].at[z], out_sem.at[k * len(cuts) + c]))
            last[-1].start()
    if turned:
        for z in range(Z):
            for r in range(held[-1].shape[1]):
                for c in range(2):
                    flat[z, r, c] = held[-1][z, r, c].astype(f32)
        vec_ref[...] = flat[...].reshape(vec_ref.shape[1], LANES).T[: vec_ref.shape[0]]
    for copy in last:
        copy.wait()


def place(me, pieces, Z, widths, turned=0):
    n = len(pieces)
    R, rows = pieces[0].shape[0], pieces[0].shape[-2]
    cuts = cut_points(widths)
    if turned and rows % 8:
        outs = place(me, pieces, Z, widths)
        return outs + [outs[-1][:, :turned].T.astype(f32)]
    shapes = [(Z, R, 2, rows, w) for w in widths]
    total = 2 * Z * R * rows
    outs = run(
        functools.partial(place_body, n, cuts, 1 if turned else 0), "place", (1,), (me, *pieces), [SMEM] + [ANY] * n,
        [sds(s, bf16) for s in shapes] + ([sds((turned, total), f32)] if turned else []),
        [ANY] * len(cuts) + ([full_spec((turned, total))] if turned else []),
        scratch=[pltpu.VMEM(s, bf16) for s in shapes] + ([pltpu.VMEM(shapes[-1], f32)] if turned else [])
        + [pltpu.SemaphoreType.DMA((2 * Z * len(cuts),)), pltpu.SemaphoreType.DMA((Z * len(cuts),))],
        moved=4 * total * cuts[-1][1], vmem=60,
    )
    return [o.reshape(total, o.shape[-1]) for o in outs[: len(cuts)]] + list(outs[len(cuts) :])


def hand_out(me_ref, part, Z, R, keep_ref, send_ref, cols=slice(None)):
    rows = part.shape[0] // (Z * R * 2)
    part = part.reshape(Z, R, 2, rows, part.shape[1])
    first = me_ref[2] == 0
    for z in range(Z):
        for r in range(R):
            one, two = part[z, r, 0], part[z, r, 1]
            keep_ref[r, z, :, cols] = jnp.where(first, one, two).astype(bf16)
            send_ref[r, z, :, cols] = jnp.where(first, two, one).astype(bf16)


def grads_body(plan, nvec, has_retr, Z, R, me_ref, *refs):
    at_out = len(refs) - 2 - (2 if nvec else 0)
    keep_ref, send_ref = refs[at_out : at_out + 2]
    col = 0

    def give(part):
        nonlocal col
        hand_out(me_ref, part, Z, R, keep_ref, send_ref, slice(col, col + part.shape[1]))
        col += part.shape[1]

    def read(spot):
        return refs[spot[0]][...] if spot[1] is None else refs[spot[0]][spot[1]]

    for lefts, right in plan:
        y = read(right)
        parts = [dot(read(left), y, 0, 0) for left in lefts]
        give(parts[0] if len(parts) == 1 else jnp.concatenate(parts, axis=0))
    at = at_out - nvec
    if has_retr:
        give(refs[at - 1][...])
    if nvec:
        turn = refs[-1]
        D = turn.shape[1]
        rows = D // (Z * R * 2)
        turn[...] = jnp.zeros_like(turn)
        row, lane = 0, 0
        for r in refs[at:at_out]:
            w = r.shape[1]
            if w <= D:
                turn[row : row + 1, lane : lane + w] = r[...]
                lane += w
                if lane == D:
                    row, lane = row + 1, 0
        total = turn[...].T
        r = refs[at_out - 1]
        if r.shape[1] > D:
            Q = r.shape[1] // D
            wide = refs[-2]
            wide[...] = jnp.zeros_like(wide)
            place_of = lax.broadcasted_iota(jnp.int32, r.shape, 1) % (Q * rows) // rows
            for q in range(Q):
                wide[row + q : row + q + 1, :] = jnp.where(place_of == q, r[...], 0.0)
            spread = wide[...].T.reshape(Z * R * 2, Q, rows, LANES)
            for q in range(Q):
                total += spread[:, q].reshape(total.shape)
        give(total)


def hand_out_plain(me, whole, Z, N, rows):
    whole = whole.astype(bf16).reshape(Z, N // 2, 2, rows, -1).swapaxes(0, 1)
    return [lax.dynamic_index_in_dim(whole, c, 2, keepdims=False) for c in (me[2], 1 - me[2])]


def grads(me, Z, N, name, arrays, plan, retr=None, vectors=(), tile=None):
    read = lambda spot: arrays[spot[0]] if spot[1] is None else arrays[spot[0]][spot[1]]
    shape = lambda spot: arrays[spot[0]].shape[-2:]
    D = sum(shape(left)[1] for left in plan[0][0])
    T = shape(plan[0][1])[0]
    rows, R = D // (Z * N), N // 2
    width = sum(shape(right)[1] for _, right in plan) + (0 if retr is None else retr.shape[1]) + (LANES if vectors else 0)
    if rows % 8:
        cols = [jnp.concatenate([dot(read(x), read(y), 0, 0) for x in xs], axis=0) for xs, y in plan]
        cols += [] if retr is None else [retr]
        if vectors:
            narrow = [jnp.concatenate([v for v in vectors if v.shape[1] <= D], axis=1).reshape(-1, D)]
            wide = [v.reshape(Z * N, -1, rows).swapaxes(0, 1).reshape(-1, D) for v in vectors if v.shape[1] > D]
            turned = jnp.concatenate(narrow + wide, axis=0).T
            cols += [turned, jnp.zeros((D, LANES - turned.shape[1]), f32)]
        return hand_out_plain(me, jnp.concatenate(cols, axis=1), Z, N, rows)
    ins = [*arrays] + ([] if retr is None else [retr]) + list(vectors)
    if tile is None:
        tile, specs, grid = width, [full_spec(a.shape) for a in ins], (1,)
    else:
        specs, grid = [full_spec(ins[0].shape), pl.BlockSpec((T, tile), lambda i: (0, i))], (width // tile,)
    return run(
        functools.partial(grads_body, plan, len(vectors), retr is not None, Z, R), name, grid, (me, *ins), [SMEM] + specs,
        [sds((R, Z, rows, width), bf16)] * 2, [pl.BlockSpec((R, Z, rows, tile), lambda i: (0, 0, 0, i))] * 2,
        scratch=[pltpu.VMEM((LANES, max(D, vectors[-1].shape[1])), f32), pltpu.VMEM((LANES, D), f32)] if vectors else [],
        flops=2 * T * D * width, moved=2 * T * (D + width) + 2 * D * width,
    )


def down_grad_body(me_ref, x_ref, y_ref, keep_ref, send_ref):
    hand_out(me_ref, dot(x_ref[...], y_ref[...], 0, 0), 1, keep_ref.shape[0], keep_ref, send_ref)


def down_grad(me, Z, N, act, feed):
    T, D = feed.shape
    F = act.shape[1]
    R, rows = N // 2, F // (Z * N)
    if rows % 8:
        return hand_out_plain(me, dot(act, feed, 0, 0), Z, N, rows)
    return run(
        down_grad_body, "down_grad", (Z,), (me, act, feed),
        [SMEM, pl.BlockSpec((T, N * rows), lambda i: (0, i)), full_spec(feed.shape)],
        [sds((R, Z, rows, D), bf16)] * 2, [pl.BlockSpec((R, 1, rows, D), lambda i: (0, i, 0, 0))] * 2,
        flops=2 * T * F * D, moved=2 * (T * F + T * D + F * D),
    )


def pair_body(n, me_ref, *refs):
    out_ref = refs[-1]
    width = out_ref.shape[3]
    at = 0
    for keep_ref, got_ref in zip(refs[:n], refs[n : 2 * n]):
        rows = keep_ref.shape[2]
        for lo in range(0, keep_ref.shape[3], width):
            cols = slice(lo, lo + width)
            out_ref[:, :, at : at + rows, :] = (
                keep_ref[:, :, :, cols].astype(f32) + got_ref[:, :, :, cols].astype(f32)
            ).astype(bf16)
            at += rows
    if len(refs) > 2 * n + 1:
        mine, other = refs[2 * n][...].astype(f32), refs[2 * n + 1][...].astype(f32)
        first = me_ref[2] == 0
        both = [jnp.where(first, mine, other), jnp.where(first, other, mine)]
        n_rows, w = mine.shape
        line = jnp.concatenate(both + [jnp.zeros((n_rows, width - 2 * w), f32)], axis=1).astype(bf16)
        for z in range(out_ref.shape[1]):
            out_ref[0, z, at : at + n_rows, :] = line


def pair_sum(parts, N, tok, me=None, term=None):
    n = len(parts)
    keeps = [keep for keep, _ in parts]
    got = [other_core(send, N) for _, send in parts]
    R, Z, _, width = keeps[0].shape
    rows = sum(k.size for k in keeps) // (R * Z * width)
    keeps[0] = after(keeps[0], tok)
    ins = keeps + got
    specs = [pl.BlockSpec((1,) + a.shape[1:], lambda i: (i, 0, 0, 0)) for a in ins]
    if term is not None:
        ins += [term, other_core(term, N)]
        specs += [full_spec(term.shape)] * 2
        rows += term.shape[0]
    return run(
        functools.partial(pair_body, n), "pair_sum", (R,), [jnp.zeros((3,), jnp.int32) if me is None else me] + ins, [SMEM] + specs,
        sds((R, Z, rows, width), bf16), pl.BlockSpec((1, Z, rows, width), lambda i: (i, 0, 0, 0)), moved=6 * R * Z * rows * width, vmem=60,
    )


def spots(n, width, shape):
    each = width // shape[1]
    return [(t // each * shape[0], t % each * shape[1]) for t in range(n)], -(-n // each) * shape[0]


def chips_body(term, me_ref, in_ref, *outs):
    R, _, rows, width = in_ref.shape
    rows -= term[0]
    where, _ = spots(2 * R, width, term)
    for k, out in enumerate(outs):
        z = me_ref[0] ^ k
        total = in_ref[0, z, :rows].astype(f32)
        for r in range(1, R):
            total += in_ref[r, z, :rows].astype(f32)
        out[:rows, :] = total.astype(out.dtype)
        if term[0]:
            out[rows:, :] = jnp.zeros((out.shape[0] - rows, width), out.dtype)
            for t, (row, col) in enumerate(where):
                tile = in_ref[t // 2, z, rows : rows + term[0], t % 2 * term[1] : (t % 2 + 1) * term[1]]
                out[rows + row : rows + row + term[0], col : col + term[1]] = tile.astype(out.dtype)


def chips_sum(me, got, tok, term=(0, LANES)):
    R, Z, rows, width = got.shape
    rows += spots(2 * R, width, term)[1] - term[0]
    return once(
        functools.partial(chips_body, term), "chips_sum", (me, after(got, tok)), [SMEM, None],
        [sds((rows, width), f32)] + [sds((rows, width), bf16)] * (Z - 1), moved=2 * got.size + 2 * Z * rows * width,
    )


def total_of(parts, lo, hi, rows=None):
    total = parts[0][:rows, lo:hi].astype(f32)
    for p in parts[1:]:
        total += p[:rows, lo:hi].astype(f32)
    return total


def last_body(n, cuts, G, gc, *refs):
    parts, (out_ref, in_ref, retr_ref, small_ref, turn) = refs[:n], refs[n:]
    rows = parts[0].shape[0]
    out_ref[...] = total_of(parts, *cuts[0])
    for g in range(G):
        for m in range(3):
            lo = cuts[1 + g][0] + m * gc
            in_ref[:, (m * G + g) * gc : (m * G + g + 1) * gc] = total_of(parts, lo, lo + gc)
    retr_ref[...] = total_of(parts, *cuts[1 + G])
    turn[...] = jnp.zeros_like(turn)
    turn[0:rows, :] = total_of(parts, *cuts[2 + G])
    small_ref[...] = turn[...].T[: small_ref.shape[0], :rows]


def last_sum(ins, widths, turned, G, gc, tok):
    rows = ins[0].shape[0]
    cuts = cut_points(widths)
    shapes = [(rows, widths[0]), (rows, 3 * G * gc), (rows, widths[-2]), (turned, rows)]
    return once(
        functools.partial(last_body, len(ins), cuts, G, gc), "last_sum", (after(ins[0], tok), *ins[1:]), [None] * len(ins),
        [sds(s, f32) for s in shapes], scratch=[pltpu.VMEM((LANES, LANES), f32)], moved=12 * rows * cuts[-1][1],
    )


def last_feed_body(n, term, N, me_ref, *refs):
    parts, (down_ref, up_ref, table_ref, held) = refs[:n], refs[n:]
    drows, D = down_ref.shape
    rows = up_ref.shape[0]
    total = total_of(parts, 0, D, 2 * drows)
    down_ref[...] = total[:drows]
    for q in range(drows // rows):
        up_ref[:, q * D : (q + 1) * D] = total[drows + q * rows : drows + (q + 1) * rows]
    where, _ = spots(N, D, term)
    trows = table_ref.shape[0]
    count, half = N * n * term[0], term[0] // 2
    for i, p in enumerate(parts):
        for t, (row, col) in enumerate(where):
            at = (i * N + t) * term[0]
            tile = p[2 * drows + row : 2 * drows + row + term[0], col : col + term[1]]
            held[at : at + term[0], :] = tile.astype(f32)
    held[count:, :] = jnp.zeros((term[0], term[1]), f32)
    below = held[half : half + count, :]
    ids = (below[:, 0:1] * 256.0 + below[:, 1:2]).astype(jnp.int32) - (me_ref[0] * N + 2 * me_ref[1] + me_ref[2]) * trows
    line = lax.broadcasted_iota(jnp.int32, (count, trows), 0) % term[0]
    picker = (lax.broadcasted_iota(jnp.int32, (count, trows), 1) == ids) & (line < half)
    table_ref[...] = dot(picker.astype(bf16), held[0:count, :].astype(bf16), 0, 0)


def last_feed(me, ins, F, tok, trows, term, N):
    D = ins[0].shape[1]
    both = ins[0].shape[0] - spots(N, D, term)[1]
    return once(
        functools.partial(last_feed_body, len(ins), term, N), "last_feed", (me, after(ins[0], tok), *ins[1:]), [SMEM] + [None] * len(ins),
        [sds((both // 2, D), f32), sds((both // 2 * D // F, F), f32), sds((trows, term[1]), f32)], moved=12 * both * D,
        scratch=[pltpu.VMEM(((N * len(ins) + 1) * term[0], term[1]), f32)],
    )


def along_dp_sums(sums):
    return [sums[0]] + [lax.ppermute(sums[k], "dp", pairs(len(sums), k)) for k in range(1, len(sums))]


def lookup_body(start, trows, rows, index_ref, sg_ref, w_ref, r_ref, chosen_ref, back_ref, lead_ref, held, sem):
    seqs, _, width = held.shape
    copies = []
    for s in range(seqs):
        owner, within = index_ref[s] // trows, index_ref[s] % trows
        at = owner * rows + within % rows
        row = pl.multiple_of((at // 16) * 16, 16)
        col = pl.multiple_of(start + width * (within // rows), LANES)
        copies.append(
            (pltpu.make_async_copy(w_ref.at[pl.ds(row, 16), pl.ds(col, width)], held.at[s], sem.at[s]), at % 16)
        )
        copies[s][0].start()
    chosen_ref[...] = jnp.zeros_like(chosen_ref)
    line = lax.broadcasted_iota(jnp.int32, (16, width), 0)
    for s in range(seqs):
        copies[s][0].wait()
        block = jnp.where(line == copies[s][1], held[s].astype(f32), 0.0)
        chosen_ref[s : s + 1, :] = jnp.sum(block, axis=0, keepdims=True)
    back_ref[...] = jnp.zeros_like(back_ref)
    back_ref[0:seqs, :] = sg_ref[...] * chosen_ref[0:seqs, :]
    lead = dot(back_ref[...].astype(bf16), r_ref[...], 1, 1)
    for s in range(seqs):
        lead_ref[s] = lead[s : s + 1, :]


def lookup(index, sg, wide, F, D, width, trows, rows):
    seqs = sg.shape[0]
    return once(
        functools.partial(lookup_body, F + D + width, trows, rows), "lookup", (index, sg, wide, wide),
        [SMEM, None, ANY, pl.BlockSpec((D, width), lambda i: (0, (F + D) // width))],
        [sds((16, width), f32), sds((16, width), f32), sds((seqs, 1, D), f32)],
        scratch=[pltpu.VMEM((seqs, 16, width), bf16), pltpu.SemaphoreType.DMA((seqs,))], moved=4 * D * width,
    )


def score_body(top_ref, r_ref, chosen_ref, back_ref, sg_ref, id_ref, score_ref, retr_ref, term_ref, held):
    seqs = top_ref.shape[0]
    width = r_ref.shape[1]
    held[...] = jnp.zeros_like(held)
    for s in range(seqs):
        held[s : s + 1, :] = top_ref[s]
    leading = held[...].astype(bf16)
    projected = dot(leading, r_ref[...]).astype(bf16).astype(f32)[:seqs]
    score_ref[...] = jnp.sum(projected * chosen_ref[0:seqs, :], axis=-1, keepdims=True)
    retr_ref[...] = dot(leading, back_ref[...].astype(bf16), 0, 0)
    lane = lax.broadcasted_iota(jnp.int32, (seqs, width), 1)
    high, low = id_ref[...] // 256, id_ref[...] % 256
    ids = jnp.where(lane == 0, high, jnp.where(lane == 1, low, 0)).astype(f32)
    term_ref[...] = jnp.concatenate([sg_ref[...] * projected, ids], axis=0).astype(bf16)


def score(top, wide, F, chosen, back, sg, index):
    seqs, _, D = top.shape
    width = chosen.shape[1]
    return once(
        score_body, "score", (top, wide, chosen, back, sg, index),
        [None, pl.BlockSpec((D, width), lambda i: (0, (F + D) // width))] + [None] * 4,
        [sds((seqs, 1), f32), sds((D, width), f32), sds((2 * seqs, width), bf16)],
        scratch=[pltpu.VMEM((16, D), f32)], moved=8 * D * width,
    )


def bias_row_body(Z, N, Q, s_ref, v_ref, out_ref):
    D = s_ref.shape[0]
    rows = D // (Z * N)
    lane = lax.broadcasted_iota(jnp.int32, (Z * N, rows, LANES), 2)
    whole = s_ref[...].astype(f32).reshape(Z * N, rows, LANES)
    parts = [jnp.where(lane == UB + q, whole, 0.0).reshape(Z * N, 1, rows, LANES) for q in range(Q)]
    turned = jnp.concatenate(parts, axis=1).reshape(Q * D, LANES).T
    out_ref[...] = jnp.sum(turned, axis=0, keepdims=True)


def bias_row(small, vec, Z, N, Q):
    D = small.shape[0]
    rows = D // (Z * N)
    if rows % 8:
        return vec[UB : UB + Q].reshape(Q, Z * N, rows).transpose(1, 0, 2).reshape(1, Q * D)
    return once(
        functools.partial(bias_row_body, Z, N, Q), "bias_row", (small, vec), [None] * 2, [sds((1, Q * D), f32)],
        moved=8 * Q * D * LANES,
    )[0]


def local(
    Z, N, tokens, input_weight, query_bias, value_bias, output_weight, output_bias, first_gain, first_shift,
    up_weight, up_bias, down_weight, down_bias, second_gain, second_shift, retriever_weight, document_table,
    document_index, output_grad, score_grad,
):
    both = ("dp", "fsdp")
    T, D = tokens.shape
    R = N // 2
    F = up_weight.shape[1]
    Rw = retriever_weight.shape[1]
    seqs = document_index.shape[0]
    L = T // seqs
    gc = 4 * HEAD_DIM
    G = D // gc
    Q = F // D
    trows, rows = document_table.shape[0], input_weight.shape[0]
    f = lax.axis_index("fsdp")
    me = jnp.stack([lax.axis_index("dp"), f // 2, f % 2]).astype(jnp.int32)

    vectors = [
        v.reshape(1, -1)
        for v in (query_bias, value_bias, output_bias, first_gain, first_shift, down_bias, second_gain, second_shift, up_bias)
    ]
    head, rest, wide = pack(input_weight, output_weight, retriever_weight, up_weight, document_table, vectors, gc)
    wide = lax.all_gather(wide, both, axis=0, tiled=True)
    head = repeat(along_dp(head, Z), R)
    rest = along_dp(after(rest, head), Z)
    head = between_chips(head, N)
    win_one, small, vec = place(me, [head, other_core(head, N)], Z, [3 * gc, LANES], turned=16)
    rest = repeat([after(p, vec) for p in rest], R)
    wd = along_dp(after(down_weight, rest), Z)
    rest = between_chips(rest, N)

    ub = bias_row(small, vec, Z, N, Q)
    held = attend(after(tokens, ub), win_one, vec, seqs, G, 0)
    wd = repeat([after(w, held[2]) for w in wd], R)
    rest = after(rest, wd)
    (win_two,) = place(me, [rest, other_core(rest, N)], Z, [3 * gc * (G - 1)])
    wd = between_chips(wd, N)
    qkv, soft, ctx = attend(tokens, win_two, vec, seqs, G, 1, held)
    wd = after(wd, ctx)
    n, inv, first, act, slope = up(ctx, tokens, vec, wide, ub, L)
    (wd,) = place(me, [after(wd, first), other_core(wd, N)], Z, [D])
    chosen, back_projected, lead = lookup(document_index, score_grad.reshape(seqs, 1), after(wide, first), F, D, Rw, trows, rows)
    final, top, two, feed, inner, gsg, gss, gdb, gub = down(first, act, slope, wd, vec, output_grad, lead, seqs)
    scores, retriever_back, term = score(top, wide, F, chosen, back_projected, score_grad.reshape(seqs, 1), document_index.reshape(seqs, 1))
    down_parts = down_grad(me, Z, N, act, feed)
    up_parts = grads(me, Z, N, "up_grad", [after(first, *down_parts), inner], [([(0, None)], (1, None))], tile=D)
    feed_sums = pair_sum([down_parts, up_parts], N, up_parts[0], me, term)
    one, att, bctx, gfg, gfs, gob = mid(after(two, feed_sums), inner, wide, n, inv, vec, L)
    mixed, gq, gv = attend_back(qkv, soft, ctx, after(bctx, feed_sums), seqs)
    parts = grads(
        me, Z, N, "mix_grad", [ctx, att, tokens, mixed],
        [([(0, g) for g in range(G)], (1, None))] + [([(2, None)], (3, g)) for g in range(G)],
        retr=retriever_back, vectors=[gq, gv, gob, gfg, gfs, gdb, gsg, gss, gub],
    )
    mix_pair = pair_sum([parts], N, parts[0])
    feed_sums = between_chips(feed_sums, N)
    mix_sums = between_chips(after(mix_pair, feed_sums), N)
    feed_sums = chips_sum(me, feed_sums, mix_pair, term.shape)
    back_tokens = tokens_back(after(one, feed_sums[0]), mixed, [win_one, win_two], L)
    mix_sums = chips_sum(me, mix_sums, back_tokens)
    down_back, up_back, table_back = last_feed(me, along_dp_sums(feed_sums), F, mix_sums[0], trows, term.shape, N)
    output_back, input_back, retriever_back, small = last_sum(
        along_dp_sums(mix_sums), [D] + [3 * gc] * G + [Rw, LANES], 16, G, gc, down_back
    )
    ub_back = small[8 : 8 + Q].reshape(-1)
    return (
        final, scores.reshape(seqs), back_tokens, input_back, small[0], small[1], output_back, small[2], small[3], small[4],
        up_back, ub_back, down_back, small[5], small[6], small[7], retriever_back, table_back,
    )


def solution(mesh):
    both = ("dp", "fsdp")
    mat, vec = P(both, None), P(both)
    in_specs = (mat, mat, vec, vec, mat, vec, vec, vec, mat, vec, mat, vec, vec, vec, mat, mat, vec, mat, vec)
    out_specs = (mat, vec, mat, mat, vec, vec, mat, vec, vec, vec, mat, vec, mat, vec, vec, vec, mat, mat)
    body = functools.partial(local, mesh.shape["dp"], mesh.shape["fsdp"])
    return jax.shard_map(body, mesh=mesh, in_specs=in_specs, out_specs=out_specs, check_vma=False)
```

```python
import functools
import math
import jax
import jax.numpy as jnp
from jax import lax
from jax.experimental import pallas as pl
from jax.experimental.pallas import tpu as pltpu
from jax.sharding import PartitionSpec as P

HEAD_DIM = 64
EPS = 1e-12
QB, VB, OB, FG, FS, DB, SG, SS, UB = range(9)
bf16, f32 = jnp.bfloat16, jnp.float32


def dot(a, b, ca=1, cb=0):
    return lax.dot_general(a, b, (((ca,), (cb,)), ((), ())), preferred_element_type=f32)


def rows_spec(rows, cols):
    return pl.BlockSpec((rows, cols), lambda i: (i, 0))


def full_spec(shape):
    return pl.BlockSpec(shape, lambda *_: (0,) * len(shape))


def head_mask(rows, cols, h):
    lane = lax.broadcasted_iota(jnp.int32, (rows, cols), 1)
    return (lane >= h * HEAD_DIM) & (lane < (h + 1) * HEAD_DIM)


def run(body, name, grid, ins, in_specs, outs, out_specs, scratch=(), flops=0, moved=0, vmem=60, alias=None):
    return pl.pallas_call(
        body,
        name=name,
        grid=grid,
        in_specs=in_specs,
        out_specs=out_specs,
        out_shape=outs,
        scratch_shapes=list(scratch),
        cost_estimate=estimate(flops, moved),
        input_output_aliases=alias or {},
        compiler_params=pltpu.CompilerParams(vmem_limit_bytes=vmem * 2**20),
    )(*ins)


def estimate(flops, moved):
    return pl.CostEstimate(flops=int(flops), bytes_accessed=int(moved), transcendentals=0)


def sds(shape, dtype):
    return jax.ShapeDtypeStruct(shape, dtype)


def attend_body(x_ref, w_ref, v_ref, *refs):
    qkv_ref, soft_ref, ctx_ref = refs[-3:]
    length = x_ref.shape[0]
    gc = ctx_ref.shape[1]
    mixed = dot(x_ref[...], w_ref[...])
    q = (mixed[:, :gc] + v_ref[QB : QB + 1, :]).astype(bf16)
    k = mixed[:, gc : 2 * gc].astype(bf16)
    v = (mixed[:, 2 * gc :] + v_ref[VB : VB + 1, :]).astype(bf16)
    qkv_ref[:, :gc] = q
    qkv_ref[:, gc : 2 * gc] = k
    qkv_ref[:, 2 * gc :] = v
    qs = q * bf16(HEAD_DIM ** -0.5)
    zero = jnp.zeros((), bf16)
    total = jnp.zeros((length, gc), f32)
    for h in range(gc // HEAD_DIM):
        mask = head_mask(length, gc, h)
        s = dot(jnp.where(mask, qs, zero), k, 1, 1)
        peak = jnp.max(s, axis=-1, keepdims=True)
        e = jnp.exp(s - peak)
        norm = 1.0 / jnp.sum(e, axis=-1, keepdims=True)
        p = (e * norm).astype(bf16)
        soft_ref[h] = p
        total += dot(p, jnp.where(mask, v, zero))
    ctx_ref[...] = total.astype(bf16)


def attend(x, w, vec, seqs, groups, at, into=()):
    T, D = x.shape
    gc = D // groups
    hg = gc // HEAD_DIM
    L = T // seqs
    count = w.shape[1] // (3 * gc)
    ins = (x, w, vec, *into)
    return run(
        attend_body, "attend", (count, seqs), ins,
        [
            pl.BlockSpec((L, D), lambda g, s: (s, 0)), pl.BlockSpec((D, 3 * gc), lambda g, s: (0, g)),
            pl.BlockSpec((vec.shape[0], gc), lambda g, s: (0, at + g)),
        ] + [pl.BlockSpec(memory_space=pl.ANY)] * len(into),
        [sds((groups, T, 3 * gc), bf16), sds((groups, hg, T, L), bf16), sds((groups, T, gc), bf16)],
        [
            pl.BlockSpec((None, L, 3 * gc), lambda g, s: (at + g, s, 0)),
            pl.BlockSpec((None, hg, L, L), lambda g, s: (at + g, 0, s, 0)),
            pl.BlockSpec((None, L, gc), lambda g, s: (at + g, s, 0)),
        ],
        flops=count * (2 * T * D * 3 * gc + 16 * T * L * gc), moved=2 * (T * D + w.size + count * (4 * T * gc + hg * T * L)),
        alias={3 + i: i for i in range(len(into))},
    )


def norm_rows(h):
    mean = jnp.mean(h, axis=-1, keepdims=True)
    c = h - mean
    var = jnp.mean(c * c, axis=-1, keepdims=True)
    inv = lax.rsqrt(var + EPS)
    return c * inv, inv


def norm_rows_back(cot, n, inv, gain):
    scaled = cot * gain
    return inv * (scaled - jnp.mean(scaled, axis=-1, keepdims=True) - n * jnp.mean(scaled * n, axis=-1, keepdims=True))


def in_turn(blocks, first, then):
    held = first(blocks[0])
    for i, block in enumerate(blocks):
        ahead = first(blocks[i + 1]) if i + 1 < len(blocks) else None
        then(i, block, held)
        held = ahead


def blocks_of(rows, size):
    return [slice(at, at + size) for at in range(0, rows, size)]


def up_body(size, step, ctx_ref, x_ref, wo_ref, v_ref, wu_ref, ub_ref, n_ref, inv_ref, first_ref, act_ref, slope_ref):
    G, rows, gc = ctx_ref.shape

    def attended(block):
        hidden = x_ref[block].astype(f32) + v_ref[OB : OB + 1, :]
        for g in range(G):
            hidden += dot(ctx_ref[g, block], wo_ref[g * gc : (g + 1) * gc, :])
        return hidden

    def rest(_, block, hidden):
        n, inv = norm_rows(hidden)
        n_ref[block] = n
        inv_ref[block] = inv
        first = (n * v_ref[FG : FG + 1, :] + v_ref[FS : FS + 1, :]).astype(bf16)
        first_ref[block] = first
        ff = wu_ref.shape[1]
        for at in range(0, ff, step):
            cols = slice(at, at + step)
            u = dot(first, wu_ref[:, cols]) + ub_ref[:, cols]
            phi = 0.5 + 0.5 * lax.erf(u * math.sqrt(0.5))
            act_ref[block, cols] = (u * phi).astype(bf16)
            slope_ref[block, cols] = (phi + u * jnp.exp(u * u * -0.5) * (1.0 / math.sqrt(2 * math.pi))).astype(bf16)

    in_turn(blocks_of(rows, size), attended, rest)


def out_spec(D, F):
    return pl.BlockSpec((D, D), lambda i: (0, F // D))


def up(ctx, x, vec, wide, ub, rows, size, step=512):
    T, D = x.shape
    F = ub.shape[1]
    return run(
        functools.partial(up_body, size, step), "up", (T // rows,), (ctx, x, wide, vec, wide, ub),
        [pl.BlockSpec((ctx.shape[0], rows, ctx.shape[2]), lambda i: (0, i, 0)), rows_spec(rows, D)] + [out_spec(D, F), full_spec(vec.shape), full_spec((D, F)), full_spec(ub.shape)],
        [sds((T, D), f32), sds((T, 1), f32), sds((T, D), bf16), sds((T, F), bf16), sds((T, F), bf16)],
        [rows_spec(rows, D), rows_spec(rows, 1), rows_spec(rows, D), rows_spec(rows, F), rows_spec(rows, F)],
        flops=2 * T * D * (D + F), moved=T * D * 10 + 4 * T * F + 2 * D * (D + F),
    )


def add_rows(ref, value, cols=slice(None), axis=0):
    held = jnp.where(pl.program_id(axis) == 0, 0.0, ref[:, cols])
    ref[:, cols] = held + jnp.sum(value, axis=0, keepdims=True)


def down_body(size, step, first_ref, act_ref, slope_ref, w_ref, v_ref, og_ref, lead_ref,
              out_ref, top_ref, two_ref, feed_ref, inner_ref, gg_ref, gs_ref, gb_ref, gub_ref):
    gain = v_ref[SG : SG + 1, :]
    ff = w_ref.shape[0]
    sums = {}

    def count(name, value):
        total = jnp.sum(value, axis=0, keepdims=True)
        sums[name] = sums[name] + total if name in sums else total

    def fed(block):
        return first_ref[block].astype(f32) + v_ref[DB : DB + 1, :] + dot(act_ref[block], w_ref[...])

    def rest(i, block, hidden):
        n, inv = norm_rows(hidden)
        out = (n * gain + v_ref[SS : SS + 1, :]).astype(bf16)
        out_ref[block] = out
        top_ref[i] = out[0:16, :].astype(f32)[0:1, :]
        row = lax.broadcasted_iota(jnp.int32, (size, 1), 0)
        cot = og_ref[block].astype(f32) + jnp.where(row == 0, lead_ref[i], 0.0)
        count("gain", cot * n)
        count("shift", cot)
        two = norm_rows_back(cot, n, inv, gain)
        two_ref[block] = two
        feed = two.astype(bf16)
        feed_ref[block] = feed
        count("bias", feed.astype(f32))
        for at in range(0, ff, step):
            cols = slice(at, at + step)
            inner = (dot(feed, w_ref[cols, :], 1, 1) * slope_ref[block, cols].astype(f32)).astype(bf16)
            inner_ref[block, cols] = inner
            count(at, inner.astype(f32))

    in_turn(blocks_of(first_ref.shape[0], size), fed, rest)
    add_rows(gg_ref, sums["gain"])
    add_rows(gs_ref, sums["shift"])
    add_rows(gb_ref, sums["bias"])
    for at in range(0, ff, step):
        add_rows(gub_ref, sums[at], slice(at, at + step))


def down(first, act, slope, w, vec, og, lead, seqs, per, step=512):
    T, D = first.shape
    F = act.shape[1]
    L = T // seqs
    rows = per * L
    each = pl.BlockSpec((per, 1, D), lambda i: (i, 0, 0))
    return run(
        functools.partial(down_body, L, step), "down", (seqs // per,), (first, act, slope, w, vec, og, lead),
        [rows_spec(rows, D), rows_spec(rows, F), rows_spec(rows, F), full_spec((F, D)), full_spec(vec.shape), rows_spec(rows, D), each],
        [sds((T, D), bf16), sds((seqs, 1, D), f32), sds((T, D), f32), sds((T, D), bf16), sds((T, F), bf16),
         sds((1, D), f32), sds((1, D), f32), sds((1, D), f32), sds((1, F), f32)],
        [rows_spec(rows, D), each, rows_spec(rows, D), rows_spec(rows, D), rows_spec(rows, F)]
        + [full_spec((1, D))] * 3 + [full_spec((1, F))],
        flops=4 * T * D * F, moved=6 * T * F + 12 * T * D + 2 * F * D,
    )


def mid_body(size, two_ref, inner_ref, wu_ref, n_ref, inv_ref, v_ref, wo_ref,
             one_ref, att_ref, bctx_ref, gg_ref, gs_ref, gob_ref):
    sums = {}

    def count(name, value):
        total = jnp.sum(value, axis=0, keepdims=True)
        sums[name] = sums[name] + total if name in sums else total

    def back(block):
        return two_ref[block] + dot(inner_ref[block], wu_ref[...], 1, 1)

    def rest(_, block, cot):
        n = n_ref[block]
        count("gain", cot * n)
        count("shift", cot)
        one = norm_rows_back(cot, n, inv_ref[block], v_ref[FG : FG + 1, :])
        one_ref[block] = one
        att = one.astype(bf16)
        att_ref[block] = att
        count("bias", att.astype(f32))
        bctx_ref[block] = dot(att, wo_ref[...], 1, 1).astype(bf16)

    in_turn(blocks_of(two_ref.shape[0], size), back, rest)
    add_rows(gg_ref, sums["gain"])
    add_rows(gs_ref, sums["shift"])
    add_rows(gob_ref, sums["bias"])


def mid(two, inner, wide, n, inv, vec, rows, size):
    T, D = two.shape
    F = inner.shape[1]
    return run(
        functools.partial(mid_body, size), "mid", (T // rows,), (two, inner, wide, n, inv, vec, wide),
        [rows_spec(rows, D), rows_spec(rows, F), full_spec((D, F)), rows_spec(rows, D), rows_spec(rows, 1), full_spec(vec.shape), out_spec(D, F)],
        [sds((T, D), f32), sds((T, D), bf16), sds((T, D), bf16)] + [sds((1, D), f32)] * 3,
        [rows_spec(rows, D)] * 3 + [full_spec((1, D))] * 3,
        flops=2 * T * D * (F + D), moved=2 * T * F + 16 * T * D + 2 * D * (D + F),
    )


def attend_back_body(qkv_ref, soft_ref, ctx_ref, bctx_ref, out_ref, gq_ref, gv_ref):
    length, gc = ctx_ref.shape
    q = qkv_ref[:, :gc]
    k = qkv_ref[:, gc : 2 * gc]
    v = qkv_ref[:, 2 * gc :]
    do = bctx_ref[...]
    prod = do.astype(f32) * ctx_ref[...].astype(f32)
    zero = jnp.zeros((), bf16)
    dq = jnp.zeros((length, gc), f32)
    dk = jnp.zeros((length, gc), f32)
    dv = jnp.zeros((length, gc), f32)
    for h in range(gc // HEAD_DIM):
        mask = head_mask(length, gc, h)
        p = soft_ref[h]
        do_h = jnp.where(mask, do, zero)
        dp = dot(do_h, v, 1, 1)
        delta = jnp.sum(jnp.where(mask, prod, 0.0), axis=-1, keepdims=True)
        ds = (p.astype(f32) * (dp - delta)).astype(bf16)
        dv += dot(p, do_h, 0, 0)
        dq += dot(ds, jnp.where(mask, k, zero))
        dk += dot(ds, jnp.where(mask, q, zero), 0, 0)
    scale = HEAD_DIM ** -0.5
    dq = (dq * scale).astype(bf16)
    dv = dv.astype(bf16)
    out_ref[:, :gc] = dq
    out_ref[:, gc : 2 * gc] = (dk * scale).astype(bf16)
    out_ref[:, 2 * gc :] = dv
    add_rows(gq_ref, dq.astype(f32), axis=1)
    add_rows(gv_ref, dv.astype(f32), axis=1)


def attend_back(qkv, soft, ctx, bctx, seqs):
    G, T, gc = ctx.shape
    hg = gc // HEAD_DIM
    L = T // seqs
    line = lambda w: pl.BlockSpec((None, L, w), lambda g, s: (g, s, 0))
    row = pl.BlockSpec((1, gc), lambda g, s: (0, g))
    return run(
        attend_back_body, "attend_back", (G, seqs), (qkv, soft, ctx, bctx),
        [
            line(3 * gc), pl.BlockSpec((None, hg, L, L), lambda g, s: (g, 0, s, 0)), line(gc),
            pl.BlockSpec((L, gc), lambda g, s: (s, g)),
        ],
        [sds((G, T, 3 * gc), bf16), sds((1, G * gc), f32), sds((1, G * gc), f32)], [line(3 * gc), row, row],
        flops=G * 32 * T * L * gc, moved=2 * G * (8 * T * gc + hg * T * L),
    )


def tokens_back_body(one_ref, mixed_ref, *refs):
    total = one_ref[...]
    width = mixed_ref.shape[2]
    g = 0
    for w_ref in refs[:-1]:
        for at in range(0, w_ref.shape[1], width):
            total += dot(mixed_ref[g], w_ref[:, at : at + width], 1, 1)
            g += 1
    refs[-1][...] = total.astype(bf16)


def tokens_back(one, mixed, ws, rows):
    T, D = one.shape
    G, _, width = mixed.shape
    return run(
        tokens_back_body, "tokens_back", (T // rows,), (one, mixed, *ws),
        [rows_spec(rows, D), pl.BlockSpec((G, rows, width), lambda i: (0, i, 0))] + [full_spec(w.shape) for w in ws],
        sds((T, D), bf16), rows_spec(rows, D), flops=2 * T * D * G * width, moved=T * D * 12,
    )


def after(x, *deps):
    return lax.optimization_barrier((x,) + deps)[0]


ANY = pl.BlockSpec(memory_space=pl.ANY)
SMEM = pl.BlockSpec(memory_space=pltpu.SMEM)
LANES = 128


def once(body, name, ins, in_specs, outs, scratch=(), moved=0, flops=0, vmem=60):
    specs = [full_spec(a.shape) if spec is None else spec for a, spec in zip(ins, in_specs)]
    return run(body, name, (1,), ins, specs, outs, [full_spec(o.shape) for o in outs], scratch, flops, moved, vmem)


def cut_points(widths):
    cuts, at = [], 0
    for w in widths:
        cuts.append((at, at + w))
        at += w
    return cuts


def pack_body(D, gc, nvec, *refs):
    id_ref, w_ref, o_ref, r_ref, u_ref = refs[:5]
    head_ref, rest_ref, up_ref, held = refs[5 + nvec :]
    G = D // gc
    rows = w_ref.shape[0]
    held[...] = jnp.zeros_like(held)
    row = 0
    for v_ref in refs[5 : 5 + nvec]:
        v = v_ref[...].astype(f32)
        for at in range(0, v.shape[1], rows):
            held[row : row + 1, 0:rows] = v[:, at : at + rows]
            row += 1
    lane = lax.broadcasted_iota(jnp.int32, (1, LANES), 1)
    ids = jnp.zeros((1, LANES), jnp.int32)
    seqs = id_ref.shape[0]
    for i in range(seqs):
        ids = jnp.where(lane == i, id_ref[i] // 256, jnp.where(lane == seqs + i, id_ref[i] % 256, ids))
    held[row : row + 1, :] = ids.astype(f32)
    turned = held[...].T
    for m in range(3):
        head_ref[:, m * gc : (m + 1) * gc] = w_ref[:, m * D : m * D + gc]
    head_ref[:, 3 * gc :] = turned[:rows, :].astype(bf16)
    at = 0
    for g in range(1, G):
        for m in range(3):
            rest_ref[:, at : at + gc] = w_ref[:, m * D + g * gc : m * D + (g + 1) * gc]
            at += gc
    F = u_ref.shape[1]
    up_ref[:, :F] = u_ref[...]
    up_ref[:, F : F + D] = o_ref[...]
    up_ref[:, F + D :] = r_ref[...]


def pack(ids, w, o, r, u, vectors, gc):
    rows, D = o.shape
    head = 3 * gc + LANES
    rest = 3 * D - 3 * gc
    ups = u.shape[1] + D + r.shape[1]
    return once(
        functools.partial(pack_body, D, gc, len(vectors)), "pack", (ids, w, o, r, u, *vectors), [SMEM] + [None] * (4 + len(vectors)),
        [sds((rows, head), bf16), sds((rows, rest), bf16), sds((rows, ups), bf16)],
        scratch=[pltpu.VMEM((LANES, LANES), f32)], moved=4 * rows * (head + rest + ups),
    )


def pairs(n, flip):
    return [(i, i ^ flip) for i in range(n)]


def along_dp(blocks):
    return [blocks[0]] + [lax.ppermute(b, "dp", pairs(len(blocks), k)) for k, b in enumerate(blocks) if k]


def between_chips(blocks, N):
    return lax.all_to_all(blocks, "fsdp", 0, 0, axis_index_groups=[list(range(c, N, 2)) for c in range(2)], tiled=True)


def other_core(blocks, N):
    return lax.ppermute(blocks, "fsdp", pairs(N, 1))


def repeat_body(n, *refs):
    out, blocks, tiles = refs[-1], refs[:n], refs[n:-1]
    rows, width = blocks[0].shape
    for r in range(out.shape[0]):
        for k, ref in enumerate(blocks):
            out[r, k, :rows] = ref[...]
        if tiles:
            w = tiles[0].shape[1] // out.shape[0]
            total = tiles[0][:, r * w : (r + 1) * w].astype(f32)
            for ref in tiles[1:]:
                total += ref[:, r * w : (r + 1) * w].astype(f32)
            blank = jnp.zeros((total.shape[0], width - w), f32)
            out[r, 0, rows:] = jnp.concatenate([total, blank], axis=1).astype(bf16)
            for k in range(1, n):
                out[r, k, rows:] = jnp.zeros((total.shape[0], width), bf16)


def repeat(blocks, R, tiles=()):
    n = len(blocks)
    rows, width = blocks[0].shape
    rows += tiles[0].shape[0] if tiles else 0
    return once(
        functools.partial(repeat_body, n), "repeat", [*blocks, *tiles], [None] * (n + len(tiles)),
        [sds((R, n, rows, width), bf16)], moved=2 * (R + 1) * n * rows * width,
    )[0]


def ask_body(seqs, Z, R, at, me_ref, s_ref, t_ref, *refs):
    outs, below, held = refs[:Z], refs[Z], refs[Z + 1]
    D, trows = s_ref.shape[0], t_ref.shape[0]
    rows = D // (Z * R * 2)
    flat = s_ref[...].astype(f32)
    below[0:D, :] = flat
    below[D:, :] = jnp.zeros((below.shape[0] - D, LANES), f32)
    ids = flat[:, at : at + 1] * 256.0 + below[seqs : seqs + D, at : at + 1]
    ids = ids.astype(jnp.int32) - ((me_ref[0] * R + me_ref[1]) * 2 + me_ref[2]) * trows
    line = lax.broadcasted_iota(jnp.int32, (D, trows), 0) % rows
    picker = (lax.broadcasted_iota(jnp.int32, (D, trows), 1) == ids) & (line < seqs)
    held[...] = dot(picker.astype(bf16), t_ref[...]).reshape(held.shape)
    for k, out in enumerate(outs):
        z = me_ref[0] ^ k
        tiles = [jnp.concatenate([held[z, r, 0, 0:seqs], held[z, r, 1, 0:seqs]], axis=0) for r in range(R)]
        out[...] = jnp.concatenate(tiles, axis=1).astype(bf16)


def ask(me, small, table, seqs, Z, N, at):
    D = small.shape[0]
    R, width = N // 2, table.shape[1]
    return once(
        functools.partial(ask_body, seqs, Z, R, at), "ask", (me, small, table), [SMEM, None, None],
        [sds((2 * seqs, R * width), bf16)] * Z,
        scratch=[pltpu.VMEM((D + 8, LANES), f32), pltpu.VMEM((Z, R, 2, D // (Z * N), width), f32)],
        flops=2 * D * width * table.shape[0], moved=2 * table.size,
    )


def place_body(n, cuts, turned, me_ref, *refs):
    pieces = refs[:n]
    outs = refs[n : n + len(cuts)]
    vec_ref = refs[n + len(cuts)] if turned else None
    held = refs[n + len(cuts) + turned : n + 2 * len(cuts) + turned]
    flat = refs[-3] if turned else None
    in_sem, out_sem = refs[-2:]
    Z = held[0].shape[0]
    copies = []
    for k in range(Z):
        for other in range(2):
            z = me_ref[0] ^ k
            for c, (lo, hi) in enumerate(cuts):
                copy = pltpu.make_async_copy(
                    pieces[other].at[:, k, 0 : held[c].shape[3], lo:hi], held[c].at[z, :, me_ref[2] ^ other], in_sem.at[len(copies)]
                )
                copies.append((copy, k))
    for copy, _ in copies:
        copy.start()
    last = []
    for k in range(Z):
        for copy, slot in copies:
            if slot == k:
                copy.wait()
        for c in range(len(cuts)):
            z = me_ref[0] ^ k
            last.append(pltpu.make_async_copy(held[c].at[z], outs[c].at[z], out_sem.at[k * len(cuts) + c]))
            last[-1].start()
    if turned:
        for z in range(Z):
            for r in range(held[-1].shape[1]):
                for c in range(2):
                    flat[z, r, c] = held[-1][z, r, c].astype(f32)
        vec_ref[...] = flat[...].reshape(vec_ref.shape[1], LANES).T[: vec_ref.shape[0]]
    for copy in last:
        copy.wait()


def place(me, pieces, Z, widths, turned=0, rows=None):
    n = len(pieces)
    R, rows = pieces[0].shape[0], rows or pieces[0].shape[-2]
    cuts = cut_points(widths)
    if turned and rows % 8:
        outs = place(me, pieces, Z, widths)
        return outs + [outs[-1][:, :turned].T.astype(f32)]
    shapes = [(Z, R, 2, rows, w) for w in widths]
    total = 2 * Z * R * rows
    outs = run(
        functools.partial(place_body, n, cuts, 1 if turned else 0), "place", (1,), (me, *pieces), [SMEM] + [ANY] * n,
        [sds(s, bf16) for s in shapes] + ([sds((turned, total), f32)] if turned else []),
        [ANY] * len(cuts) + ([full_spec((turned, total))] if turned else []),
        scratch=[pltpu.VMEM(s, bf16) for s in shapes] + ([pltpu.VMEM(shapes[-1], f32)] if turned else [])
        + [pltpu.SemaphoreType.DMA((2 * Z * len(cuts),)), pltpu.SemaphoreType.DMA((Z * len(cuts),))],
        moved=4 * total * cuts[-1][1], vmem=60,
    )
    return [o.reshape(total, o.shape[-1]) for o in outs[: len(cuts)]] + list(outs[len(cuts) :])


def hand_out(me_ref, part, Z, R, keep_ref, send_ref, cols=slice(None)):
    rows = part.shape[0] // (Z * R * 2)
    part = part.reshape(Z, R, 2, rows, part.shape[1])
    first = me_ref[2] == 0
    for z in range(Z):
        for r in range(R):
            one, two = part[z, r, 0], part[z, r, 1]
            keep_ref[r, z, :, cols] = jnp.where(first, one, two).astype(bf16)
            send_ref[r, z, :, cols] = jnp.where(first, two, one).astype(bf16)


def grads_body(plan, nvec, has_retr, Z, R, me_ref, *refs):
    at_out = len(refs) - 2 - (2 if nvec else 0)
    keep_ref, send_ref = refs[at_out : at_out + 2]
    col = 0

    def give(part):
        nonlocal col
        hand_out(me_ref, part, Z, R, keep_ref, send_ref, slice(col, col + part.shape[1]))
        col += part.shape[1]

    def read(spot):
        return refs[spot[0]][...] if spot[1] is None else refs[spot[0]][spot[1]]

    for lefts, right in plan:
        y = read(right)
        parts = [dot(read(left), y, 0, 0) for left in lefts]
        give(parts[0] if len(parts) == 1 else jnp.concatenate(parts, axis=0))
    at = at_out - nvec
    if has_retr:
        give(refs[at - 1][...])
    if nvec:
        turn = refs[-1]
        D = turn.shape[1]
        rows = D // (Z * R * 2)
        turn[...] = jnp.zeros_like(turn)
        row, lane = 0, 0
        for r in refs[at:at_out]:
            w = r.shape[1]
            if w <= D:
                turn[row : row + 1, lane : lane + w] = r[...]
                lane += w
                if lane == D:
                    row, lane = row + 1, 0
        total = turn[...].T
        r = refs[at_out - 1]
        if r.shape[1] > D:
            Q = r.shape[1] // D
            wide = refs[-2]
            wide[...] = jnp.zeros_like(wide)
            place_of = lax.broadcasted_iota(jnp.int32, r.shape, 1) % (Q * rows) // rows
            for q in range(Q):
                wide[row + q : row + q + 1, :] = jnp.where(place_of == q, r[...], 0.0)
            spread = wide[...].T.reshape(Z * R * 2, Q, rows, LANES)
            for q in range(Q):
                total += spread[:, q].reshape(total.shape)
        give(total)


def hand_out_plain(me, whole, Z, N, rows):
    whole = whole.astype(bf16).reshape(Z, N // 2, 2, rows, -1).swapaxes(0, 1)
    return [lax.dynamic_index_in_dim(whole, c, 2, keepdims=False) for c in (me[2], 1 - me[2])]


def grads(me, Z, N, name, arrays, plan, retr=None, vectors=(), tile=None):
    read = lambda spot: arrays[spot[0]] if spot[1] is None else arrays[spot[0]][spot[1]]
    shape = lambda spot: arrays[spot[0]].shape[-2:]
    D = sum(shape(left)[1] for left in plan[0][0])
    T = shape(plan[0][1])[0]
    rows, R = D // (Z * N), N // 2
    width = sum(shape(right)[1] for _, right in plan) + (0 if retr is None else retr.shape[1]) + (LANES if vectors else 0)
    if rows % 8:
        cols = [jnp.concatenate([dot(read(x), read(y), 0, 0) for x in xs], axis=0) for xs, y in plan]
        cols += [] if retr is None else [retr]
        if vectors:
            narrow = [jnp.concatenate([v for v in vectors if v.shape[1] <= D], axis=1).reshape(-1, D)]
            wide = [v.reshape(Z * N, -1, rows).swapaxes(0, 1).reshape(-1, D) for v in vectors if v.shape[1] > D]
            turned = jnp.concatenate(narrow + wide, axis=0).T
            cols += [turned, jnp.zeros((D, LANES - turned.shape[1]), f32)]
        return hand_out_plain(me, jnp.concatenate(cols, axis=1), Z, N, rows)
    ins = [*arrays] + ([] if retr is None else [retr]) + list(vectors)
    if tile is None:
        tile, specs, grid = width, [full_spec(a.shape) for a in ins], (1,)
    else:
        specs, grid = [full_spec(ins[0].shape), pl.BlockSpec((T, tile), lambda i: (0, i))], (width // tile,)
    return run(
        functools.partial(grads_body, plan, len(vectors), retr is not None, Z, R), name, grid, (me, *ins), [SMEM] + specs,
        [sds((R, Z, rows, width), bf16)] * 2, [pl.BlockSpec((R, Z, rows, tile), lambda i: (0, 0, 0, i))] * 2,
        scratch=[pltpu.VMEM((LANES, max(D, vectors[-1].shape[1])), f32), pltpu.VMEM((LANES, D), f32)] if vectors else [],
        flops=2 * T * D * width, moved=2 * T * (D + width) + 2 * D * width,
    )


def down_grad_body(me_ref, x_ref, y_ref, keep_ref, send_ref):
    hand_out(me_ref, dot(x_ref[...], y_ref[...], 0, 0), 1, keep_ref.shape[0], keep_ref, send_ref)


def down_grad(me, Z, N, act, feed):
    T, D = feed.shape
    F = act.shape[1]
    R, rows = N // 2, F // (Z * N)
    if rows % 8:
        return hand_out_plain(me, dot(act, feed, 0, 0), Z, N, rows)
    return run(
        down_grad_body, "down_grad", (Z,), (me, act, feed),
        [SMEM, pl.BlockSpec((T, N * rows), lambda i: (0, i)), full_spec(feed.shape)],
        [sds((R, Z, rows, D), bf16)] * 2, [pl.BlockSpec((R, 1, rows, D), lambda i: (0, i, 0, 0))] * 2,
        flops=2 * T * F * D, moved=2 * (T * F + T * D + F * D),
    )


def pair_body(n, me_ref, *refs):
    out_ref = refs[-1]
    width = out_ref.shape[3]
    at = 0
    for keep_ref, got_ref in zip(refs[:n], refs[n : 2 * n]):
        rows = keep_ref.shape[2]
        for lo in range(0, keep_ref.shape[3], width):
            cols = slice(lo, lo + width)
            out_ref[:, :, at : at + rows, :] = (
                keep_ref[:, :, :, cols].astype(f32) + got_ref[:, :, :, cols].astype(f32)
            ).astype(bf16)
            at += rows
    if len(refs) > 2 * n + 1:
        mine, other = refs[2 * n][...].astype(f32), refs[2 * n + 1][...].astype(f32)
        first = me_ref[2] == 0
        both = [jnp.where(first, mine, other), jnp.where(first, other, mine)]
        n_rows, w = mine.shape
        line = jnp.concatenate(both + [jnp.zeros((n_rows, width - 2 * w), f32)], axis=1).astype(bf16)
        for z in range(out_ref.shape[1]):
            out_ref[0, z, at : at + n_rows, :] = line


def pair_sum(parts, N, tok, me=None, term=None):
    n = len(parts)
    keeps = [keep for keep, _ in parts]
    got = [other_core(send, N) for _, send in parts]
    R, Z, _, width = keeps[0].shape
    rows = sum(k.size for k in keeps) // (R * Z * width)
    keeps[0] = after(keeps[0], tok)
    ins = keeps + got
    specs = [pl.BlockSpec((1,) + a.shape[1:], lambda i: (i, 0, 0, 0)) for a in ins]
    if term is not None:
        ins += [term, other_core(term, N)]
        specs += [full_spec(term.shape)] * 2
        rows += term.shape[0]
    return run(
        functools.partial(pair_body, n), "pair_sum", (R,), [jnp.zeros((3,), jnp.int32) if me is None else me] + ins, [SMEM] + specs,
        sds((R, Z, rows, width), bf16), pl.BlockSpec((1, Z, rows, width), lambda i: (i, 0, 0, 0)), moved=6 * R * Z * rows * width, vmem=60,
    )


def spots(n, width, shape):
    each = width // shape[1]
    return [(t // each * shape[0], t % each * shape[1]) for t in range(n)], -(-n // each) * shape[0]


def chips_body(term, me_ref, in_ref, *outs):
    R, _, rows, width = in_ref.shape
    rows -= term[0]
    where, _ = spots(2 * R, width, term)
    for k, out in enumerate(outs):
        z = me_ref[0] ^ k
        total = in_ref[0, z, :rows].astype(f32)
        for r in range(1, R):
            total += in_ref[r, z, :rows].astype(f32)
        out[:rows, :] = total.astype(out.dtype)
        if term[0]:
            out[rows:, :] = jnp.zeros((out.shape[0] - rows, width), out.dtype)
            for t, (row, col) in enumerate(where):
                tile = in_ref[t // 2, z, rows : rows + term[0], t % 2 * term[1] : (t % 2 + 1) * term[1]]
                out[rows + row : rows + row + term[0], col : col + term[1]] = tile.astype(out.dtype)


def chips_sum(me, got, tok, term=(0, LANES)):
    R, Z, rows, width = got.shape
    rows += spots(2 * R, width, term)[1] - term[0]
    return once(
        functools.partial(chips_body, term), "chips_sum", (me, after(got, tok)), [SMEM, None],
        [sds((rows, width), f32)] + [sds((rows, width), bf16)] * (Z - 1), moved=2 * got.size + 2 * Z * rows * width,
    )


def total_of(parts, lo, hi, rows=None):
    total = parts[0][:rows, lo:hi].astype(f32)
    for p in parts[1:]:
        total += p[:rows, lo:hi].astype(f32)
    return total


def last_body(n, cuts, G, gc, *refs):
    parts, (out_ref, in_ref, retr_ref, small_ref, turn) = refs[:n], refs[n:]
    rows = parts[0].shape[0]
    out_ref[...] = total_of(parts, *cuts[0])
    for g in range(G):
        for m in range(3):
            lo = cuts[1 + g][0] + m * gc
            in_ref[:, (m * G + g) * gc : (m * G + g + 1) * gc] = total_of(parts, lo, lo + gc)
    retr_ref[...] = total_of(parts, *cuts[1 + G])
    turn[...] = jnp.zeros_like(turn)
    turn[0:rows, :] = total_of(parts, *cuts[2 + G])
    small_ref[...] = turn[...].T[: small_ref.shape[0], :rows]


def last_sum(ins, widths, turned, G, gc, tok):
    rows = ins[0].shape[0]
    cuts = cut_points(widths)
    shapes = [(rows, widths[0]), (rows, 3 * G * gc), (rows, widths[-2]), (turned, rows)]
    return once(
        functools.partial(last_body, len(ins), cuts, G, gc), "last_sum", (after(ins[0], tok), *ins[1:]), [None] * len(ins),
        [sds(s, f32) for s in shapes], scratch=[pltpu.VMEM((LANES, LANES), f32)], moved=12 * rows * cuts[-1][1],
    )


def last_feed_body(n, term, N, me_ref, *refs):
    parts, (down_ref, up_ref, table_ref, held) = refs[:n], refs[n:]
    drows, D = down_ref.shape
    rows = up_ref.shape[0]
    total = total_of(parts, 0, D, 2 * drows)
    down_ref[...] = total[:drows]
    for q in range(drows // rows):
        up_ref[:, q * D : (q + 1) * D] = total[drows + q * rows : drows + (q + 1) * rows]
    where, _ = spots(N, D, term)
    trows = table_ref.shape[0]
    count, half = N * n * term[0], term[0] // 2
    for i, p in enumerate(parts):
        for t, (row, col) in enumerate(where):
            at = (i * N + t) * term[0]
            tile = p[2 * drows + row : 2 * drows + row + term[0], col : col + term[1]]
            held[at : at + term[0], :] = tile.astype(f32)
    held[count:, :] = jnp.zeros((term[0], term[1]), f32)
    below = held[half : half + count, :]
    ids = (below[:, 0:1] * 256.0 + below[:, 1:2]).astype(jnp.int32) - (me_ref[0] * N + 2 * me_ref[1] + me_ref[2]) * trows
    line = lax.broadcasted_iota(jnp.int32, (count, trows), 0) % term[0]
    picker = (lax.broadcasted_iota(jnp.int32, (count, trows), 1) == ids) & (line < half)
    table_ref[...] = dot(picker.astype(bf16), held[0:count, :].astype(bf16), 0, 0)


def last_feed(me, ins, F, tok, trows, term, N):
    D = ins[0].shape[1]
    both = ins[0].shape[0] - spots(N, D, term)[1]
    return once(
        functools.partial(last_feed_body, len(ins), term, N), "last_feed", (me, after(ins[0], tok), *ins[1:]), [SMEM] + [None] * len(ins),
        [sds((both // 2, D), f32), sds((both // 2 * D // F, F), f32), sds((trows, term[1]), f32)], moved=12 * both * D,
        scratch=[pltpu.VMEM(((N * len(ins) + 1) * term[0], term[1]), f32)],
    )


def along_dp_sums(sums):
    return [sums[0]] + [lax.ppermute(sums[k], "dp", pairs(len(sums), k)) for k in range(1, len(sums))]


def lookup_body(found, me_ref, sg_ref, r_ref, *refs):
    chosen_ref, back_ref, lead_ref = refs[found:]
    seqs = sg_ref.shape[0]
    chosen_ref[...] = jnp.zeros_like(chosen_ref)
    if found == 2:
        total = jnp.zeros((2 * seqs, r_ref.shape[1]), f32)
        for ref in refs[:2]:
            for r in range(ref.shape[0]):
                total += ref[r, 0, ref.shape[2] - 2 * seqs :].astype(f32)
        chosen_ref[0:seqs, :] = jnp.where(me_ref[2] == 0, total[:seqs], total[seqs:])
    else:
        chosen_ref[0:seqs, :] = refs[0][...].astype(f32)
    back_ref[...] = jnp.zeros_like(back_ref)
    back_ref[0:seqs, :] = sg_ref[...] * chosen_ref[0:seqs, :]
    lead = dot(back_ref[...].astype(bf16), r_ref[...], 1, 1)
    for s in range(seqs):
        lead_ref[s] = lead[s : s + 1, :]


def lookup(me, sg, wide, F, D, width, found):
    seqs = sg.shape[0]
    specs = [None]
    if len(found) == 2:
        specs = [pl.BlockSpec((a.shape[0], 1, a.shape[2], width), lambda i: (0, 0, 0, 0)) for a in found]
    return once(
        functools.partial(lookup_body, len(found)), "lookup", (me, sg, wide, *found),
        [SMEM, None, pl.BlockSpec((D, width), lambda i: (0, (F + D) // width))] + specs,
        [sds((16, width), f32), sds((16, width), f32), sds((seqs, 1, D), f32)], moved=4 * D * width,
    )


def score_body(top_ref, r_ref, chosen_ref, back_ref, sg_ref, id_ref, score_ref, retr_ref, term_ref, held):
    seqs = top_ref.shape[0]
    width = r_ref.shape[1]
    held[...] = jnp.zeros_like(held)
    for s in range(seqs):
        held[s : s + 1, :] = top_ref[s]
    leading = held[...].astype(bf16)
    projected = dot(leading, r_ref[...]).astype(bf16).astype(f32)[:seqs]
    score_ref[...] = jnp.sum(projected * chosen_ref[0:seqs, :], axis=-1, keepdims=True)
    retr_ref[...] = dot(leading, back_ref[...].astype(bf16), 0, 0)
    lane = lax.broadcasted_iota(jnp.int32, (seqs, width), 1)
    high, low = id_ref[...] // 256, id_ref[...] % 256
    ids = jnp.where(lane == 0, high, jnp.where(lane == 1, low, 0)).astype(f32)
    term_ref[...] = jnp.concatenate([sg_ref[...] * projected, ids], axis=0).astype(bf16)


def score(top, wide, F, chosen, back, sg, index):
    seqs, _, D = top.shape
    width = chosen.shape[1]
    return once(
        score_body, "score", (top, wide, chosen, back, sg, index),
        [None, pl.BlockSpec((D, width), lambda i: (0, (F + D) // width))] + [None] * 4,
        [sds((seqs, 1), f32), sds((D, width), f32), sds((2 * seqs, width), bf16)],
        scratch=[pltpu.VMEM((16, D), f32)], moved=8 * D * width,
    )


def bias_row_body(Z, N, Q, s_ref, v_ref, out_ref):
    D = s_ref.shape[0]
    rows = D // (Z * N)
    lane = lax.broadcasted_iota(jnp.int32, (Z * N, rows, LANES), 2)
    whole = s_ref[...].astype(f32).reshape(Z * N, rows, LANES)
    parts = [jnp.where(lane == UB + q, whole, 0.0).reshape(Z * N, 1, rows, LANES) for q in range(Q)]
    turned = jnp.concatenate(parts, axis=1).reshape(Q * D, LANES).T
    out_ref[...] = jnp.sum(turned, axis=0, keepdims=True)


def bias_row(small, vec, Z, N, Q):
    D = small.shape[0]
    rows = D // (Z * N)
    if rows % 8:
        return vec[UB : UB + Q].reshape(Q, Z * N, rows).transpose(1, 0, 2).reshape(1, Q * D)
    return once(
        functools.partial(bias_row_body, Z, N, Q), "bias_row", (small, vec), [None] * 2, [sds((1, Q * D), f32)],
        moved=8 * Q * D * LANES,
    )[0]


def local(
    Z, N, tokens, input_weight, query_bias, value_bias, output_weight, output_bias, first_gain, first_shift,
    up_weight, up_bias, down_weight, down_bias, second_gain, second_shift, retriever_weight, document_table,
    document_index, output_grad, score_grad,
):
    both = ("dp", "fsdp")
    T, D = tokens.shape
    R = N // 2
    F = up_weight.shape[1]
    Rw = retriever_weight.shape[1]
    seqs = document_index.shape[0]
    L = T // seqs
    per = 2 - seqs % 2
    gc = 4 * HEAD_DIM
    G = D // gc
    Q = F // D
    trows, rows = document_table.shape[0], input_weight.shape[0]
    f = lax.axis_index("fsdp")
    me = jnp.stack([lax.axis_index("dp"), f // 2, f % 2]).astype(jnp.int32)

    vectors = [
        v.reshape(1, -1)
        for v in (query_bias, value_bias, output_bias, first_gain, first_shift, down_bias, second_gain, second_shift, up_bias)
    ]
    head, rest, wide = pack(document_index, input_weight, output_weight, retriever_weight, up_weight, vectors, gc)
    wide = lax.all_gather(wide, both, axis=0, tiled=True)
    head = repeat(along_dp([head] * Z), R)
    rest = along_dp([after(rest, head)] * Z)
    head = between_chips(head, N)
    win_one, small, vec = place(me, [head, other_core(head, N)], Z, [3 * gc, LANES], turned=16)
    ub = bias_row(small, vec, Z, N, Q)
    rest = repeat([after(p, ub) for p in rest], R)
    if rows % 8:
        found, asked = [lax.all_gather(document_table, both, axis=0, tiled=True)[document_index]], ()
    else:
        asked = along_dp(ask(me, small, after(document_table, rest), seqs, Z, N, UB + Q))
    wd = along_dp([after(down_weight, rest)] * Z)
    rest = between_chips(rest, N)

    held = attend(after(tokens, ub), win_one, vec, seqs, G, 0)
    wd = repeat([after(w, held[2]) for w in wd], R, asked)
    rest = after(rest, wd)
    (win_two,) = place(me, [rest, other_core(rest, N)], Z, [3 * gc * (G - 1)])
    wd = between_chips(wd, N)
    qkv, soft, ctx = attend(tokens, win_two, vec, seqs, G, 1, held)
    wd = after(wd, ctx)
    n, inv, first, act, slope = up(ctx, tokens, vec, wide, ub, L, L // 2)
    wd = [wd, other_core(wd, N)]
    if rows % 8 == 0:
        found = wd
    (wd,) = place(me, [after(wd[0], first), wd[1]], Z, [D], rows=down_weight.shape[0])
    chosen, back_projected, lead = lookup(me, score_grad.reshape(seqs, 1), after(wide, first), F, D, Rw, found)
    final, top, two, feed, inner, gsg, gss, gdb, gub = down(first, act, slope, wd, vec, output_grad, lead, seqs, per)
    scores, retriever_back, term = score(top, wide, F, chosen, back_projected, score_grad.reshape(seqs, 1), document_index.reshape(seqs, 1))
    down_parts = down_grad(me, Z, N, act, feed)
    up_parts = grads(me, Z, N, "up_grad", [after(first, *down_parts), inner], [([(0, None)], (1, None))], tile=D)
    feed_sums = pair_sum([down_parts, up_parts], N, up_parts[0], me, term)
    one, att, bctx, gfg, gfs, gob = mid(after(two, feed_sums), inner, wide, n, inv, vec, per * L, L)
    mixed, gq, gv = attend_back(qkv, soft, ctx, after(bctx, feed_sums), seqs)
    parts = grads(
        me, Z, N, "mix_grad", [ctx, att, tokens, mixed],
        [([(0, g) for g in range(G)], (1, None))] + [([(2, None)], (3, g)) for g in range(G)],
        retr=retriever_back, vectors=[gq, gv, gob, gfg, gfs, gdb, gsg, gss, gub],
    )
    mix_pair = pair_sum([parts], N, parts[0])
    feed_sums = between_chips(feed_sums, N)
    mix_sums = between_chips(after(mix_pair, feed_sums), N)
    feed_sums = chips_sum(me, feed_sums, mix_pair, term.shape)
    back_tokens = tokens_back(after(one, feed_sums[0]), mixed, [win_one, win_two], L)
    mix_sums = chips_sum(me, mix_sums, back_tokens)
    down_back, up_back, table_back = last_feed(me, along_dp_sums(feed_sums), F, mix_sums[0], trows, term.shape, N)
    output_back, input_back, retriever_back, small = last_sum(
        along_dp_sums(mix_sums), [D] + [3 * gc] * G + [Rw, LANES], 16, G, gc, down_back
    )
    ub_back = small[8 : 8 + Q].reshape(-1)
    return (
        final, scores.reshape(seqs), back_tokens, input_back, small[0], small[1], output_back, small[2], small[3], small[4],
        up_back, ub_back, down_back, small[5], small[6], small[7], retriever_back, table_back,
    )


def solution(mesh):
    both = ("dp", "fsdp")
    mat, vec = P(both, None), P(both)
    in_specs = (mat, mat, vec, vec, mat, vec, vec, vec, mat, vec, mat, vec, vec, vec, mat, mat, vec, mat, vec)
    out_specs = (mat, vec, mat, mat, vec, vec, mat, vec, vec, vec, mat, vec, mat, vec, vec, vec, mat, mat)
    body = functools.partial(local, mesh.shape["dp"], mesh.shape["fsdp"])
    return jax.shard_map(body, mesh=mesh, in_specs=in_specs, out_specs=out_specs, check_vma=False)
```

```python
import functools
import math
import jax
import jax.numpy as jnp
from jax import lax
from jax.experimental import pallas as pl
from jax.experimental.pallas import tpu as pltpu
from jax.sharding import PartitionSpec as P

HEAD_DIM = 64
EPS = 1e-12
ROOM = {"tokens_back": 28, "chips_sum": 28, "last_sum": 28, "last_feed": 28, "pair_sum": 28, "lookup": 28, "score": 28, "place": 28, "repeat": 28, "ask": 28, "bias_row": 28}
QB, VB, OB, FG, FS, DB, SG, SS, UB = range(9)
bf16, f32 = jnp.bfloat16, jnp.float32


def dot(a, b, ca=1, cb=0):
    return lax.dot_general(a, b, (((ca,), (cb,)), ((), ())), preferred_element_type=f32)


def rows_spec(rows, cols):
    return pl.BlockSpec((rows, cols), lambda i: (i, 0))


def full_spec(shape):
    return pl.BlockSpec(shape, lambda *_: (0,) * len(shape))


def head_mask(rows, cols, h):
    lane = lax.broadcasted_iota(jnp.int32, (rows, cols), 1)
    return (lane >= h * HEAD_DIM) & (lane < (h + 1) * HEAD_DIM)


def run(body, name, grid, ins, in_specs, outs, out_specs, scratch=(), flops=0, moved=0, alias=None):
    return pl.pallas_call(
        body,
        name=name,
        grid=grid,
        in_specs=in_specs,
        out_specs=out_specs,
        out_shape=outs,
        scratch_shapes=list(scratch),
        cost_estimate=estimate(flops, moved),
        input_output_aliases=alias or {},
        compiler_params=pltpu.CompilerParams(vmem_limit_bytes=ROOM.get(name, 60) * 2**20),
    )(*ins)


def estimate(flops, moved):
    return pl.CostEstimate(flops=int(flops), bytes_accessed=int(moved), transcendentals=0)


def sds(shape, dtype):
    return jax.ShapeDtypeStruct(shape, dtype)


def attend_body(x_ref, w_ref, v_ref, *refs):
    qkv_ref, soft_ref, ctx_ref = refs[-3:]
    length = x_ref.shape[0]
    gc = ctx_ref.shape[1]
    mixed = dot(x_ref[...], w_ref[...])
    q = (mixed[:, :gc] + v_ref[QB : QB + 1, :]).astype(bf16)
    k = mixed[:, gc : 2 * gc].astype(bf16)
    v = (mixed[:, 2 * gc :] + v_ref[VB : VB + 1, :]).astype(bf16)
    qkv_ref[:, :gc] = q
    qkv_ref[:, gc : 2 * gc] = k
    qkv_ref[:, 2 * gc :] = v
    qs = q * bf16(HEAD_DIM ** -0.5)
    zero = jnp.zeros((), bf16)
    total = jnp.zeros((length, gc), f32)
    for h in range(gc // HEAD_DIM):
        mask = head_mask(length, gc, h)
        s = dot(jnp.where(mask, qs, zero), k, 1, 1)
        peak = jnp.max(s, axis=-1, keepdims=True)
        e = jnp.exp(s - peak)
        norm = 1.0 / jnp.sum(e, axis=-1, keepdims=True)
        p = (e * norm).astype(bf16)
        soft_ref[h] = p
        total += dot(p, jnp.where(mask, v, zero))
    ctx_ref[...] = total.astype(bf16)


def attend(x, w, vec, seqs, groups, at, into=()):
    T, D = x.shape
    gc = D // groups
    hg = gc // HEAD_DIM
    L = T // seqs
    count = w.shape[1] // (3 * gc)
    ins = (x, w, vec, *into)
    return run(
        attend_body, "attend", (count, seqs), ins,
        [
            pl.BlockSpec((L, D), lambda g, s: (s, 0)), pl.BlockSpec((D, 3 * gc), lambda g, s: (0, g)),
            pl.BlockSpec((vec.shape[0], gc), lambda g, s: (0, at + g)),
        ] + [pl.BlockSpec(memory_space=pl.ANY)] * len(into),
        [sds((groups, T, 3 * gc), bf16), sds((groups, hg, T, L), bf16), sds((groups, T, gc), bf16)],
        [
            pl.BlockSpec((None, L, 3 * gc), lambda g, s: (at + g, s, 0)),
            pl.BlockSpec((None, hg, L, L), lambda g, s: (at + g, 0, s, 0)),
            pl.BlockSpec((None, L, gc), lambda g, s: (at + g, s, 0)),
        ],
        flops=count * (2 * T * D * 3 * gc + 16 * T * L * gc), moved=2 * (T * D + w.size + count * (4 * T * gc + hg * T * L)),
        alias={3 + i: i for i in range(len(into))},
    )


def norm_rows(h):
    mean = jnp.mean(h, axis=-1, keepdims=True)
    c = h - mean
    var = jnp.mean(c * c, axis=-1, keepdims=True)
    inv = lax.rsqrt(var + EPS)
    return c * inv, inv


def norm_rows_back(cot, n, inv, gain):
    scaled = cot * gain
    return inv * (scaled - jnp.mean(scaled, axis=-1, keepdims=True) - n * jnp.mean(scaled * n, axis=-1, keepdims=True))


def in_turn(blocks, first, then):
    held = first(blocks[0])
    for i, block in enumerate(blocks):
        ahead = first(blocks[i + 1]) if i + 1 < len(blocks) else None
        then(i, block, held)
        held = ahead


def blocks_of(rows, size):
    return [slice(at, at + size) for at in range(0, rows, size)]


def up_body(size, step, ctx_ref, x_ref, wo_ref, v_ref, wu_ref, ub_ref, n_ref, inv_ref, first_ref, act_ref, slope_ref):
    G, rows, gc = ctx_ref.shape

    def attended(block):
        hidden = x_ref[block].astype(f32) + v_ref[OB : OB + 1, :]
        for g in range(G):
            hidden += dot(ctx_ref[g, block], wo_ref[g * gc : (g + 1) * gc, :])
        return hidden

    def rest(_, block, hidden):
        n, inv = norm_rows(hidden)
        n_ref[block] = n
        inv_ref[block] = inv
        first = (n * v_ref[FG : FG + 1, :] + v_ref[FS : FS + 1, :]).astype(bf16)
        first_ref[block] = first
        ff = wu_ref.shape[1]
        for at in range(0, ff, step):
            cols = slice(at, at + step)
            u = dot(first, wu_ref[:, cols]) + ub_ref[:, cols]
            phi = 0.5 + 0.5 * lax.erf(u * math.sqrt(0.5))
            act_ref[block, cols] = (u * phi).astype(bf16)
            slope_ref[block, cols] = (phi + u * jnp.exp(u * u * -0.5) * (1.0 / math.sqrt(2 * math.pi))).astype(bf16)

    in_turn(blocks_of(rows, size), attended, rest)


def out_spec(D, F):
    return pl.BlockSpec((D, D), lambda i: (0, F // D))


def up(ctx, x, vec, wide, ub, rows, size, step=512):
    T, D = x.shape
    F = ub.shape[1]
    return run(
        functools.partial(up_body, size, step), "up", (T // rows,), (ctx, x, wide, vec, wide, ub),
        [pl.BlockSpec((ctx.shape[0], rows, ctx.shape[2]), lambda i: (0, i, 0)), rows_spec(rows, D)] + [out_spec(D, F), full_spec(vec.shape), full_spec((D, F)), full_spec(ub.shape)],
        [sds((T, D), f32), sds((T, 1), f32), sds((T, D), bf16), sds((T, F), bf16), sds((T, F), bf16)],
        [rows_spec(rows, D), rows_spec(rows, 1), rows_spec(rows, D), rows_spec(rows, F), rows_spec(rows, F)],
        flops=2 * T * D * (D + F), moved=T * D * 10 + 4 * T * F + 2 * D * (D + F),
    )


def add_rows(ref, value, cols=slice(None), axis=0):
    held = jnp.where(pl.program_id(axis) == 0, 0.0, ref[:, cols])
    ref[:, cols] = held + jnp.sum(value, axis=0, keepdims=True)


def down_body(size, step, first_ref, act_ref, slope_ref, w_ref, v_ref, og_ref, lead_ref,
              out_ref, top_ref, two_ref, feed_ref, inner_ref, gg_ref, gs_ref, gb_ref, gub_ref):
    gain = v_ref[SG : SG + 1, :]
    ff = w_ref.shape[0]
    sums = {}

    def count(name, value):
        total = jnp.sum(value, axis=0, keepdims=True)
        sums[name] = sums[name] + total if name in sums else total

    def fed(block):
        return first_ref[block].astype(f32) + v_ref[DB : DB + 1, :] + dot(act_ref[block], w_ref[...])

    def rest(i, block, hidden):
        n, inv = norm_rows(hidden)
        out = (n * gain + v_ref[SS : SS + 1, :]).astype(bf16)
        out_ref[block] = out
        top_ref[i] = out[0:16, :].astype(f32)[0:1, :]
        row = lax.broadcasted_iota(jnp.int32, (size, 1), 0)
        cot = og_ref[block].astype(f32) + jnp.where(row == 0, lead_ref[i], 0.0)
        count("gain", cot * n)
        count("shift", cot)
        two = norm_rows_back(cot, n, inv, gain)
        two_ref[block] = two
        feed = two.astype(bf16)
        feed_ref[block] = feed
        count("bias", feed.astype(f32))
        for at in range(0, ff, step):
            cols = slice(at, at + step)
            inner = (dot(feed, w_ref[cols, :], 1, 1) * slope_ref[block, cols].astype(f32)).astype(bf16)
            inner_ref[block, cols] = inner
            count(at, inner.astype(f32))

    in_turn(blocks_of(first_ref.shape[0], size), fed, rest)
    add_rows(gg_ref, sums["gain"])
    add_rows(gs_ref, sums["shift"])
    add_rows(gb_ref, sums["bias"])
    for at in range(0, ff, step):
        add_rows(gub_ref, sums[at], slice(at, at + step))


def down(first, act, slope, w, vec, og, lead, seqs, per, step=512):
    T, D = first.shape
    F = act.shape[1]
    L = T // seqs
    rows = per * L
    each = pl.BlockSpec((per, 1, D), lambda i: (i, 0, 0))
    return run(
        functools.partial(down_body, L, step), "down", (seqs // per,), (first, act, slope, w, vec, og, lead),
        [rows_spec(rows, D), rows_spec(rows, F), rows_spec(rows, F), full_spec((F, D)), full_spec(vec.shape), rows_spec(rows, D), each],
        [sds((T, D), bf16), sds((seqs, 1, D), f32), sds((T, D), f32), sds((T, D), bf16), sds((T, F), bf16),
         sds((1, D), f32), sds((1, D), f32), sds((1, D), f32), sds((1, F), f32)],
        [rows_spec(rows, D), each, rows_spec(rows, D), rows_spec(rows, D), rows_spec(rows, F)]
        + [full_spec((1, D))] * 3 + [full_spec((1, F))],
        flops=4 * T * D * F, moved=6 * T * F + 12 * T * D + 2 * F * D,
    )


def mid_body(size, two_ref, inner_ref, wu_ref, n_ref, inv_ref, v_ref, wo_ref,
             one_ref, att_ref, bctx_ref, gg_ref, gs_ref, gob_ref):
    sums = {}

    def count(name, value):
        total = jnp.sum(value, axis=0, keepdims=True)
        sums[name] = sums[name] + total if name in sums else total

    def back(block):
        return two_ref[block] + dot(inner_ref[block], wu_ref[...], 1, 1)

    def rest(_, block, cot):
        n = n_ref[block]
        count("gain", cot * n)
        count("shift", cot)
        one = norm_rows_back(cot, n, inv_ref[block], v_ref[FG : FG + 1, :])
        one_ref[block] = one
        att = one.astype(bf16)
        att_ref[block] = att
        count("bias", att.astype(f32))
        bctx_ref[block] = dot(att, wo_ref[...], 1, 1).astype(bf16)

    in_turn(blocks_of(two_ref.shape[0], size), back, rest)
    add_rows(gg_ref, sums["gain"])
    add_rows(gs_ref, sums["shift"])
    add_rows(gob_ref, sums["bias"])


def mid(two, inner, wide, n, inv, vec, rows, size):
    T, D = two.shape
    F = inner.shape[1]
    return run(
        functools.partial(mid_body, size), "mid", (T // rows,), (two, inner, wide, n, inv, vec, wide),
        [rows_spec(rows, D), rows_spec(rows, F), full_spec((D, F)), rows_spec(rows, D), rows_spec(rows, 1), full_spec(vec.shape), out_spec(D, F)],
        [sds((T, D), f32), sds((T, D), bf16), sds((T, D), bf16)] + [sds((1, D), f32)] * 3,
        [rows_spec(rows, D)] * 3 + [full_spec((1, D))] * 3,
        flops=2 * T * D * (F + D), moved=2 * T * F + 16 * T * D + 2 * D * (D + F),
    )


def attend_back_body(qkv_ref, soft_ref, ctx_ref, bctx_ref, out_ref, gq_ref, gv_ref):
    length, gc = ctx_ref.shape
    q = qkv_ref[:, :gc]
    k = qkv_ref[:, gc : 2 * gc]
    v = qkv_ref[:, 2 * gc :]
    do = bctx_ref[...]
    prod = do.astype(f32) * ctx_ref[...].astype(f32)
    zero = jnp.zeros((), bf16)
    dq = jnp.zeros((length, gc), f32)
    dk = jnp.zeros((length, gc), f32)
    dv = jnp.zeros((length, gc), f32)
    for h in range(gc // HEAD_DIM):
        mask = head_mask(length, gc, h)
        p = soft_ref[h]
        do_h = jnp.where(mask, do, zero)
        dp = dot(do_h, v, 1, 1)
        delta = jnp.sum(jnp.where(mask, prod, 0.0), axis=-1, keepdims=True)
        ds = (p.astype(f32) * (dp - delta)).astype(bf16)
        dv += dot(p, do_h, 0, 0)
        dq += dot(ds, jnp.where(mask, k, zero))
        dk += dot(ds, jnp.where(mask, q, zero), 0, 0)
    scale = HEAD_DIM ** -0.5
    dq = (dq * scale).astype(bf16)
    dv = dv.astype(bf16)
    out_ref[:, :gc] = dq
    out_ref[:, gc : 2 * gc] = (dk * scale).astype(bf16)
    out_ref[:, 2 * gc :] = dv
    add_rows(gq_ref, dq.astype(f32), axis=1)
    add_rows(gv_ref, dv.astype(f32), axis=1)


def attend_back(qkv, soft, ctx, bctx, seqs):
    G, T, gc = ctx.shape
    hg = gc // HEAD_DIM
    L = T // seqs
    line = lambda w: pl.BlockSpec((None, L, w), lambda g, s: (g, s, 0))
    row = pl.BlockSpec((1, gc), lambda g, s: (0, g))
    return run(
        attend_back_body, "attend_back", (G, seqs), (qkv, soft, ctx, bctx),
        [
            line(3 * gc), pl.BlockSpec((None, hg, L, L), lambda g, s: (g, 0, s, 0)), line(gc),
            pl.BlockSpec((L, gc), lambda g, s: (s, g)),
        ],
        [sds((G, T, 3 * gc), bf16), sds((1, G * gc), f32), sds((1, G * gc), f32)], [line(3 * gc), row, row],
        flops=G * 32 * T * L * gc, moved=2 * G * (8 * T * gc + hg * T * L),
    )


def tokens_back_body(one_ref, mixed_ref, *refs):
    total = one_ref[...]
    width = mixed_ref.shape[2]
    g = 0
    for w_ref in refs[:-1]:
        for at in range(0, w_ref.shape[1], width):
            total += dot(mixed_ref[g], w_ref[:, at : at + width], 1, 1)
            g += 1
    refs[-1][...] = total.astype(bf16)


def tokens_back(one, mixed, ws, rows):
    T, D = one.shape
    G, _, width = mixed.shape
    return run(
        tokens_back_body, "tokens_back", (T // rows,), (one, mixed, *ws),
        [rows_spec(rows, D), pl.BlockSpec((G, rows, width), lambda i: (0, i, 0))] + [full_spec(w.shape) for w in ws],
        sds((T, D), bf16), rows_spec(rows, D), flops=2 * T * D * G * width, moved=T * D * 12,
    )


def after(x, *deps):
    return lax.optimization_barrier((x,) + deps)[0]


ANY = pl.BlockSpec(memory_space=pl.ANY)
SMEM = pl.BlockSpec(memory_space=pltpu.SMEM)
LANES = 128


def once(body, name, ins, in_specs, outs, scratch=(), moved=0, flops=0):
    specs = [full_spec(a.shape) if spec is None else spec for a, spec in zip(ins, in_specs)]
    return run(body, name, (1,), ins, specs, outs, [full_spec(o.shape) for o in outs], scratch, flops, moved)


def cut_points(widths):
    cuts, at = [], 0
    for w in widths:
        cuts.append((at, at + w))
        at += w
    return cuts


def pack_body(D, gc, nvec, *refs):
    id_ref, w_ref, o_ref, r_ref, u_ref = refs[:5]
    head_ref, rest_ref, up_ref, held = refs[5 + nvec :]
    G = D // gc
    rows = w_ref.shape[0]
    held[...] = jnp.zeros_like(held)
    row = 0
    for v_ref in refs[5 : 5 + nvec]:
        v = v_ref[...].astype(f32)
        for at in range(0, v.shape[1], rows):
            held[row : row + 1, 0:rows] = v[:, at : at + rows]
            row += 1
    lane = lax.broadcasted_iota(jnp.int32, (1, LANES), 1)
    ids = jnp.zeros((1, LANES), jnp.int32)
    seqs = id_ref.shape[0]
    for i in range(seqs):
        ids = jnp.where(lane == i, id_ref[i] // 256, jnp.where(lane == seqs + i, id_ref[i] % 256, ids))
    held[row : row + 1, :] = ids.astype(f32)
    turned = held[...].T
    for m in range(3):
        head_ref[:, m * gc : (m + 1) * gc] = w_ref[:, m * D : m * D + gc]
    head_ref[:, 3 * gc :] = turned[:rows, :].astype(bf16)
    at = 0
    for g in range(1, G):
        for m in range(3):
            rest_ref[:, at : at + gc] = w_ref[:, m * D + g * gc : m * D + (g + 1) * gc]
            at += gc
    F = u_ref.shape[1]
    up_ref[:, :F] = u_ref[...]
    up_ref[:, F : F + D] = o_ref[...]
    up_ref[:, F + D :] = r_ref[...]


def pack(ids, w, o, r, u, vectors, gc):
    rows, D = o.shape
    head = 3 * gc + LANES
    rest = 3 * D - 3 * gc
    ups = u.shape[1] + D + r.shape[1]
    return once(
        functools.partial(pack_body, D, gc, len(vectors)), "pack", (ids, w, o, r, u, *vectors), [SMEM] + [None] * (4 + len(vectors)),
        [sds((rows, head), bf16), sds((rows, rest), bf16), sds((rows, ups), bf16)],
        scratch=[pltpu.VMEM((LANES, LANES), f32)], moved=4 * rows * (head + rest + ups),
    )


def pairs(n, flip):
    return [(i, i ^ flip) for i in range(n)]


def along_dp(blocks):
    return [blocks[0]] + [lax.ppermute(b, "dp", pairs(len(blocks), k)) for k, b in enumerate(blocks) if k]


def between_chips(blocks, N):
    return lax.all_to_all(blocks, "fsdp", 0, 0, axis_index_groups=[list(range(c, N, 2)) for c in range(2)], tiled=True)


def other_core(blocks, N):
    return lax.ppermute(blocks, "fsdp", pairs(N, 1))


def repeat_body(n, *refs):
    out, blocks, tiles = refs[-1], refs[:n], refs[n:-1]
    rows, width = blocks[0].shape
    for r in range(out.shape[0]):
        for k, ref in enumerate(blocks):
            out[r, k, :rows] = ref[...]
        if tiles:
            w = tiles[0].shape[1] // out.shape[0]
            total = tiles[0][:, r * w : (r + 1) * w].astype(f32)
            for ref in tiles[1:]:
                total += ref[:, r * w : (r + 1) * w].astype(f32)
            blank = jnp.zeros((total.shape[0], width - w), f32)
            out[r, 0, rows:] = jnp.concatenate([total, blank], axis=1).astype(bf16)
            for k in range(1, n):
                out[r, k, rows:] = jnp.zeros((total.shape[0], width), bf16)


def repeat(blocks, R, tiles=()):
    n = len(blocks)
    rows, width = blocks[0].shape
    rows += tiles[0].shape[0] if tiles else 0
    return once(
        functools.partial(repeat_body, n), "repeat", [*blocks, *tiles], [None] * (n + len(tiles)),
        [sds((R, n, rows, width), bf16)], moved=2 * (R + 1) * n * rows * width,
    )[0]


def ask_body(seqs, Z, R, at, me_ref, s_ref, t_ref, *refs):
    outs, below, held = refs[:Z], refs[Z], refs[Z + 1]
    D, trows = s_ref.shape[0], t_ref.shape[0]
    rows = D // (Z * R * 2)
    flat = s_ref[...].astype(f32)
    below[0:D, :] = flat
    below[D:, :] = jnp.zeros((below.shape[0] - D, LANES), f32)
    ids = flat[:, at : at + 1] * 256.0 + below[seqs : seqs + D, at : at + 1]
    ids = ids.astype(jnp.int32) - ((me_ref[0] * R + me_ref[1]) * 2 + me_ref[2]) * trows
    line = lax.broadcasted_iota(jnp.int32, (D, trows), 0) % rows
    picker = (lax.broadcasted_iota(jnp.int32, (D, trows), 1) == ids) & (line < seqs)
    held[...] = dot(picker.astype(bf16), t_ref[...]).reshape(held.shape)
    for k, out in enumerate(outs):
        z = me_ref[0] ^ k
        tiles = [jnp.concatenate([held[z, r, 0, 0:seqs], held[z, r, 1, 0:seqs]], axis=0) for r in range(R)]
        out[...] = jnp.concatenate(tiles, axis=1).astype(bf16)


def ask(me, small, table, seqs, Z, N, at):
    D = small.shape[0]
    R, width = N // 2, table.shape[1]
    return once(
        functools.partial(ask_body, seqs, Z, R, at), "ask", (me, small, table), [SMEM, None, None],
        [sds((2 * seqs, R * width), bf16)] * Z,
        scratch=[pltpu.VMEM((D + 8, LANES), f32), pltpu.VMEM((Z, R, 2, D // (Z * N), width), f32)],
        flops=2 * D * width * table.shape[0], moved=2 * table.size,
    )


def place_body(n, cuts, turned, me_ref, *refs):
    pieces = refs[:n]
    outs = refs[n : n + len(cuts)]
    vec_ref = refs[n + len(cuts)] if turned else None
    held = refs[n + len(cuts) + turned : n + 2 * len(cuts) + turned]
    flat = refs[-3] if turned else None
    in_sem, out_sem = refs[-2:]
    Z = held[0].shape[0]
    copies = []
    for k in range(Z):
        for other in range(2):
            z = me_ref[0] ^ k
            for c, (lo, hi) in enumerate(cuts):
                copy = pltpu.make_async_copy(
                    pieces[other].at[:, k, 0 : held[c].shape[3], lo:hi], held[c].at[z, :, me_ref[2] ^ other], in_sem.at[len(copies)]
                )
                copies.append((copy, k))
    for copy, _ in copies:
        copy.start()
    last = []
    for k in range(Z):
        for copy, slot in copies:
            if slot == k:
                copy.wait()
        for c in range(len(cuts)):
            z = me_ref[0] ^ k
            last.append(pltpu.make_async_copy(held[c].at[z], outs[c].at[z], out_sem.at[k * len(cuts) + c]))
            last[-1].start()
    if turned:
        for z in range(Z):
            for r in range(held[-1].shape[1]):
                for c in range(2):
                    flat[z, r, c] = held[-1][z, r, c].astype(f32)
        vec_ref[...] = flat[...].reshape(vec_ref.shape[1], LANES).T[: vec_ref.shape[0]]
    for copy in last:
        copy.wait()


def place(me, pieces, Z, widths, turned=0, rows=None):
    n = len(pieces)
    R, rows = pieces[0].shape[0], rows or pieces[0].shape[-2]
    cuts = cut_points(widths)
    if turned and rows % 8:
        outs = place(me, pieces, Z, widths)
        return outs + [outs[-1][:, :turned].T.astype(f32)]
    shapes = [(Z, R, 2, rows, w) for w in widths]
    total = 2 * Z * R * rows
    outs = run(
        functools.partial(place_body, n, cuts, 1 if turned else 0), "place", (1,), (me, *pieces), [SMEM] + [ANY] * n,
        [sds(s, bf16) for s in shapes] + ([sds((turned, total), f32)] if turned else []),
        [ANY] * len(cuts) + ([full_spec((turned, total))] if turned else []),
        scratch=[pltpu.VMEM(s, bf16) for s in shapes] + ([pltpu.VMEM(shapes[-1], f32)] if turned else [])
        + [pltpu.SemaphoreType.DMA((2 * Z * len(cuts),)), pltpu.SemaphoreType.DMA((Z * len(cuts),))],
        moved=4 * total * cuts[-1][1],
    )
    return [o.reshape(total, o.shape[-1]) for o in outs[: len(cuts)]] + list(outs[len(cuts) :])


def hand_out(me_ref, part, Z, R, keep_ref, send_ref, cols=slice(None)):
    rows = part.shape[0] // (Z * R * 2)
    part = part.reshape(Z, R, 2, rows, part.shape[1])
    first = me_ref[2] == 0
    for z in range(Z):
        for r in range(R):
            one, two = part[z, r, 0], part[z, r, 1]
            keep_ref[r, z, :, cols] = jnp.where(first, one, two).astype(bf16)
            send_ref[r, z, :, cols] = jnp.where(first, two, one).astype(bf16)


def grads_body(plan, nvec, has_retr, Z, R, me_ref, *refs):
    at_out = len(refs) - 2 - (2 if nvec else 0)
    keep_ref, send_ref = refs[at_out : at_out + 2]
    col = 0

    def give(part):
        nonlocal col
        hand_out(me_ref, part, Z, R, keep_ref, send_ref, slice(col, col + part.shape[1]))
        col += part.shape[1]

    def read(spot):
        return refs[spot[0]][...] if spot[1] is None else refs[spot[0]][spot[1]]

    for lefts, right in plan:
        y = read(right)
        parts = [dot(read(left), y, 0, 0) for left in lefts]
        give(parts[0] if len(parts) == 1 else jnp.concatenate(parts, axis=0))
    at = at_out - nvec
    if has_retr:
        give(refs[at - 1][...])
    if nvec:
        turn = refs[-1]
        D = turn.shape[1]
        rows = D // (Z * R * 2)
        turn[...] = jnp.zeros_like(turn)
        row, lane = 0, 0
        for r in refs[at:at_out]:
            w = r.shape[1]
            if w <= D:
                turn[row : row + 1, lane : lane + w] = r[...]
                lane += w
                if lane == D:
                    row, lane = row + 1, 0
        total = turn[...].T
        r = refs[at_out - 1]
        if r.shape[1] > D:
            Q = r.shape[1] // D
            wide = refs[-2]
            wide[...] = jnp.zeros_like(wide)
            place_of = lax.broadcasted_iota(jnp.int32, r.shape, 1) % (Q * rows) // rows
            for q in range(Q):
                wide[row + q : row + q + 1, :] = jnp.where(place_of == q, r[...], 0.0)
            spread = wide[...].T.reshape(Z * R * 2, Q, rows, LANES)
            for q in range(Q):
                total += spread[:, q].reshape(total.shape)
        give(total)


def hand_out_plain(me, whole, Z, N, rows):
    whole = whole.astype(bf16).reshape(Z, N // 2, 2, rows, -1).swapaxes(0, 1)
    return [lax.dynamic_index_in_dim(whole, c, 2, keepdims=False) for c in (me[2], 1 - me[2])]


def grads(me, Z, N, name, arrays, plan, retr=None, vectors=(), tile=None):
    read = lambda spot: arrays[spot[0]] if spot[1] is None else arrays[spot[0]][spot[1]]
    shape = lambda spot: arrays[spot[0]].shape[-2:]
    D = sum(shape(left)[1] for left in plan[0][0])
    T = shape(plan[0][1])[0]
    rows, R = D // (Z * N), N // 2
    width = sum(shape(right)[1] for _, right in plan) + (0 if retr is None else retr.shape[1]) + (LANES if vectors else 0)
    if rows % 8:
        cols = [jnp.concatenate([dot(read(x), read(y), 0, 0) for x in xs], axis=0) for xs, y in plan]
        cols += [] if retr is None else [retr]
        if vectors:
            narrow = [jnp.concatenate([v for v in vectors if v.shape[1] <= D], axis=1).reshape(-1, D)]
            wide = [v.reshape(Z * N, -1, rows).swapaxes(0, 1).reshape(-1, D) for v in vectors if v.shape[1] > D]
            turned = jnp.concatenate(narrow + wide, axis=0).T
            cols += [turned, jnp.zeros((D, LANES - turned.shape[1]), f32)]
        return hand_out_plain(me, jnp.concatenate(cols, axis=1), Z, N, rows)
    ins = [*arrays] + ([] if retr is None else [retr]) + list(vectors)
    if tile is None:
        tile, specs, grid = width, [full_spec(a.shape) for a in ins], (1,)
    else:
        specs, grid = [full_spec(ins[0].shape), pl.BlockSpec((T, tile), lambda i: (0, i))], (width // tile,)
    return run(
        functools.partial(grads_body, plan, len(vectors), retr is not None, Z, R), name, grid, (me, *ins), [SMEM] + specs,
        [sds((R, Z, rows, width), bf16)] * 2, [pl.BlockSpec((R, Z, rows, tile), lambda i: (0, 0, 0, i))] * 2,
        scratch=[pltpu.VMEM((LANES, max(D, vectors[-1].shape[1])), f32), pltpu.VMEM((LANES, D), f32)] if vectors else [],
        flops=2 * T * D * width, moved=2 * T * (D + width) + 2 * D * width,
    )


def down_grad_body(me_ref, x_ref, y_ref, keep_ref, send_ref):
    hand_out(me_ref, dot(x_ref[...], y_ref[...], 0, 0), 1, keep_ref.shape[0], keep_ref, send_ref)


def down_grad(me, Z, N, act, feed):
    T, D = feed.shape
    F = act.shape[1]
    R, rows = N // 2, F // (Z * N)
    if rows % 8:
        return hand_out_plain(me, dot(act, feed, 0, 0), Z, N, rows)
    return run(
        down_grad_body, "down_grad", (Z,), (me, act, feed),
        [SMEM, pl.BlockSpec((T, N * rows), lambda i: (0, i)), full_spec(feed.shape)],
        [sds((R, Z, rows, D), bf16)] * 2, [pl.BlockSpec((R, 1, rows, D), lambda i: (0, i, 0, 0))] * 2,
        flops=2 * T * F * D, moved=2 * (T * F + T * D + F * D),
    )


def pair_body(n, me_ref, *refs):
    out_ref = refs[-1]
    width = out_ref.shape[3]
    at = 0
    for keep_ref, got_ref in zip(refs[:n], refs[n : 2 * n]):
        rows = keep_ref.shape[2]
        for lo in range(0, keep_ref.shape[3], width):
            cols = slice(lo, lo + width)
            out_ref[:, :, at : at + rows, :] = (
                keep_ref[:, :, :, cols].astype(f32) + got_ref[:, :, :, cols].astype(f32)
            ).astype(bf16)
            at += rows
    if len(refs) > 2 * n + 1:
        mine, other = refs[2 * n][...].astype(f32), refs[2 * n + 1][...].astype(f32)
        first = me_ref[2] == 0
        both = [jnp.where(first, mine, other), jnp.where(first, other, mine)]
        n_rows, w = mine.shape
        line = jnp.concatenate(both + [jnp.zeros((n_rows, width - 2 * w), f32)], axis=1).astype(bf16)
        for z in range(out_ref.shape[1]):
            out_ref[0, z, at : at + n_rows, :] = line


def pair_sum(parts, N, tok, me=None, term=None):
    n = len(parts)
    keeps = [keep for keep, _ in parts]
    got = [other_core(send, N) for _, send in parts]
    R, Z, _, width = keeps[0].shape
    rows = sum(k.size for k in keeps) // (R * Z * width)
    keeps[0] = after(keeps[0], tok)
    ins = keeps + got
    specs = [pl.BlockSpec((1,) + a.shape[1:], lambda i: (i, 0, 0, 0)) for a in ins]
    if term is not None:
        ins += [term, other_core(term, N)]
        specs += [full_spec(term.shape)] * 2
        rows += term.shape[0]
    return run(
        functools.partial(pair_body, n), "pair_sum", (R,), [jnp.zeros((3,), jnp.int32) if me is None else me] + ins, [SMEM] + specs,
        sds((R, Z, rows, width), bf16), pl.BlockSpec((1, Z, rows, width), lambda i: (i, 0, 0, 0)), moved=6 * R * Z * rows * width,
    )


def spots(n, width, shape):
    each = width // shape[1]
    return [(t // each * shape[0], t % each * shape[1]) for t in range(n)], -(-n // each) * shape[0]


def chips_body(term, me_ref, in_ref, *outs):
    R, _, rows, width = in_ref.shape
    rows -= term[0]
    where, _ = spots(2 * R, width, term)
    for k, out in enumerate(outs):
        z = me_ref[0] ^ k
        total = in_ref[0, z, :rows].astype(f32)
        for r in range(1, R):
            total += in_ref[r, z, :rows].astype(f32)
        out[:rows, :] = total.astype(out.dtype)
        if term[0]:
            out[rows:, :] = jnp.zeros((out.shape[0] - rows, width), out.dtype)
            for t, (row, col) in enumerate(where):
                tile = in_ref[t // 2, z, rows : rows + term[0], t % 2 * term[1] : (t % 2 + 1) * term[1]]
                out[rows + row : rows + row + term[0], col : col + term[1]] = tile.astype(out.dtype)


def chips_sum(me, got, tok, term=(0, LANES)):
    R, Z, rows, width = got.shape
    rows += spots(2 * R, width, term)[1] - term[0]
    return once(
        functools.partial(chips_body, term), "chips_sum", (me, after(got, tok)), [SMEM, None],
        [sds((rows, width), f32)] + [sds((rows, width), bf16)] * (Z - 1), moved=2 * got.size + 2 * Z * rows * width,
    )


def total_of(parts, lo, hi, rows=None):
    total = parts[0][:rows, lo:hi].astype(f32)
    for p in parts[1:]:
        total += p[:rows, lo:hi].astype(f32)
    return total


def last_body(n, cuts, G, gc, *refs):
    parts, (out_ref, in_ref, retr_ref, small_ref, turn) = refs[:n], refs[n:]
    rows = parts[0].shape[0]
    out_ref[...] = total_of(parts, *cuts[0])
    for g in range(G):
        for m in range(3):
            lo = cuts[1 + g][0] + m * gc
            in_ref[:, (m * G + g) * gc : (m * G + g + 1) * gc] = total_of(parts, lo, lo + gc)
    retr_ref[...] = total_of(parts, *cuts[1 + G])
    turn[...] = jnp.zeros_like(turn)
    turn[0:rows, :] = total_of(parts, *cuts[2 + G])
    small_ref[...] = turn[...].T[: small_ref.shape[0], :rows]


def last_sum(ins, widths, turned, G, gc, tok):
    rows = ins[0].shape[0]
    cuts = cut_points(widths)
    shapes = [(rows, widths[0]), (rows, 3 * G * gc), (rows, widths[-2]), (turned, rows)]
    return once(
        functools.partial(last_body, len(ins), cuts, G, gc), "last_sum", (after(ins[0], tok), *ins[1:]), [None] * len(ins),
        [sds(s, f32) for s in shapes], scratch=[pltpu.VMEM((LANES, LANES), f32)], moved=12 * rows * cuts[-1][1],
    )


def last_feed_body(n, term, N, me_ref, *refs):
    parts, (down_ref, up_ref, table_ref, held) = refs[:n], refs[n:]
    drows, D = down_ref.shape
    rows = up_ref.shape[0]
    total = total_of(parts, 0, D, 2 * drows)
    down_ref[...] = total[:drows]
    for q in range(drows // rows):
        up_ref[:, q * D : (q + 1) * D] = total[drows + q * rows : drows + (q + 1) * rows]
    where, _ = spots(N, D, term)
    trows = table_ref.shape[0]
    count, half = N * n * term[0], term[0] // 2
    for i, p in enumerate(parts):
        for t, (row, col) in enumerate(where):
            at = (i * N + t) * term[0]
            tile = p[2 * drows + row : 2 * drows + row + term[0], col : col + term[1]]
            held[at : at + term[0], :] = tile.astype(f32)
    held[count:, :] = jnp.zeros((term[0], term[1]), f32)
    below = held[half : half + count, :]
    ids = (below[:, 0:1] * 256.0 + below[:, 1:2]).astype(jnp.int32) - (me_ref[0] * N + 2 * me_ref[1] + me_ref[2]) * trows
    line = lax.broadcasted_iota(jnp.int32, (count, trows), 0) % term[0]
    picker = (lax.broadcasted_iota(jnp.int32, (count, trows), 1) == ids) & (line < half)
    table_ref[...] = dot(picker.astype(bf16), held[0:count, :].astype(bf16), 0, 0)


def last_feed(me, ins, F, tok, trows, term, N):
    D = ins[0].shape[1]
    both = ins[0].shape[0] - spots(N, D, term)[1]
    return once(
        functools.partial(last_feed_body, len(ins), term, N), "last_feed", (me, after(ins[0], tok), *ins[1:]), [SMEM] + [None] * len(ins),
        [sds((both // 2, D), f32), sds((both // 2 * D // F, F), f32), sds((trows, term[1]), f32)], moved=12 * both * D,
        scratch=[pltpu.VMEM(((N * len(ins) + 1) * term[0], term[1]), f32)],
    )


def along_dp_sums(sums):
    return [sums[0]] + [lax.ppermute(sums[k], "dp", pairs(len(sums), k)) for k in range(1, len(sums))]


def column(ref, n):
    line = lax.broadcasted_iota(jnp.int32, (n, 1), 0)
    total = jnp.zeros((n, 1), ref.dtype)
    for i in range(n):
        total = jnp.where(line == i, ref[i], total)
    return total


def lookup_body(found, me_ref, sg_ref, r_ref, *refs):
    chosen_ref, back_ref, lead_ref = refs[found:]
    seqs = sg_ref.shape[0]
    chosen_ref[...] = jnp.zeros_like(chosen_ref)
    if found == 2:
        total = jnp.zeros((2 * seqs, r_ref.shape[1]), f32)
        for ref in refs[:2]:
            for r in range(ref.shape[0]):
                total += ref[r, 0, ref.shape[2] - 2 * seqs :].astype(f32)
        chosen_ref[0:seqs, :] = jnp.where(me_ref[2] == 0, total[:seqs], total[seqs:])
    else:
        chosen_ref[0:seqs, :] = refs[0][...].astype(f32)
    back_ref[...] = jnp.zeros_like(back_ref)
    back_ref[0:seqs, :] = column(sg_ref, seqs) * chosen_ref[0:seqs, :]
    lead = dot(back_ref[...].astype(bf16), r_ref[...], 1, 1)
    for s in range(seqs):
        lead_ref[s] = lead[s : s + 1, :]


def lookup(me, sg, wide, F, D, width, found):
    seqs = sg.shape[0]
    specs = [None]
    if len(found) == 2:
        specs = [pl.BlockSpec((a.shape[0], 1, a.shape[2], width), lambda i: (0, 0, 0, 0)) for a in found]
    return once(
        functools.partial(lookup_body, len(found)), "lookup", (me, sg, wide, *found),
        [SMEM, SMEM, pl.BlockSpec((D, width), lambda i: (0, (F + D) // width))] + specs,
        [sds((16, width), f32), sds((16, width), f32), sds((seqs, 1, D), f32)], moved=4 * D * width,
    )


def score_body(top_ref, r_ref, chosen_ref, back_ref, sg_ref, id_ref, score_ref, retr_ref, term_ref, held):
    seqs = top_ref.shape[0]
    width = r_ref.shape[1]
    held[...] = jnp.zeros_like(held)
    for s in range(seqs):
        held[s : s + 1, :] = top_ref[s]
    leading = held[...].astype(bf16)
    projected = dot(leading, r_ref[...]).astype(bf16).astype(f32)[:seqs]
    score_ref[...] = jnp.sum(projected * chosen_ref[0:seqs, :], axis=-1, keepdims=True)
    retr_ref[...] = dot(leading, back_ref[...].astype(bf16), 0, 0)
    lane = lax.broadcasted_iota(jnp.int32, (seqs, width), 1)
    index = column(id_ref, seqs)
    high, low = index // 256, index % 256
    ids = jnp.where(lane == 0, high, jnp.where(lane == 1, low, 0)).astype(f32)
    term_ref[...] = jnp.concatenate([column(sg_ref, seqs) * projected, ids], axis=0).astype(bf16)


def score(top, wide, F, chosen, back, sg, index):
    seqs, _, D = top.shape
    width = chosen.shape[1]
    return once(
        score_body, "score", (top, wide, chosen, back, sg, index),
        [None, pl.BlockSpec((D, width), lambda i: (0, (F + D) // width))] + [None] * 2 + [SMEM] * 2,
        [sds((seqs, 1), f32), sds((D, width), f32), sds((2 * seqs, width), bf16)],
        scratch=[pltpu.VMEM((16, D), f32)], moved=8 * D * width,
    )


def bias_row_body(Z, N, Q, s_ref, v_ref, out_ref):
    D = s_ref.shape[0]
    rows = D // (Z * N)
    lane = lax.broadcasted_iota(jnp.int32, (Z * N, rows, LANES), 2)
    whole = s_ref[...].astype(f32).reshape(Z * N, rows, LANES)
    parts = [jnp.where(lane == UB + q, whole, 0.0).reshape(Z * N, 1, rows, LANES) for q in range(Q)]
    turned = jnp.concatenate(parts, axis=1).reshape(Q * D, LANES).T
    out_ref[...] = jnp.sum(turned, axis=0, keepdims=True)


def bias_row(small, vec, Z, N, Q):
    D = small.shape[0]
    rows = D // (Z * N)
    if rows % 8:
        return vec[UB : UB + Q].reshape(Q, Z * N, rows).transpose(1, 0, 2).reshape(1, Q * D)
    return once(
        functools.partial(bias_row_body, Z, N, Q), "bias_row", (small, vec), [None] * 2, [sds((1, Q * D), f32)],
        moved=8 * Q * D * LANES,
    )[0]


def local(
    Z, N, tokens, input_weight, query_bias, value_bias, output_weight, output_bias, first_gain, first_shift,
    up_weight, up_bias, down_weight, down_bias, second_gain, second_shift, retriever_weight, document_table,
    document_index, output_grad, score_grad,
):
    both = ("dp", "fsdp")
    T, D = tokens.shape
    R = N // 2
    F = up_weight.shape[1]
    Rw = retriever_weight.shape[1]
    seqs = document_index.shape[0]
    L = T // seqs
    per = 2 - seqs % 2
    gc = 4 * HEAD_DIM
    G = D // gc
    Q = F // D
    trows, rows = document_table.shape[0], input_weight.shape[0]
    f = lax.axis_index("fsdp")
    me = jnp.stack([lax.axis_index("dp"), f // 2, f % 2]).astype(jnp.int32)

    vectors = [
        v.reshape(1, -1)
        for v in (query_bias, value_bias, output_bias, first_gain, first_shift, down_bias, second_gain, second_shift, up_bias)
    ]
    head, rest, wide = pack(document_index, input_weight, output_weight, retriever_weight, up_weight, vectors, gc)
    wide = lax.all_gather(wide, both, axis=0, tiled=True)
    head = repeat(along_dp([head] * Z), R)
    rest = along_dp([after(rest, head)] * Z)
    head = between_chips(head, N)
    win_one, small, vec = place(me, [head, other_core(head, N)], Z, [3 * gc, LANES], turned=16)
    ub = bias_row(small, vec, Z, N, Q)
    rest = repeat([after(p, ub) for p in rest], R)
    if rows % 8:
        found, asked = [lax.all_gather(document_table, both, axis=0, tiled=True)[document_index]], ()
    else:
        asked = along_dp(ask(me, small, after(document_table, rest), seqs, Z, N, UB + Q))
    wd = along_dp([after(down_weight, rest)] * Z)
    rest = between_chips(rest, N)

    held = attend(after(tokens, ub), win_one, vec, seqs, G, 0)
    wd = repeat([after(w, held[2]) for w in wd], R, asked)
    rest = after(rest, wd)
    (win_two,) = place(me, [rest, other_core(rest, N)], Z, [3 * gc * (G - 1)])
    wd = between_chips(wd, N)
    qkv, soft, ctx = attend(tokens, win_two, vec, seqs, G, 1, held)
    wd = after(wd, ctx)
    n, inv, first, act, slope = up(ctx, tokens, vec, wide, ub, L, L // 2)
    wd = [wd, other_core(wd, N)]
    if rows % 8 == 0:
        found = wd
    (wd,) = place(me, [after(wd[0], first), wd[1]], Z, [D], rows=down_weight.shape[0])
    chosen, back_projected, lead = lookup(me, score_grad, after(wide, first), F, D, Rw, found)
    final, top, two, feed, inner, gsg, gss, gdb, gub = down(first, act, slope, wd, vec, output_grad, lead, seqs, per)
    scores, retriever_back, term = score(top, wide, F, chosen, back_projected, score_grad, document_index)
    down_parts = down_grad(me, Z, N, act, feed)
    up_parts = grads(me, Z, N, "up_grad", [after(first, *down_parts), inner], [([(0, None)], (1, None))], tile=D)
    feed_sums = pair_sum([down_parts, up_parts], N, up_parts[0], me, term)
    one, att, bctx, gfg, gfs, gob = mid(after(two, feed_sums), inner, wide, n, inv, vec, per * L, L)
    mixed, gq, gv = attend_back(qkv, soft, ctx, after(bctx, feed_sums), seqs)
    parts = grads(
        me, Z, N, "mix_grad", [ctx, att, tokens, mixed],
        [([(0, g) for g in range(G)], (1, None))] + [([(2, None)], (3, g)) for g in range(G)],
        retr=retriever_back, vectors=[gq, gv, gob, gfg, gfs, gdb, gsg, gss, gub],
    )
    mix_pair = pair_sum([parts], N, parts[0])
    feed_sums = between_chips(feed_sums, N)
    mix_sums = between_chips(after(mix_pair, feed_sums), N)
    feed_sums = chips_sum(me, feed_sums, mix_pair, term.shape)
    back_tokens = tokens_back(after(one, feed_sums[0]), mixed, [win_one, win_two], L)
    mix_sums = chips_sum(me, mix_sums, back_tokens)
    down_back, up_back, table_back = last_feed(me, along_dp_sums(feed_sums), F, mix_sums[0], trows, term.shape, N)
    output_back, input_back, retriever_back, small = last_sum(
        along_dp_sums(mix_sums), [D] + [3 * gc] * G + [Rw, LANES], 16, G, gc, down_back
    )
    ub_back = small[8 : 8 + Q].reshape(-1)
    return (
        final, scores.reshape(seqs), back_tokens, input_back, small[0], small[1], output_back, small[2], small[3], small[4],
        up_back, ub_back, down_back, small[5], small[6], small[7], retriever_back, table_back,
    )


def solution(mesh):
    both = ("dp", "fsdp")
    mat, vec = P(both, None), P(both)
    in_specs = (mat, mat, vec, vec, mat, vec, vec, vec, mat, vec, mat, vec, vec, vec, mat, mat, vec, mat, vec)
    out_specs = (mat, vec, mat, mat, vec, vec, mat, vec, vec, vec, mat, vec, mat, vec, vec, vec, mat, mat)
    body = functools.partial(local, mesh.shape["dp"], mesh.shape["fsdp"])
    return jax.shard_map(body, mesh=mesh, in_specs=in_specs, out_specs=out_specs, check_vma=False)
```

```python
import functools
import math
import jax
import jax.numpy as jnp
from jax import lax
from jax.experimental import pallas as pl
from jax.experimental.pallas import tpu as pltpu
from jax.sharding import PartitionSpec as P

HEAD_DIM = 64
EPS = 1e-12
ROOM = {"tokens_back": 28, "chips_sum": 28, "last_sum": 28, "last_feed": 28, "pair_sum": 28, "lookup": 28, "score": 28, "place": 40, "repeat": 40, "ask": 28, "bias_row": 28}
QB, VB, OB, FG, FS, DB, SG, SS, UB = range(9)
bf16, f32 = jnp.bfloat16, jnp.float32


def dot(a, b, ca=1, cb=0):
    return lax.dot_general(a, b, (((ca,), (cb,)), ((), ())), preferred_element_type=f32)


def rows_spec(rows, cols):
    return pl.BlockSpec((rows, cols), lambda i: (i, 0))


def full_spec(shape):
    return pl.BlockSpec(shape, lambda *_: (0,) * len(shape))


def head_mask(rows, cols, h):
    lane = lax.broadcasted_iota(jnp.int32, (rows, cols), 1)
    return (lane >= h * HEAD_DIM) & (lane < (h + 1) * HEAD_DIM)


def run(body, name, grid, ins, in_specs, outs, out_specs, scratch=(), flops=0, moved=0, alias=None):
    return pl.pallas_call(
        body,
        name=name,
        grid=grid,
        in_specs=in_specs,
        out_specs=out_specs,
        out_shape=outs,
        scratch_shapes=list(scratch),
        cost_estimate=estimate(flops, moved),
        input_output_aliases=alias or {},
        compiler_params=pltpu.CompilerParams(vmem_limit_bytes=ROOM.get(name, 60) * 2**20),
    )(*ins)


def estimate(flops, moved):
    return pl.CostEstimate(flops=int(flops), bytes_accessed=int(moved), transcendentals=0)


def sds(shape, dtype):
    return jax.ShapeDtypeStruct(shape, dtype)


def attend_body(x_ref, w_ref, v_ref, *refs):
    qkv_ref, soft_ref, ctx_ref = refs[-3:]
    length = x_ref.shape[0]
    gc = ctx_ref.shape[1]
    mixed = dot(x_ref[...], w_ref[...])
    q = (mixed[:, :gc] + v_ref[QB : QB + 1, :]).astype(bf16)
    k = mixed[:, gc : 2 * gc].astype(bf16)
    v = (mixed[:, 2 * gc :] + v_ref[VB : VB + 1, :]).astype(bf16)
    qkv_ref[:, :gc] = q
    qkv_ref[:, gc : 2 * gc] = k
    qkv_ref[:, 2 * gc :] = v
    qs = q * bf16(HEAD_DIM ** -0.5)
    zero = jnp.zeros((), bf16)
    total = jnp.zeros((length, gc), f32)
    for h in range(gc // HEAD_DIM):
        mask = head_mask(length, gc, h)
        s = dot(jnp.where(mask, qs, zero), k, 1, 1)
        peak = jnp.max(s, axis=-1, keepdims=True)
        e = jnp.exp(s - peak)
        norm = 1.0 / jnp.sum(e, axis=-1, keepdims=True)
        p = (e * norm).astype(bf16)
        soft_ref[h] = p
        total += dot(p, jnp.where(mask, v, zero))
    ctx_ref[...] = total.astype(bf16)


def attend(x, w, vec, seqs, groups, at, into=()):
    T, D = x.shape
    gc = D // groups
    hg = gc // HEAD_DIM
    L = T // seqs
    count = w.shape[1] // (3 * gc)
    ins = (x, w, vec, *into)
    return run(
        attend_body, "attend", (count, seqs), ins,
        [
            pl.BlockSpec((L, D), lambda g, s: (s, 0)), pl.BlockSpec((D, 3 * gc), lambda g, s: (0, g)),
            pl.BlockSpec((vec.shape[0], gc), lambda g, s: (0, at + g)),
        ] + [pl.BlockSpec(memory_space=pl.ANY)] * len(into),
        [sds((groups, T, 3 * gc), bf16), sds((groups, hg, T, L), bf16), sds((groups, T, gc), bf16)],
        [
            pl.BlockSpec((None, L, 3 * gc), lambda g, s: (at + g, s, 0)),
            pl.BlockSpec((None, hg, L, L), lambda g, s: (at + g, 0, s, 0)),
            pl.BlockSpec((None, L, gc), lambda g, s: (at + g, s, 0)),
        ],
        flops=count * (2 * T * D * 3 * gc + 16 * T * L * gc), moved=2 * (T * D + w.size + count * (4 * T * gc + hg * T * L)),
        alias={3 + i: i for i in range(len(into))},
    )


def norm_rows(h):
    mean = jnp.mean(h, axis=-1, keepdims=True)
    c = h - mean
    var = jnp.mean(c * c, axis=-1, keepdims=True)
    inv = lax.rsqrt(var + EPS)
    return c * inv, inv


def norm_rows_back(cot, n, inv, gain):
    scaled = cot * gain
    return inv * (scaled - jnp.mean(scaled, axis=-1, keepdims=True) - n * jnp.mean(scaled * n, axis=-1, keepdims=True))


def in_turn(blocks, first, then):
    held = first(blocks[0])
    for i, block in enumerate(blocks):
        ahead = first(blocks[i + 1]) if i + 1 < len(blocks) else None
        then(i, block, held)
        held = ahead


def blocks_of(rows, size):
    return [slice(at, at + size) for at in range(0, rows, size)]


def up_body(size, step, ctx_ref, x_ref, wo_ref, v_ref, wu_ref, ub_ref, n_ref, inv_ref, first_ref, act_ref, slope_ref):
    G, rows, gc = ctx_ref.shape

    def attended(block):
        hidden = x_ref[block].astype(f32) + v_ref[OB : OB + 1, :]
        for g in range(G):
            hidden += dot(ctx_ref[g, block], wo_ref[g * gc : (g + 1) * gc, :])
        return hidden

    def rest(_, block, hidden):
        n, inv = norm_rows(hidden)
        n_ref[block] = n
        inv_ref[block] = inv
        first = (n * v_ref[FG : FG + 1, :] + v_ref[FS : FS + 1, :]).astype(bf16)
        first_ref[block] = first
        ff = wu_ref.shape[1]
        for at in range(0, ff, step):
            cols = slice(at, at + step)
            u = dot(first, wu_ref[:, cols]) + ub_ref[:, cols]
            phi = 0.5 + 0.5 * lax.erf(u * math.sqrt(0.5))
            act_ref[block, cols] = (u * phi).astype(bf16)
            bell = jnp.exp2(u * u * (-0.5 / math.log(2)) - 0.5 * math.log2(2 * math.pi))
            slope_ref[block, cols] = (phi + u * bell).astype(bf16)

    in_turn(blocks_of(rows, size), attended, rest)


def out_spec(D, F):
    return pl.BlockSpec((D, D), lambda i: (0, F // D))


def up(ctx, x, vec, wide, ub, rows, size, step=512):
    T, D = x.shape
    F = ub.shape[1]
    return run(
        functools.partial(up_body, size, step), "up", (T // rows,), (ctx, x, wide, vec, wide, ub),
        [pl.BlockSpec((ctx.shape[0], rows, ctx.shape[2]), lambda i: (0, i, 0)), rows_spec(rows, D)] + [out_spec(D, F), full_spec(vec.shape), full_spec((D, F)), full_spec(ub.shape)],
        [sds((T, D), f32), sds((T, 1), f32), sds((T, D), bf16), sds((T, F), bf16), sds((T, F), bf16)],
        [rows_spec(rows, D), rows_spec(rows, 1), rows_spec(rows, D), rows_spec(rows, F), rows_spec(rows, F)],
        flops=2 * T * D * (D + F), moved=T * D * 10 + 4 * T * F + 2 * D * (D + F),
    )


def add_rows(ref, value, cols=slice(None), axis=0):
    held = jnp.where(pl.program_id(axis) == 0, 0.0, ref[:, cols])
    ref[:, cols] = held + jnp.sum(value, axis=0, keepdims=True)


def down_body(size, step, first_ref, act_ref, slope_ref, w_ref, v_ref, og_ref, lead_ref,
              out_ref, top_ref, two_ref, feed_ref, inner_ref, gg_ref, gs_ref, gb_ref, gub_ref):
    gain = v_ref[SG : SG + 1, :]
    ff = w_ref.shape[0]
    sums = {}

    def count(name, value):
        total = jnp.sum(value, axis=0, keepdims=True)
        sums[name] = sums[name] + total if name in sums else total

    def fed(block):
        return first_ref[block].astype(f32) + v_ref[DB : DB + 1, :] + dot(act_ref[block], w_ref[...])

    def rest(i, block, hidden):
        n, inv = norm_rows(hidden)
        out = (n * gain + v_ref[SS : SS + 1, :]).astype(bf16)
        out_ref[block] = out
        top_ref[i] = out[0:16, :].astype(f32)[0:1, :]
        row = lax.broadcasted_iota(jnp.int32, (size, 1), 0)
        cot = og_ref[block].astype(f32) + jnp.where(row == 0, lead_ref[i], 0.0)
        count("gain", cot * n)
        count("shift", cot)
        two = norm_rows_back(cot, n, inv, gain)
        two_ref[block] = two
        feed = two.astype(bf16)
        feed_ref[block] = feed
        count("bias", feed.astype(f32))
        for at in range(0, ff, step):
            cols = slice(at, at + step)
            inner = (dot(feed, w_ref[cols, :], 1, 1) * slope_ref[block, cols].astype(f32)).astype(bf16)
            inner_ref[block, cols] = inner
            count(at, inner.astype(f32))

    in_turn(blocks_of(first_ref.shape[0], size), fed, rest)
    add_rows(gg_ref, sums["gain"])
    add_rows(gs_ref, sums["shift"])
    add_rows(gb_ref, sums["bias"])
    for at in range(0, ff, step):
        add_rows(gub_ref, sums[at], slice(at, at + step))


def down(first, act, slope, w, vec, og, lead, seqs, per, step=512):
    T, D = first.shape
    F = act.shape[1]
    L = T // seqs
    rows = per * L
    each = pl.BlockSpec((per, 1, D), lambda i: (i, 0, 0))
    return run(
        functools.partial(down_body, L, step), "down", (seqs // per,), (first, act, slope, w, vec, og, lead),
        [rows_spec(rows, D), rows_spec(rows, F), rows_spec(rows, F), full_spec((F, D)), full_spec(vec.shape), rows_spec(rows, D), each],
        [sds((T, D), bf16), sds((seqs, 1, D), f32), sds((T, D), f32), sds((T, D), bf16), sds((T, F), bf16),
         sds((1, D), f32), sds((1, D), f32), sds((1, D), f32), sds((1, F), f32)],
        [rows_spec(rows, D), each, rows_spec(rows, D), rows_spec(rows, D), rows_spec(rows, F)]
        + [full_spec((1, D))] * 3 + [full_spec((1, F))],
        flops=4 * T * D * F, moved=6 * T * F + 12 * T * D + 2 * F * D,
    )


def mid_body(size, two_ref, inner_ref, wu_ref, n_ref, inv_ref, v_ref, wo_ref,
             one_ref, att_ref, bctx_ref, gg_ref, gs_ref, gob_ref):
    sums = {}

    def count(name, value):
        total = jnp.sum(value, axis=0, keepdims=True)
        sums[name] = sums[name] + total if name in sums else total

    def back(block):
        return two_ref[block] + dot(inner_ref[block], wu_ref[...], 1, 1)

    def rest(_, block, cot):
        n = n_ref[block]
        count("gain", cot * n)
        count("shift", cot)
        one = norm_rows_back(cot, n, inv_ref[block], v_ref[FG : FG + 1, :])
        one_ref[block] = one
        att = one.astype(bf16)
        att_ref[block] = att
        count("bias", att.astype(f32))
        bctx_ref[block] = dot(att, wo_ref[...], 1, 1).astype(bf16)

    in_turn(blocks_of(two_ref.shape[0], size), back, rest)
    add_rows(gg_ref, sums["gain"])
    add_rows(gs_ref, sums["shift"])
    add_rows(gob_ref, sums["bias"])


def mid(two, inner, wide, n, inv, vec, rows, size):
    T, D = two.shape
    F = inner.shape[1]
    return run(
        functools.partial(mid_body, size), "mid", (T // rows,), (two, inner, wide, n, inv, vec, wide),
        [rows_spec(rows, D), rows_spec(rows, F), full_spec((D, F)), rows_spec(rows, D), rows_spec(rows, 1), full_spec(vec.shape), out_spec(D, F)],
        [sds((T, D), f32), sds((T, D), bf16), sds((T, D), bf16)] + [sds((1, D), f32)] * 3,
        [rows_spec(rows, D)] * 3 + [full_spec((1, D))] * 3,
        flops=2 * T * D * (F + D), moved=2 * T * F + 16 * T * D + 2 * D * (D + F),
    )


def attend_back_body(qkv_ref, soft_ref, ctx_ref, bctx_ref, out_ref, gq_ref, gv_ref):
    length, gc = ctx_ref.shape
    q = qkv_ref[:, :gc]
    k = qkv_ref[:, gc : 2 * gc]
    v = qkv_ref[:, 2 * gc :]
    do = bctx_ref[...]
    prod = do.astype(f32) * ctx_ref[...].astype(f32)
    zero = jnp.zeros((), bf16)
    dq = jnp.zeros((length, gc), f32)
    dk = jnp.zeros((length, gc), f32)
    dv = jnp.zeros((length, gc), f32)
    for h in range(gc // HEAD_DIM):
        mask = head_mask(length, gc, h)
        p = soft_ref[h]
        do_h = jnp.where(mask, do, zero)
        dp = dot(do_h, v, 1, 1)
        delta = jnp.sum(jnp.where(mask, prod, 0.0), axis=-1, keepdims=True)
        ds = (p.astype(f32) * (dp - delta)).astype(bf16)
        dv += dot(p, do_h, 0, 0)
        dq += dot(ds, jnp.where(mask, k, zero))
        dk += dot(ds, jnp.where(mask, q, zero), 0, 0)
    scale = HEAD_DIM ** -0.5
    dq = (dq * scale).astype(bf16)
    dv = dv.astype(bf16)
    out_ref[:, :gc] = dq
    out_ref[:, gc : 2 * gc] = (dk * scale).astype(bf16)
    out_ref[:, 2 * gc :] = dv
    add_rows(gq_ref, dq.astype(f32), axis=1)
    add_rows(gv_ref, dv.astype(f32), axis=1)


def attend_back(qkv, soft, ctx, bctx, seqs):
    G, T, gc = ctx.shape
    hg = gc // HEAD_DIM
    L = T // seqs
    line = lambda w: pl.BlockSpec((None, L, w), lambda g, s: (g, s, 0))
    row = pl.BlockSpec((1, gc), lambda g, s: (0, g))
    return run(
        attend_back_body, "attend_back", (G, seqs), (qkv, soft, ctx, bctx),
        [
            line(3 * gc), pl.BlockSpec((None, hg, L, L), lambda g, s: (g, 0, s, 0)), line(gc),
            pl.BlockSpec((L, gc), lambda g, s: (s, g)),
        ],
        [sds((G, T, 3 * gc), bf16), sds((1, G * gc), f32), sds((1, G * gc), f32)], [line(3 * gc), row, row],
        flops=G * 32 * T * L * gc, moved=2 * G * (8 * T * gc + hg * T * L),
    )


def tokens_back_body(one_ref, mixed_ref, *refs):
    total = one_ref[...]
    width = mixed_ref.shape[2]
    g = 0
    for w_ref in refs[:-1]:
        for at in range(0, w_ref.shape[1], width):
            total += dot(mixed_ref[g], w_ref[:, at : at + width], 1, 1)
            g += 1
    refs[-1][...] = total.astype(bf16)


def tokens_back(one, mixed, ws, rows):
    T, D = one.shape
    G, _, width = mixed.shape
    return run(
        tokens_back_body, "tokens_back", (T // rows,), (one, mixed, *ws),
        [rows_spec(rows, D), pl.BlockSpec((G, rows, width), lambda i: (0, i, 0))] + [full_spec(w.shape) for w in ws],
        sds((T, D), bf16), rows_spec(rows, D), flops=2 * T * D * G * width, moved=T * D * 12,
    )


def after(x, *deps):
    return lax.optimization_barrier((x,) + deps)[0]


ANY = pl.BlockSpec(memory_space=pl.ANY)
SMEM = pl.BlockSpec(memory_space=pltpu.SMEM)
LANES = 128


def once(body, name, ins, in_specs, outs, scratch=(), moved=0, flops=0):
    specs = [full_spec(a.shape) if spec is None else spec for a, spec in zip(ins, in_specs)]
    return run(body, name, (1,), ins, specs, outs, [full_spec(o.shape) for o in outs], scratch, flops, moved)


def cut_points(widths):
    cuts, at = [], 0
    for w in widths:
        cuts.append((at, at + w))
        at += w
    return cuts


def pack_body(D, gc, nvec, *refs):
    id_ref, w_ref, o_ref, r_ref, u_ref = refs[:5]
    head_ref, rest_ref, up_ref, held = refs[5 + nvec :]
    G = D // gc
    rows = w_ref.shape[0]
    held[...] = jnp.zeros_like(held)
    row = 0
    for v_ref in refs[5 : 5 + nvec]:
        v = v_ref[...].astype(f32)
        for at in range(0, v.shape[1], rows):
            held[row : row + 1, 0:rows] = v[:, at : at + rows]
            row += 1
    lane = lax.broadcasted_iota(jnp.int32, (1, LANES), 1)
    ids = jnp.zeros((1, LANES), jnp.int32)
    seqs = id_ref.shape[0]
    for i in range(seqs):
        ids = jnp.where(lane == i, id_ref[i] // 256, jnp.where(lane == seqs + i, id_ref[i] % 256, ids))
    held[row : row + 1, :] = ids.astype(f32)
    turned = held[...].T
    for m in range(3):
        head_ref[:, m * gc : (m + 1) * gc] = w_ref[:, m * D : m * D + gc]
    head_ref[:, 3 * gc :] = turned[:rows, :].astype(bf16)
    at = 0
    for g in range(1, G):
        for m in range(3):
            rest_ref[:, at : at + gc] = w_ref[:, m * D + g * gc : m * D + (g + 1) * gc]
            at += gc
    F = u_ref.shape[1]
    up_ref[:, :F] = u_ref[...]
    up_ref[:, F : F + D] = o_ref[...]
    up_ref[:, F + D :] = r_ref[...]


def pack(ids, w, o, r, u, vectors, gc):
    rows, D = o.shape
    head = 3 * gc + LANES
    rest = 3 * D - 3 * gc
    ups = u.shape[1] + D + r.shape[1]
    return once(
        functools.partial(pack_body, D, gc, len(vectors)), "pack", (ids, w, o, r, u, *vectors), [SMEM] + [None] * (4 + len(vectors)),
        [sds((rows, head), bf16), sds((rows, rest), bf16), sds((rows, ups), bf16)],
        scratch=[pltpu.VMEM((LANES, LANES), f32)], moved=4 * rows * (head + rest + ups),
    )


def pairs(n, flip):
    return [(i, i ^ flip) for i in range(n)]


def along_dp(blocks):
    return [blocks[0]] + [lax.ppermute(b, "dp", pairs(len(blocks), k)) for k, b in enumerate(blocks) if k]


def between_chips(blocks, N):
    return lax.all_to_all(blocks, "fsdp", 0, 0, axis_index_groups=[list(range(c, N, 2)) for c in range(2)], tiled=True)


def other_core(blocks, N):
    return lax.ppermute(blocks, "fsdp", pairs(N, 1))


def repeat_body(n, *refs):
    out, blocks, tiles = refs[-1], refs[:n], refs[n:-1]
    rows, width = blocks[0].shape
    for r in range(out.shape[0]):
        for k, ref in enumerate(blocks):
            out[r, k, :rows] = ref[...]
        if tiles:
            w = tiles[0].shape[1] // out.shape[0]
            total = tiles[0][:, r * w : (r + 1) * w].astype(f32)
            for ref in tiles[1:]:
                total += ref[:, r * w : (r + 1) * w].astype(f32)
            blank = jnp.zeros((total.shape[0], width - w), f32)
            out[r, 0, rows:] = jnp.concatenate([total, blank], axis=1).astype(bf16)
            for k in range(1, n):
                out[r, k, rows:] = jnp.zeros((total.shape[0], width), bf16)


def repeat(blocks, R, tiles=()):
    n = len(blocks)
    rows, width = blocks[0].shape
    rows += tiles[0].shape[0] if tiles else 0
    return once(
        functools.partial(repeat_body, n), "repeat", [*blocks, *tiles], [None] * (n + len(tiles)),
        [sds((R, n, rows, width), bf16)], moved=2 * (R + 1) * n * rows * width,
    )[0]


def ask_body(seqs, Z, R, at, me_ref, s_ref, t_ref, *refs):
    outs, below, held = refs[:Z], refs[Z], refs[Z + 1]
    D, trows = s_ref.shape[0], t_ref.shape[0]
    rows = D // (Z * R * 2)
    flat = s_ref[...].astype(f32)
    below[0:D, :] = flat
    below[D:, :] = jnp.zeros((below.shape[0] - D, LANES), f32)
    ids = flat[:, at : at + 1] * 256.0 + below[seqs : seqs + D, at : at + 1]
    ids = ids.astype(jnp.int32) - ((me_ref[0] * R + me_ref[1]) * 2 + me_ref[2]) * trows
    line = lax.broadcasted_iota(jnp.int32, (D, trows), 0) % rows
    picker = (lax.broadcasted_iota(jnp.int32, (D, trows), 1) == ids) & (line < seqs)
    held[...] = dot(picker.astype(bf16), t_ref[...]).reshape(held.shape)
    for k, out in enumerate(outs):
        z = me_ref[0] ^ k
        tiles = [jnp.concatenate([held[z, r, 0, 0:seqs], held[z, r, 1, 0:seqs]], axis=0) for r in range(R)]
        out[...] = jnp.concatenate(tiles, axis=1).astype(bf16)


def ask(me, small, table, seqs, Z, N, at):
    D = small.shape[0]
    R, width = N // 2, table.shape[1]
    return once(
        functools.partial(ask_body, seqs, Z, R, at), "ask", (me, small, table), [SMEM, None, None],
        [sds((2 * seqs, R * width), bf16)] * Z,
        scratch=[pltpu.VMEM((D + 8, LANES), f32), pltpu.VMEM((Z, R, 2, D // (Z * N), width), f32)],
        flops=2 * D * width * table.shape[0], moved=2 * table.size,
    )


def place_body(n, cuts, turned, me_ref, *refs):
    pieces = refs[:n]
    outs = refs[n : n + len(cuts)]
    vec_ref = refs[n + len(cuts)] if turned else None
    held = refs[n + len(cuts) + turned : n + 2 * len(cuts) + turned]
    flat = refs[-3] if turned else None
    in_sem, out_sem = refs[-2:]
    Z = held[0].shape[0]
    copies = []
    for k in range(Z):
        for other in range(2):
            z = me_ref[0] ^ k
            for c, (lo, hi) in enumerate(cuts):
                copy = pltpu.make_async_copy(
                    pieces[other].at[:, k, 0 : held[c].shape[3], lo:hi], held[c].at[z, :, me_ref[2] ^ other], in_sem.at[len(copies)]
                )
                copies.append((copy, k))
    for copy, _ in copies:
        copy.start()
    last = []
    for k in range(Z):
        for copy, slot in copies:
            if slot == k:
                copy.wait()
        for c in range(len(cuts)):
            z = me_ref[0] ^ k
            last.append(pltpu.make_async_copy(held[c].at[z], outs[c].at[z], out_sem.at[k * len(cuts) + c]))
            last[-1].start()
    if turned:
        for z in range(Z):
            for r in range(held[-1].shape[1]):
                for c in range(2):
                    flat[z, r, c] = held[-1][z, r, c].astype(f32)
        vec_ref[...] = flat[...].reshape(vec_ref.shape[1], LANES).T[: vec_ref.shape[0]]
    for copy in last:
        copy.wait()


def place(me, pieces, Z, widths, turned=0, rows=None):
    n = len(pieces)
    R, rows = pieces[0].shape[0], rows or pieces[0].shape[-2]
    cuts = cut_points(widths)
    if turned and rows % 8:
        outs = place(me, pieces, Z, widths)
        return outs + [outs[-1][:, :turned].T.astype(f32)]
    shapes = [(Z, R, 2, rows, w) for w in widths]
    total = 2 * Z * R * rows
    outs = run(
        functools.partial(place_body, n, cuts, 1 if turned else 0), "place", (1,), (me, *pieces), [SMEM] + [ANY] * n,
        [sds(s, bf16) for s in shapes] + ([sds((turned, total), f32)] if turned else []),
        [ANY] * len(cuts) + ([full_spec((turned, total))] if turned else []),
        scratch=[pltpu.VMEM(s, bf16) for s in shapes] + ([pltpu.VMEM(shapes[-1], f32)] if turned else [])
        + [pltpu.SemaphoreType.DMA((2 * Z * len(cuts),)), pltpu.SemaphoreType.DMA((Z * len(cuts),))],
        moved=4 * total * cuts[-1][1],
    )
    return [o.reshape(total, o.shape[-1]) for o in outs[: len(cuts)]] + list(outs[len(cuts) :])


def hand_out(me_ref, part, Z, R, keep_ref, send_ref, cols=slice(None)):
    rows = part.shape[0] // (Z * R * 2)
    part = part.reshape(Z, R, 2, rows, part.shape[1])
    first = me_ref[2] == 0
    for z in range(Z):
        for r in range(R):
            one, two = part[z, r, 0], part[z, r, 1]
            keep_ref[r, z, :, cols] = jnp.where(first, one, two).astype(bf16)
            send_ref[r, z, :, cols] = jnp.where(first, two, one).astype(bf16)


def grads_body(plan, nvec, has_retr, Z, R, me_ref, *refs):
    at_out = len(refs) - 2 - (2 if nvec else 0)
    keep_ref, send_ref = refs[at_out : at_out + 2]
    col = 0

    def give(part):
        nonlocal col
        hand_out(me_ref, part, Z, R, keep_ref, send_ref, slice(col, col + part.shape[1]))
        col += part.shape[1]

    def read(spot):
        return refs[spot[0]][...] if spot[1] is None else refs[spot[0]][spot[1]]

    for lefts, right in plan:
        y = read(right)
        parts = [dot(read(left), y, 0, 0) for left in lefts]
        give(parts[0] if len(parts) == 1 else jnp.concatenate(parts, axis=0))
    at = at_out - nvec
    if has_retr:
        give(refs[at - 1][...])
    if nvec:
        turn = refs[-1]
        D = turn.shape[1]
        rows = D // (Z * R * 2)
        turn[...] = jnp.zeros_like(turn)
        row, lane = 0, 0
        for r in refs[at:at_out]:
            w = r.shape[1]
            if w <= D:
                turn[row : row + 1, lane : lane + w] = r[...]
                lane += w
                if lane == D:
                    row, lane = row + 1, 0
        total = turn[...].T
        r = refs[at_out - 1]
        if r.shape[1] > D:
            Q = r.shape[1] // D
            wide = refs[-2]
            wide[...] = jnp.zeros_like(wide)
            place_of = lax.broadcasted_iota(jnp.int32, r.shape, 1) % (Q * rows) // rows
            for q in range(Q):
                wide[row + q : row + q + 1, :] = jnp.where(place_of == q, r[...], 0.0)
            spread = wide[...].T.reshape(Z * R * 2, Q, rows, LANES)
            for q in range(Q):
                total += spread[:, q].reshape(total.shape)
        give(total)


def hand_out_plain(me, whole, Z, N, rows):
    whole = whole.astype(bf16).reshape(Z, N // 2, 2, rows, -1).swapaxes(0, 1)
    return [lax.dynamic_index_in_dim(whole, c, 2, keepdims=False) for c in (me[2], 1 - me[2])]


def grads(me, Z, N, name, arrays, plan, retr=None, vectors=(), tile=None):
    read = lambda spot: arrays[spot[0]] if spot[1] is None else arrays[spot[0]][spot[1]]
    shape = lambda spot: arrays[spot[0]].shape[-2:]
    D = sum(shape(left)[1] for left in plan[0][0])
    T = shape(plan[0][1])[0]
    rows, R = D // (Z * N), N // 2
    width = sum(shape(right)[1] for _, right in plan) + (0 if retr is None else retr.shape[1]) + (LANES if vectors else 0)
    if rows % 8:
        cols = [jnp.concatenate([dot(read(x), read(y), 0, 0) for x in xs], axis=0) for xs, y in plan]
        cols += [] if retr is None else [retr]
        if vectors:
            narrow = [jnp.concatenate([v for v in vectors if v.shape[1] <= D], axis=1).reshape(-1, D)]
            wide = [v.reshape(Z * N, -1, rows).swapaxes(0, 1).reshape(-1, D) for v in vectors if v.shape[1] > D]
            turned = jnp.concatenate(narrow + wide, axis=0).T
            cols += [turned, jnp.zeros((D, LANES - turned.shape[1]), f32)]
        return hand_out_plain(me, jnp.concatenate(cols, axis=1), Z, N, rows)
    ins = [*arrays] + ([] if retr is None else [retr]) + list(vectors)
    if tile is None:
        tile, specs, grid = width, [full_spec(a.shape) for a in ins], (1,)
    else:
        specs, grid = [full_spec(ins[0].shape), pl.BlockSpec((T, tile), lambda i: (0, i))], (width // tile,)
    return run(
        functools.partial(grads_body, plan, len(vectors), retr is not None, Z, R), name, grid, (me, *ins), [SMEM] + specs,
        [sds((R, Z, rows, width), bf16)] * 2, [pl.BlockSpec((R, Z, rows, tile), lambda i: (0, 0, 0, i))] * 2,
        scratch=[pltpu.VMEM((LANES, max(D, vectors[-1].shape[1])), f32), pltpu.VMEM((LANES, D), f32)] if vectors else [],
        flops=2 * T * D * width, moved=2 * T * (D + width) + 2 * D * width,
    )


def down_grad_body(me_ref, x_ref, y_ref, keep_ref, send_ref):
    hand_out(me_ref, dot(x_ref[...], y_ref[...], 0, 0), 1, keep_ref.shape[0], keep_ref, send_ref)


def down_grad(me, Z, N, act, feed):
    T, D = feed.shape
    F = act.shape[1]
    R, rows = N // 2, F // (Z * N)
    if rows % 8:
        return hand_out_plain(me, dot(act, feed, 0, 0), Z, N, rows)
    return run(
        down_grad_body, "down_grad", (Z,), (me, act, feed),
        [SMEM, pl.BlockSpec((T, N * rows), lambda i: (0, i)), full_spec(feed.shape)],
        [sds((R, Z, rows, D), bf16)] * 2, [pl.BlockSpec((R, 1, rows, D), lambda i: (0, i, 0, 0))] * 2,
        flops=2 * T * F * D, moved=2 * (T * F + T * D + F * D),
    )


def pair_body(n, me_ref, *refs):
    out_ref = refs[-1]
    width = out_ref.shape[3]
    at = 0
    for keep_ref, got_ref in zip(refs[:n], refs[n : 2 * n]):
        rows = keep_ref.shape[2]
        for lo in range(0, keep_ref.shape[3], width):
            cols = slice(lo, lo + width)
            out_ref[:, :, at : at + rows, :] = (
                keep_ref[:, :, :, cols].astype(f32) + got_ref[:, :, :, cols].astype(f32)
            ).astype(bf16)
            at += rows
    if len(refs) > 2 * n + 1:
        mine, other = refs[2 * n][...].astype(f32), refs[2 * n + 1][...].astype(f32)
        first = me_ref[2] == 0
        both = [jnp.where(first, mine, other), jnp.where(first, other, mine)]
        n_rows, w = mine.shape
        line = jnp.concatenate(both + [jnp.zeros((n_rows, width - 2 * w), f32)], axis=1).astype(bf16)
        for z in range(out_ref.shape[1]):
            out_ref[0, z, at : at + n_rows, :] = line


def pair_sum(parts, N, tok, me=None, term=None):
    n = len(parts)
    keeps = [keep for keep, _ in parts]
    got = [other_core(send, N) for _, send in parts]
    R, Z, _, width = keeps[0].shape
    rows = sum(k.size for k in keeps) // (R * Z * width)
    keeps[0] = after(keeps[0], tok)
    ins = keeps + got
    specs = [pl.BlockSpec((1,) + a.shape[1:], lambda i: (i, 0, 0, 0)) for a in ins]
    if term is not None:
        ins += [term, other_core(term, N)]
        specs += [full_spec(term.shape)] * 2
        rows += term.shape[0]
    return run(
        functools.partial(pair_body, n), "pair_sum", (R,), [jnp.zeros((3,), jnp.int32) if me is None else me] + ins, [SMEM] + specs,
        sds((R, Z, rows, width), bf16), pl.BlockSpec((1, Z, rows, width), lambda i: (i, 0, 0, 0)), moved=6 * R * Z * rows * width,
    )


def spots(n, width, shape):
    each = width // shape[1]
    return [(t // each * shape[0], t % each * shape[1]) for t in range(n)], -(-n // each) * shape[0]


def chips_body(term, me_ref, in_ref, *outs):
    R, _, rows, width = in_ref.shape
    rows -= term[0]
    where, _ = spots(2 * R, width, term)
    for k, out in enumerate(outs):
        z = me_ref[0] ^ k
        total = in_ref[0, z, :rows].astype(f32)
        for r in range(1, R):
            total += in_ref[r, z, :rows].astype(f32)
        out[:rows, :] = total.astype(out.dtype)
        if term[0]:
            out[rows:, :] = jnp.zeros((out.shape[0] - rows, width), out.dtype)
            for t, (row, col) in enumerate(where):
                tile = in_ref[t // 2, z, rows : rows + term[0], t % 2 * term[1] : (t % 2 + 1) * term[1]]
                out[rows + row : rows + row + term[0], col : col + term[1]] = tile.astype(out.dtype)


def chips_sum(me, got, tok, term=(0, LANES)):
    R, Z, rows, width = got.shape
    rows += spots(2 * R, width, term)[1] - term[0]
    return once(
        functools.partial(chips_body, term), "chips_sum", (me, after(got, tok)), [SMEM, None],
        [sds((rows, width), f32)] + [sds((rows, width), bf16)] * (Z - 1), moved=2 * got.size + 2 * Z * rows * width,
    )


def total_of(parts, lo, hi, rows=None):
    total = parts[0][:rows, lo:hi].astype(f32)
    for p in parts[1:]:
        total += p[:rows, lo:hi].astype(f32)
    return total


def last_body(n, cuts, G, gc, *refs):
    parts, (out_ref, in_ref, retr_ref, small_ref, turn) = refs[:n], refs[n:]
    rows = parts[0].shape[0]
    out_ref[...] = total_of(parts, *cuts[0])
    for g in range(G):
        for m in range(3):
            lo = cuts[1 + g][0] + m * gc
            in_ref[:, (m * G + g) * gc : (m * G + g + 1) * gc] = total_of(parts, lo, lo + gc)
    retr_ref[...] = total_of(parts, *cuts[1 + G])
    turn[...] = jnp.zeros_like(turn)
    turn[0:rows, :] = total_of(parts, *cuts[2 + G])
    small_ref[...] = turn[...].T[: small_ref.shape[0], :rows]


def last_sum(ins, widths, turned, G, gc, tok):
    rows = ins[0].shape[0]
    cuts = cut_points(widths)
    shapes = [(rows, widths[0]), (rows, 3 * G * gc), (rows, widths[-2]), (turned, rows)]
    return once(
        functools.partial(last_body, len(ins), cuts, G, gc), "last_sum", (after(ins[0], tok), *ins[1:]), [None] * len(ins),
        [sds(s, f32) for s in shapes], scratch=[pltpu.VMEM((LANES, LANES), f32)], moved=12 * rows * cuts[-1][1],
    )


def last_feed_body(n, term, N, me_ref, *refs):
    parts, (down_ref, up_ref, table_ref, held) = refs[:n], refs[n:]
    drows, D = down_ref.shape
    rows = up_ref.shape[0]
    total = total_of(parts, 0, D, 2 * drows)
    down_ref[...] = total[:drows]
    for q in range(drows // rows):
        up_ref[:, q * D : (q + 1) * D] = total[drows + q * rows : drows + (q + 1) * rows]
    where, _ = spots(N, D, term)
    trows = table_ref.shape[0]
    count, half = N * n * term[0], term[0] // 2
    for i, p in enumerate(parts):
        for t, (row, col) in enumerate(where):
            at = (i * N + t) * term[0]
            tile = p[2 * drows + row : 2 * drows + row + term[0], col : col + term[1]]
            held[at : at + term[0], :] = tile.astype(f32)
    held[count:, :] = jnp.zeros((term[0], term[1]), f32)
    below = held[half : half + count, :]
    ids = (below[:, 0:1] * 256.0 + below[:, 1:2]).astype(jnp.int32) - (me_ref[0] * N + 2 * me_ref[1] + me_ref[2]) * trows
    line = lax.broadcasted_iota(jnp.int32, (count, trows), 0) % term[0]
    picker = (lax.broadcasted_iota(jnp.int32, (count, trows), 1) == ids) & (line < half)
    table_ref[...] = dot(picker.astype(bf16), held[0:count, :].astype(bf16), 0, 0)


def last_feed(me, ins, F, tok, trows, term, N):
    D = ins[0].shape[1]
    both = ins[0].shape[0] - spots(N, D, term)[1]
    return once(
        functools.partial(last_feed_body, len(ins), term, N), "last_feed", (me, after(ins[0], tok), *ins[1:]), [SMEM] + [None] * len(ins),
        [sds((both // 2, D), f32), sds((both // 2 * D // F, F), f32), sds((trows, term[1]), f32)], moved=12 * both * D,
        scratch=[pltpu.VMEM(((N * len(ins) + 1) * term[0], term[1]), f32)],
    )


def along_dp_sums(sums):
    return [sums[0]] + [lax.ppermute(sums[k], "dp", pairs(len(sums), k)) for k in range(1, len(sums))]


def column(ref, n):
    line = lax.broadcasted_iota(jnp.int32, (n, 1), 0)
    total = jnp.zeros((n, 1), ref.dtype)
    for i in range(n):
        total = jnp.where(line == i, ref[i], total)
    return total


def lookup_body(found, me_ref, sg_ref, r_ref, *refs):
    chosen_ref, back_ref, lead_ref = refs[found:]
    seqs = sg_ref.shape[0]
    chosen_ref[...] = jnp.zeros_like(chosen_ref)
    if found == 2:
        total = jnp.zeros((2 * seqs, r_ref.shape[1]), f32)
        for ref in refs[:2]:
            for r in range(ref.shape[0]):
                total += ref[r, 0, ref.shape[2] - 2 * seqs :].astype(f32)
        chosen_ref[0:seqs, :] = jnp.where(me_ref[2] == 0, total[:seqs], total[seqs:])
    else:
        chosen_ref[0:seqs, :] = refs[0][...].astype(f32)
    back_ref[...] = jnp.zeros_like(back_ref)
    back_ref[0:seqs, :] = column(sg_ref, seqs) * chosen_ref[0:seqs, :]
    lead = dot(back_ref[...].astype(bf16), r_ref[...], 1, 1)
    for s in range(seqs):
        lead_ref[s] = lead[s : s + 1, :]


def lookup(me, sg, wide, F, D, width, found):
    seqs = sg.shape[0]
    specs = [None]
    if len(found) == 2:
        specs = [pl.BlockSpec((a.shape[0], 1, a.shape[2], width), lambda i: (0, 0, 0, 0)) for a in found]
    return once(
        functools.partial(lookup_body, len(found)), "lookup", (me, sg, wide, *found),
        [SMEM, SMEM, pl.BlockSpec((D, width), lambda i: (0, (F + D) // width))] + specs,
        [sds((16, width), f32), sds((16, width), f32), sds((seqs, 1, D), f32)], moved=4 * D * width,
    )


def score_body(top_ref, r_ref, chosen_ref, back_ref, sg_ref, id_ref, score_ref, retr_ref, term_ref, held):
    seqs = top_ref.shape[0]
    width = r_ref.shape[1]
    held[...] = jnp.zeros_like(held)
    for s in range(seqs):
        held[s : s + 1, :] = top_ref[s]
    leading = held[...].astype(bf16)
    projected = dot(leading, r_ref[...]).astype(bf16).astype(f32)[:seqs]
    score_ref[...] = jnp.sum(projected * chosen_ref[0:seqs, :], axis=-1, keepdims=True)
    retr_ref[...] = dot(leading, back_ref[...].astype(bf16), 0, 0)
    lane = lax.broadcasted_iota(jnp.int32, (seqs, width), 1)
    index = column(id_ref, seqs)
    high, low = index // 256, index % 256
    ids = jnp.where(lane == 0, high, jnp.where(lane == 1, low, 0)).astype(f32)
    term_ref[...] = jnp.concatenate([column(sg_ref, seqs) * projected, ids], axis=0).astype(bf16)


def score(top, wide, F, chosen, back, sg, index):
    seqs, _, D = top.shape
    width = chosen.shape[1]
    return once(
        score_body, "score", (top, wide, chosen, back, sg, index),
        [None, pl.BlockSpec((D, width), lambda i: (0, (F + D) // width))] + [None] * 2 + [SMEM] * 2,
        [sds((seqs, 1), f32), sds((D, width), f32), sds((2 * seqs, width), bf16)],
        scratch=[pltpu.VMEM((16, D), f32)], moved=8 * D * width,
    )


def bias_row_body(Z, N, Q, s_ref, v_ref, out_ref):
    D = s_ref.shape[0]
    rows = D // (Z * N)
    lane = lax.broadcasted_iota(jnp.int32, (Z * N, rows, LANES), 2)
    whole = s_ref[...].astype(f32).reshape(Z * N, rows, LANES)
    parts = [jnp.where(lane == UB + q, whole, 0.0).reshape(Z * N, 1, rows, LANES) for q in range(Q)]
    turned = jnp.concatenate(parts, axis=1).reshape(Q * D, LANES).T
    out_ref[...] = jnp.sum(turned, axis=0, keepdims=True)


def bias_row(small, vec, Z, N, Q):
    D = small.shape[0]
    rows = D // (Z * N)
    if rows % 8:
        return vec[UB : UB + Q].reshape(Q, Z * N, rows).transpose(1, 0, 2).reshape(1, Q * D)
    return once(
        functools.partial(bias_row_body, Z, N, Q), "bias_row", (small, vec), [None] * 2, [sds((1, Q * D), f32)],
        moved=8 * Q * D * LANES,
    )[0]


def local(
    Z, N, tokens, input_weight, query_bias, value_bias, output_weight, output_bias, first_gain, first_shift,
    up_weight, up_bias, down_weight, down_bias, second_gain, second_shift, retriever_weight, document_table,
    document_index, output_grad, score_grad,
):
    both = ("dp", "fsdp")
    T, D = tokens.shape
    R = N // 2
    F = up_weight.shape[1]
    Rw = retriever_weight.shape[1]
    seqs = document_index.shape[0]
    L = T // seqs
    per = 2 - seqs % 2
    gc = 4 * HEAD_DIM
    G = D // gc
    Q = F // D
    trows, rows = document_table.shape[0], input_weight.shape[0]
    f = lax.axis_index("fsdp")
    me = jnp.stack([lax.axis_index("dp"), f // 2, f % 2]).astype(jnp.int32)

    vectors = [
        v.reshape(1, -1)
        for v in (query_bias, value_bias, output_bias, first_gain, first_shift, down_bias, second_gain, second_shift, up_bias)
    ]
    head, rest, wide = pack(document_index, input_weight, output_weight, retriever_weight, up_weight, vectors, gc)
    wide = lax.all_gather(wide, both, axis=0, tiled=True)
    head = repeat(along_dp([head] * Z), R)
    rest = along_dp([after(rest, head)] * Z)
    head = between_chips(head, N)
    win_one, small, vec = place(me, [head, other_core(head, N)], Z, [3 * gc, LANES], turned=16)
    ub = bias_row(small, vec, Z, N, Q)
    rest = repeat([after(p, ub) for p in rest], R)
    if rows % 8:
        found, asked = [lax.all_gather(document_table, both, axis=0, tiled=True)[document_index]], ()
    else:
        asked = along_dp(ask(me, small, after(document_table, rest), seqs, Z, N, UB + Q))
    wd = along_dp([after(down_weight, rest)] * Z)
    rest = between_chips(rest, N)

    held = attend(after(tokens, ub), win_one, vec, seqs, G, 0)
    wd = repeat([after(w, held[2]) for w in wd], R, asked)
    rest = after(rest, wd)
    (win_two,) = place(me, [rest, other_core(rest, N)], Z, [3 * gc * (G - 1)])
    wd = between_chips(wd, N)
    qkv, soft, ctx = attend(tokens, win_two, vec, seqs, G, 1, held)
    wd = after(wd, ctx)
    n, inv, first, act, slope = up(ctx, tokens, vec, wide, ub, L, L // 2)
    wd = [wd, other_core(wd, N)]
    if rows % 8 == 0:
        found = wd
    (wd,) = place(me, [after(wd[0], first), wd[1]], Z, [D], rows=down_weight.shape[0])
    chosen, back_projected, lead = lookup(me, score_grad, after(wide, first), F, D, Rw, found)
    final, top, two, feed, inner, gsg, gss, gdb, gub = down(first, act, slope, wd, vec, output_grad, lead, seqs, per)
    scores, retriever_back, term = score(top, wide, F, chosen, back_projected, score_grad, document_index)
    down_parts = down_grad(me, Z, N, act, feed)
    up_parts = grads(me, Z, N, "up_grad", [after(first, *down_parts), inner], [([(0, None)], (1, None))], tile=D)
    feed_sums = pair_sum([down_parts, up_parts], N, up_parts[0], me, term)
    one, att, bctx, gfg, gfs, gob = mid(after(two, feed_sums), inner, wide, n, inv, vec, per * L, L)
    mixed, gq, gv = attend_back(qkv, soft, ctx, after(bctx, feed_sums), seqs)
    parts = grads(
        me, Z, N, "mix_grad", [ctx, att, tokens, mixed],
        [([(0, g) for g in range(G)], (1, None))] + [([(2, None)], (3, g)) for g in range(G)],
        retr=retriever_back, vectors=[gq, gv, gob, gfg, gfs, gdb, gsg, gss, gub],
    )
    mix_pair = pair_sum([parts], N, parts[0])
    feed_sums = between_chips(feed_sums, N)
    mix_sums = between_chips(after(mix_pair, feed_sums), N)
    feed_sums = chips_sum(me, feed_sums, mix_pair, term.shape)
    back_tokens = tokens_back(after(one, feed_sums[0]), mixed, [win_one, win_two], L)
    mix_sums = chips_sum(me, mix_sums, back_tokens)
    down_back, up_back, table_back = last_feed(me, along_dp_sums(feed_sums), F, mix_sums[0], trows, term.shape, N)
    output_back, input_back, retriever_back, small = last_sum(
        along_dp_sums(mix_sums), [D] + [3 * gc] * G + [Rw, LANES], 16, G, gc, down_back
    )
    ub_back = small[8 : 8 + Q].reshape(-1)
    return (
        final, scores.reshape(seqs), back_tokens, input_back, small[0], small[1], output_back, small[2], small[3], small[4],
        up_back, ub_back, down_back, small[5], small[6], small[7], retriever_back, table_back,
    )


def solution(mesh):
    both = ("dp", "fsdp")
    mat, vec = P(both, None), P(both)
    in_specs = (mat, mat, vec, vec, mat, vec, vec, vec, mat, vec, mat, vec, vec, vec, mat, mat, vec, mat, vec)
    out_specs = (mat, vec, mat, mat, vec, vec, mat, vec, vec, vec, mat, vec, mat, vec, vec, vec, mat, mat)
    body = functools.partial(local, mesh.shape["dp"], mesh.shape["fsdp"])
    return jax.shard_map(body, mesh=mesh, in_specs=in_specs, out_specs=out_specs, check_vma=False)
```
